32 devices in a mesh: ctx: 4 (over y, x), fsdp: 8 (over z, core).
Axes of the slice: x: 2, y: 2, z: 4, core: 2. Of those that a mesh axis runs over, the one named last changes fastest.
Arguments:
- tokens: bfloat16 [8, 1728, 1280], P('fsdp', 'ctx'), may hold values from -7.2 to 7.2
- cotangent: bfloat16 [8, 1728, 1280], P('fsdp', 'ctx'), may hold values from -7.2 to 7.2
- segments: int32 [8, 1728], P('fsdp'), may hold values from 0 to 7, as said below
- valid: int32 [8, 1728], P('fsdp'), may hold values from 0 to 1, as said below
- norm_one: bfloat16 [1280], P('fsdp'), may hold values from 0.5 to 1.5
- w_query: bfloat16 [1280, 1280], P('fsdp'), may hold values from -0.25 to 0.25
- w_key: bfloat16 [1280, 320], P('fsdp'), may hold values from -0.25 to 0.25
- w_value: bfloat16 [1280, 320], P('fsdp'), may hold values from -0.15625 to 0.15625
- w_out: bfloat16 [1280, 1280], P('fsdp'), may hold values from -0.5 to 0.5
- norm_two: bfloat16 [1280], P('fsdp'), may hold values from 0.5 to 1.5
- w_gate: bfloat16 [1280, 3584], P('fsdp'), may hold values from -0.15625 to 0.15625
- w_up: bfloat16 [1280, 3584], P('fsdp'), may hold values from -0.15625 to 0.15625
- w_down: bfloat16 [3584, 1280], P('fsdp'), may hold values from -0.09375 to 0.09375
Outputs:
- output: bfloat16 [8, 1728, 1280], P('fsdp', 'ctx')
- grad_tokens: bfloat16 [8, 1728, 1280], P('fsdp', 'ctx')
- grad_norm_one: float32 [1280], P('fsdp')
- grad_query: float32 [1280, 1280], P('fsdp')
- grad_key: float32 [1280, 320], P('fsdp')
- grad_value: float32 [1280, 320], P('fsdp')
- grad_out: float32 [1280, 1280], P('fsdp')
- grad_norm_two: float32 [1280], P('fsdp')
- grad_gate: float32 [1280, 3584], P('fsdp')
- grad_up: float32 [1280, 3584], P('fsdp')
- grad_down: float32 [3584, 1280], P('fsdp')
- spreads: float32 [5], replicated
The draws below stay inside these ranges and needn't reach their ends.
Inputs may be any that keep to these rules, and one draw needn't show every extreme that they name: `segments`: within a sequence the numbers never fall; the first document covers at least three quarters of the 1728 positions. `valid`: each sequence ends with 1 to 216 padding positions and has no others.
All inputs are finite; a program needn't handle non-finite values.
Results may differ from the reference program's by a relative error of at most 0.019.
Values may be sent and summed in bfloat16 or wider, within the bound.
No kernel may reach another device: no remote copies, remote signals or barrier semaphores. Data moves between devices by JAX's collectives and lax.ppermute only.
A program may use at most 256 MiB of HBM per device.

```python
import math
import jax
import jax.numpy as jnp
from jax import lax

D = 1280
HEADS = 20
KV_HEADS = 5
HEAD_DIM = 64
FF = 3584
BLK = 216
WINDOW = 1024
SEQS = 8
SEQ_LEN = 1728
N_CTX = 4


def rising_scale():
    index = jnp.arange(SEQS * SEQ_LEN, dtype=jnp.float32).reshape(SEQS, SEQ_LEN, 1)
    return 0.6 + 1.2 * index / (SEQS * SEQ_LEN)


def rough_field(key):
    base = jnp.clip(jax.random.normal(key, (SEQS, SEQ_LEN, D), jnp.float32), -4.0, 4.0)
    return base * rising_scale()


def draw_tokens(key, part):
    key = jax.random.fold_in(key, 11)
    return rough_field(key).astype(jnp.bfloat16)


def draw_cotangent(key, part):
    key = jax.random.fold_in(key, 12)
    return rough_field(key).astype(jnp.bfloat16)


def draw_segments(key, part):
    key = jax.random.fold_in(key, 13)
    first_key, cut_key = jax.random.split(key)
    cut_count = 6
    first_end = jax.random.randint(first_key, (SEQS, 1), 3 * SEQ_LEN // 4, 7 * SEQ_LEN // 8 + 1)
    cut_points = jax.random.randint(cut_key, (SEQS, cut_count), first_end, SEQ_LEN)
    positions = jnp.arange(SEQ_LEN, dtype=jnp.int32)
    later = (positions[None, :] >= first_end).astype(jnp.int32)
    passed = jnp.sum((positions[None, None, :] >= cut_points[:, :, None]).astype(jnp.int32), axis=1)
    return (later + passed).astype(jnp.int32)


def draw_valid(key, part):
    key = jax.random.fold_in(key, 14)
    padding = jax.random.randint(key, (SEQS, 1), 1, SEQ_LEN // 8 + 1)
    positions = jnp.arange(SEQ_LEN, dtype=jnp.int32)
    return (positions[None, :] < SEQ_LEN - padding).astype(jnp.int32)


def steps_of(own_key, dims, cuts, smallest, largest):
    level = 1.0
    for position, shards_of in cuts:
        steps = jax.random.uniform(jax.random.fold_in(jax.random.fold_in(own_key, 6), position), (shards_of,), jnp.float32, smallest / len(cuts), largest / len(cuts))
        level = level * jnp.repeat(jnp.exp(steps), dims[position] // shards_of).reshape((-1,) + (1,) * (len(dims) - 1 - position))
    return level


def scatter_about(own_key, extent, width, most, cuts=(), kind=jnp.bfloat16):
    level = steps_of(own_key, extent, cuts, -0.22, 0.18) if cuts else 1.0
    drawn = jax.random.normal(own_key, extent, jnp.float32) * width * level
    return jnp.minimum(jnp.maximum(drawn, -most), most).astype(kind)


def setup_inputs(seed: int = 0) -> dict:
    streams_of = jax.random.split(jax.random.key(seed), 14)
    return {
        "tokens": draw_tokens(jax.random.fold_in(streams_of[13], 71), 0),
        "cotangent": draw_cotangent(jax.random.fold_in(streams_of[13], 71), 0),
        "segments": draw_segments(jax.random.fold_in(streams_of[13], 71), 0),
        "valid": draw_valid(jax.random.fold_in(streams_of[13], 71), 0),
        "norm_one": jnp.clip(1.0 + 0.1 * jax.random.normal(streams_of[4], (D,), jnp.float32), 0.5, 1.5).astype(jnp.bfloat16),
        "w_query": scatter_about(streams_of[5], (D, D), (D // 2) ** -0.5, 0.25, ((0, 8),)),
        "w_key": scatter_about(streams_of[6], (D, KV_HEADS * HEAD_DIM), (D // 2) ** -0.5, 0.25, ((0, 8),)),
        "w_value": scatter_about(streams_of[7], (D, KV_HEADS * HEAD_DIM), D ** -0.5, 0.15625, ((0, 8),)),
        "w_out": scatter_about(streams_of[8], (D, D), (D // 8) ** -0.5, 0.5, ((0, 8),)),
        "norm_two": jnp.clip(1.0 + 0.1 * jax.random.normal(streams_of[9], (D,), jnp.float32), 0.5, 1.5).astype(jnp.bfloat16),
        "w_gate": scatter_about(streams_of[10], (D, FF), D ** -0.5, 0.15625, ((0, 8),)),
        "w_up": scatter_about(streams_of[11], (D, FF), D ** -0.5, 0.15625, ((0, 8),)),
        "w_down": scatter_about(streams_of[12], (FF, D), FF ** -0.5, 0.09375, ((0, 8),)),
    }


EPSILON = 1e-05
MASKED = -1e+30
ROPE_BASE = 10000.0
HIGHEST = lax.Precision.HIGHEST

@jax.custom_vjp
def low(v):
    return lax.optimization_barrier(v.astype(jnp.bfloat16)).astype(jnp.float32)

@jax.custom_vjp
def low_back(v):
    return v

def low_keep(v):
    return (low(v), None)

def low_pass(kept, grad):
    return (grad,)

def back_keep(v):
    return (v, None)

def back_low(kept, grad):
    return (low(grad),)
low.defvjp(low_keep, low_pass)
low_back.defvjp(back_keep, back_low)

def dealt_place(owner_index, within, block_rows, ctx_count):
    return jnp.where(within < block_rows, owner_index * block_rows + within, (2 * ctx_count - 1 - owner_index) * block_rows + within - block_rows)

def rope_tables(places, half_dim):
    freqs = jnp.exp(jnp.arange(half_dim, dtype=jnp.float32) * (-math.log(ROPE_BASE) / half_dim))
    angles = places.astype(jnp.float32)[:, None] * freqs[None, :]
    return (jnp.cos(angles)[:, None, :], jnp.sin(angles)[:, None, :])

def rotate(value_rows, cosine, sine):
    half_dim = value_rows.shape[-1] // 2
    first_half = value_rows[..., :half_dim]
    second_half = value_rows[..., half_dim:]
    return jnp.concatenate([first_half * cosine - second_half * sine, first_half * sine + second_half * cosine], axis=-1)

def rms_norm(value_rows, gain):
    return value_rows * lax.rsqrt(lax.optimization_barrier(jnp.mean(value_rows * value_rows, axis=-1, keepdims=True)) + EPSILON) * gain

def matmul(left, right):
    return jnp.dot(left, right, precision=HIGHEST)

def reference(tokens, cotangent, segments, valid, norm_one, w_query, w_key, w_value, w_out, norm_two, w_gate, w_up, w_down):
    row_count = 2 * BLK
    every = jnp.arange(SEQ_LEN, dtype=jnp.int32)
    places = dealt_place(every // row_count, every % row_count, BLK, N_CTX).astype(jnp.int32)
    seg_dealt = segments[:, places]
    live_dealt = valid[:, places]
    distance = places[:, None] - places[None, :]
    near_past = (distance >= 0) & (distance < WINDOW)
    cosine, sine = rope_tables(places, HEAD_DIM // 2)
    group_size = HEADS // KV_HEADS
    score_scale = 1.0 / math.sqrt(HEAD_DIM)

    def attend_one(packed):
        query_seq, key_seq, value_seq, seg_seq, live_seq = packed
        allowed = (seg_seq[:, None] == seg_seq[None, :]) & near_past & ((live_seq[None, :] == 1) | (distance == 0))
        grouped = query_seq.reshape(SEQ_LEN, KV_HEADS, group_size, HEAD_DIM)
        scores = low_back(jnp.einsum('qkgd,pkd->kgqp', grouped, key_seq, precision=HIGHEST) * score_scale)
        scores = jnp.where(allowed[None, None], scores, MASKED)
        row_peak = lax.optimization_barrier(jnp.max(scores, axis=-1, keepdims=True))
        exponent = jnp.exp(scores - row_peak)
        probabilities = exponent / lax.optimization_barrier(jnp.sum(exponent, axis=-1, keepdims=True))
        mixed_heads = jnp.einsum('kgqp,pkd->qkgd', low(probabilities), value_seq, precision=HIGHEST)
        return mixed_heads.reshape(SEQ_LEN, D)

    def forward(inputs, gain_one, query_w, key_w, value_w, out_w, gain_two, gate_w, up_w, down_w):
        first_in = low(rms_norm(inputs, gain_one))
        query_raw = low_back(matmul(first_in, query_w)).reshape(SEQS, SEQ_LEN, HEADS, HEAD_DIM)
        key_raw = low_back(matmul(first_in, key_w)).reshape(SEQS, SEQ_LEN, KV_HEADS, HEAD_DIM)
        value_rows = low(low_back(matmul(first_in, value_w))).reshape(SEQS, SEQ_LEN, KV_HEADS, HEAD_DIM)
        query_rot = low(rotate(query_raw, cosine, sine))
        key_rot = low(rotate(key_raw, cosine, sine))
        attended = lax.map(jax.checkpoint(attend_one), (query_rot, key_rot, value_rows, seg_dealt, live_dealt))
        attended = low(low_back(attended))
        branch_attn = low_back(matmul(attended, out_w))
        middle = inputs + branch_attn
        second_in = low(rms_norm(middle, gain_two))
        gate_pre = low_back(matmul(second_in, gate_w))
        up_pre = low_back(matmul(second_in, up_w))
        hidden = low(jax.nn.silu(gate_pre) * up_pre)
        branch_ffn = matmul(hidden, down_w)
        return (middle + branch_ffn, (middle, branch_attn, branch_ffn))
    floats = tuple((arg_value.astype(jnp.float32) for arg_value in (tokens, norm_one, w_query, w_key, w_value, w_out, norm_two, w_gate, w_up, w_down)))
    result, pull, extras = jax.vjp(forward, *floats, has_aux=True)
    grads = pull(cotangent.astype(jnp.float32))
    middle, branch_attn, branch_ffn = extras
    live = live_dealt.astype(jnp.float32)[:, :, None]
    count = jnp.sum(live_dealt.astype(jnp.float32))
    squares = jnp.stack([jnp.sum(live * member * member) for member in (result, grads[0], branch_attn, branch_ffn, middle)])
    spreads = jnp.sqrt(squares / (count * D))
    return (result.astype(jnp.bfloat16), grads[0].astype(jnp.bfloat16), grads[1], grads[2], grads[3], grads[4], grads[5], grads[6], grads[7], grads[8], grads[9], spreads)
```

```python
import functools
import math

import jax
import jax.numpy as jnp
from jax import lax
from jax.experimental import pallas as pl
from jax.experimental.pallas import tpu as pltpu
from jax.sharding import PartitionSpec as P

HEADS = 20
KV_HEADS = 5
HEAD_DIM = 64
GROUP = HEADS // KV_HEADS
WINDOW = 1024
EPSILON = 1e-05
MASKED = -1e30
ROPE_BASE = 10000.0
PARTS = 2
BF16 = jnp.bfloat16
F32 = jnp.float32


def core_swap(v):
    n = lax.axis_size("fsdp")
    return lax.ppermute(v, "fsdp", [(i, i ^ 1) for i in range(n)])


def swap_x(v):
    return lax.ppermute(v, "ctx", [(i, i ^ 1) for i in range(4)])


def swap_y(v):
    return lax.ppermute(v, "ctx", [(i, i ^ 2) for i in range(4)])


def put(buffer, piece, index, axis):
    return lax.dynamic_update_slice_in_dim(
        buffer, jnp.expand_dims(piece, axis), index, axis
    )


def take(v, index, axis):
    return lax.dynamic_index_in_dim(v, index, axis, keepdims=False)


def place(pieces, axis):
    first = pieces[0][1]
    shape = first.shape[:axis] + (len(pieces),) + first.shape[axis:]
    buffer = jnp.zeros(shape, first.dtype)
    for index, piece in pieces:
        buffer = put(buffer, piece, index, axis)
    return buffer


def z_groups(n):
    return [list(range(0, n, 2)), list(range(1, n, 2))]


def z_gather(piece):
    n = lax.axis_size("fsdp")
    nz = n // 2
    if nz != 4:
        return lax.all_gather(piece, "fsdp", axis=0, axis_index_groups=z_groups(n))
    z = lax.axis_index("fsdp") // 2
    pieces = [(z, piece)]
    for d in (1, 2, 3):
        got = lax.ppermute(piece, "fsdp", [(i, (i + 2 * d) % n) for i in range(n)])
        pieces.append(((z - d) % nz, got))
    return place(pieces, 0)


def z_scatter(pieces):
    n = lax.axis_size("fsdp")
    nz = n // 2
    if nz != 4:
        return lax.psum_scatter(
            pieces, "fsdp", scatter_dimension=0, axis_index_groups=z_groups(n)
        ).astype(F32)
    z = lax.axis_index("fsdp") // 2
    total = take(pieces, z, 0).astype(F32)
    for d in (1, 2, 3):
        sent = take(pieces, (z + d) % nz, 0)
        got = lax.ppermute(sent, "fsdp", [(i, (i + 2 * d) % n) for i in range(n)])
        total = total + got.astype(F32)
    return total


def half_perm(nz, s):
    return [(k * nz + (z + s) % nz, 2 * z + k) for z in range(nz) for k in range(2)]


def half_gather(piece):
    n = lax.axis_size("fsdp")
    nz = n // 2
    f = lax.axis_index("fsdp")
    z, k = f // 2, f % 2
    if nz != 4:
        every = lax.all_gather(piece, "fsdp", axis=0)
        return lax.dynamic_slice_in_dim(every, k * nz, nz, 0)
    pieces = []
    for s in range(nz):
        pieces.append(((z + s) % nz, lax.ppermute(piece, "fsdp", half_perm(nz, s))))
    return place(pieces, 0)


def half_scatter(pieces):
    n = lax.axis_size("fsdp")
    nz = n // 2
    f = lax.axis_index("fsdp")
    z, k = f // 2, f % 2
    if nz != 4:
        both = lax.dynamic_update_slice_in_dim(
            jnp.zeros((n,) + pieces.shape[1:], pieces.dtype), pieces, k * nz, 0
        )
        return lax.psum_scatter(both, "fsdp", scatter_dimension=0).astype(F32)
    total = None
    for s in range(nz):
        back = [(b, a) for a, b in half_perm(nz, s)]
        got = lax.ppermute(take(pieces, (z + s) % nz, 0), "fsdp", back).astype(F32)
        total = got if total is None else total + got
    return total


def ctx_gather(piece, axis):
    c = lax.axis_index("ctx")
    half = piece.shape[0] // 2
    from_x = swap_x(piece)
    from_y = swap_y(piece)
    from_d = jnp.concatenate([swap_y(from_x[:half]), swap_x(from_y[half:])], axis=0)
    return place([(c, piece), (c ^ 1, from_x), (c ^ 2, from_y), (c ^ 3, from_d)], axis)


def ctx_scatter(whole, axis):
    c = lax.axis_index("ctx")
    half = whole.shape[0] // 2
    low, high = whole[:half], whole[half:]
    low_got = swap_x(jnp.stack([take(low, c ^ 1, axis), take(low, c ^ 3, axis)]))
    high_got = swap_y(jnp.stack([take(high, c ^ 2, axis), take(high, c ^ 3, axis)]))
    low_own = take(low, c, axis).astype(F32) + low_got[0].astype(F32)
    low_pass = (take(low, c ^ 2, axis).astype(F32) + low_got[1].astype(F32)).astype(BF16)
    high_own = take(high, c, axis).astype(F32) + high_got[0].astype(F32)
    high_pass = (take(high, c ^ 1, axis).astype(F32) + high_got[1].astype(F32)).astype(BF16)
    low_sum = low_own + swap_y(low_pass).astype(F32)
    high_sum = high_own + swap_x(high_pass).astype(F32)
    return jnp.concatenate([low_sum, high_sum], axis=0)


def pair_bias(q_block, k_block, rows, seg_q, seg_k, valid_k):
    key_at = k_block * rows + lax.broadcasted_iota(jnp.int32, (rows, rows), 0)
    query_at = q_block * rows + lax.broadcasted_iota(jnp.int32, (rows, rows), 1)
    distance = query_at - key_at
    allowed = (
        (seg_q == seg_k)
        & (distance >= 0)
        & (distance < WINDOW)
        & ((valid_k == 1) | (distance == 0))
    )
    return jnp.where(allowed, 0.0, MASKED).astype(F32)


def first_block(q_block, rows):
    reach = (WINDOW + rows - 2) // rows
    return jnp.maximum(q_block - reach, 0)


def dot(a, b, dims):
    return lax.dot_general(a, b, (dims, ((), ())), preferred_element_type=F32)


def fill_bias(blocks_ref, seg_q_ref, seg_k_ref, valid_k_ref, bias_ref, rows):
    for side in range(2):
        b = blocks_ref[side]
        lo = first_block(b, rows)

        def body(kb, _):
            bias_ref[side, kb - lo] = pair_bias(
                b, kb, rows, seg_q_ref[side], seg_k_ref[kb], valid_k_ref[kb]
            )
            return 0

        lax.fori_loop(lo, b + 1, body, 0)


def forward_kernel(
    blocks_ref, seg_q_ref, seg_k_ref, valid_k_ref, q_ref, k_ref, v_ref,
    o_ref, lse_ref, bias_ref, acc_ref, peak_ref, total_ref,
):
    rows = q_ref.shape[-1]

    @pl.when(pl.program_id(0) == 0)
    def _():
        fill_bias(blocks_ref, seg_q_ref, seg_k_ref, valid_k_ref, bias_ref, rows)

    for side in range(2):
        b = blocks_ref[side]
        lo = first_block(b, rows)
        acc_ref[...] = jnp.zeros_like(acc_ref)
        total_ref[...] = jnp.zeros_like(total_ref)
        peak_ref[...] = jnp.full_like(peak_ref, -jnp.inf)

        def body(kb, _):
            keys = k_ref[kb, 0].T
            values_t = v_ref[kb, 0]
            bias = bias_ref[side, kb - lo]
            for h in range(GROUP):
                query = q_ref[side, h] * 0.125
                s = dot(keys, query, ((1,), (0,))) + bias
                peak_old = peak_ref[h : h + 1]
                peak = jnp.maximum(peak_old, jnp.max(s, axis=0, keepdims=True))
                p = jnp.exp(s - peak)
                shrink = jnp.exp(peak_old - peak)
                peak_ref[h : h + 1] = peak
                total_ref[h : h + 1] = total_ref[h : h + 1] * shrink + jnp.sum(
                    p, axis=0, keepdims=True
                )
                acc_ref[h] = acc_ref[h] * shrink + dot(values_t, p.astype(BF16), ((1,), (0,)))
            return 0

        body(b, 0)
        lax.fori_loop(lo, b, body, 0)
        for h in range(GROUP):
            total = total_ref[h : h + 1]
            o_ref[side, h] = (acc_ref[h] / total).astype(BF16)
            lse_ref[side, 0, h : h + 1] = peak_ref[h : h + 1] + jnp.log(total)


def backward_kernel(
    blocks_ref, seg_q_ref, seg_k_ref, valid_k_ref, q_ref, k_ref, v_ref, o_ref, do_ref, lse_ref,
    dq_ref, dk_ref, dv_ref, bias_ref, acc_ref, center_ref,
):
    rows = q_ref.shape[-1]

    @pl.when(pl.program_id(0) == 0)
    def _():
        fill_bias(blocks_ref, seg_q_ref, seg_k_ref, valid_k_ref, bias_ref, rows)

    dk_ref[...] = jnp.zeros_like(dk_ref)
    dv_ref[...] = jnp.zeros_like(dv_ref)
    for side in range(2):
        b = blocks_ref[side]
        lo = first_block(b, rows)
        acc_ref[...] = jnp.zeros_like(acc_ref)
        for h in range(GROUP):
            center_ref[h : h + 1] = jnp.sum(
                o_ref[side, h].astype(F32) * do_ref[side, h].astype(F32), axis=0, keepdims=True
            )

        def body(kb, _):
            keys_t = k_ref[kb, 0]
            keys = keys_t.T
            values = v_ref[kb, 0].T
            bias = bias_ref[side, kb - lo]
            for h in range(GROUP):
                query_t = q_ref[side, h] * 0.125
                grad_t = do_ref[side, h]
                s = dot(keys, query_t, ((1,), (0,))) + bias
                p = jnp.exp(s - lse_ref[side, 0, h : h + 1])
                dp = dot(values, grad_t, ((1,), (0,)))
                ds = (p * (dp - center_ref[h : h + 1])).astype(BF16)
                dv_ref[kb, 0] += dot(grad_t, p.astype(BF16), ((1,), (1,)))
                dk_ref[kb, 0] += dot(query_t, ds, ((1,), (1,)))
                acc_ref[h] += dot(keys_t, ds, ((1,), (0,)))
            return 0

        lax.fori_loop(lo, b + 1, body, 0)
        for h in range(GROUP):
            dq_ref[side, h] = acc_ref[h] * 0.125


def kernel_specs(blocks, rows):
    q_spec = pl.BlockSpec((2, GROUP, HEAD_DIM, rows), lambda g, s: (0, g, 0, 0))
    k_spec = pl.BlockSpec((blocks, 1, HEAD_DIM, rows), lambda g, s: (0, g, 0, 0))
    v_spec = pl.BlockSpec((blocks, 1, HEAD_DIM, rows), lambda g, s: (0, KV_HEADS + g, 0, 0))
    stat_spec = pl.BlockSpec((2, 1, GROUP, rows), lambda g, s: (0, g, 0, 0))
    seg_specs = [
        pl.BlockSpec((2, 1, rows), lambda g, s: (0, 0, 0)),
        pl.BlockSpec((blocks, rows, 1), lambda g, s: (0, 0, 0)),
        pl.BlockSpec((blocks, rows, 1), lambda g, s: (0, 0, 0)),
    ]
    return q_spec, k_spec, v_spec, stat_spec, seg_specs


def attention_forward(q_blocks, seg_q, seg_k, valid_k, q_t, kv_t):
    blocks, _, _, rows = kv_t.shape
    q_spec, k_spec, v_spec, stat_spec, seg_specs = kernel_specs(blocks, rows)
    reach = (WINDOW + rows - 2) // rows + 1
    return pl.pallas_call(
        forward_kernel,
        grid_spec=pltpu.PrefetchScalarGridSpec(
            num_scalar_prefetch=1,
            grid=(KV_HEADS,),
            in_specs=seg_specs + [q_spec, k_spec, v_spec],
            out_specs=[q_spec, stat_spec],
            scratch_shapes=[
                pltpu.VMEM((2, reach, rows, rows), F32),
                pltpu.VMEM((GROUP, HEAD_DIM, rows), F32),
                pltpu.VMEM((GROUP, rows), F32),
                pltpu.VMEM((GROUP, rows), F32),
            ],
        ),
        out_shape=[
            jax.ShapeDtypeStruct(q_t.shape, BF16),
            jax.ShapeDtypeStruct((2, KV_HEADS, GROUP, rows), F32),
        ],
        compiler_params=pltpu.CompilerParams(vmem_limit_bytes=40 * 2**20),
        cost_estimate=pl.CostEstimate(
            flops=20_000_000_000, bytes_accessed=6_000_000, transcendentals=0
        ),
    )(q_blocks, seg_q, seg_k, valid_k, q_t, kv_t, kv_t)


def attention_backward(q_blocks, seg_q, seg_k, valid_k, q_t, kv_t, o_t, do_t, lse):
    blocks, _, _, rows = kv_t.shape
    q_spec, k_spec, v_spec, stat_spec, seg_specs = kernel_specs(blocks, rows)
    reach = (WINDOW + rows - 2) // rows + 1
    return pl.pallas_call(
        backward_kernel,
        grid_spec=pltpu.PrefetchScalarGridSpec(
            num_scalar_prefetch=1,
            grid=(KV_HEADS,),
            in_specs=seg_specs + [q_spec, k_spec, v_spec, q_spec, q_spec, stat_spec],
            out_specs=[q_spec, k_spec, k_spec],
            scratch_shapes=[
                pltpu.VMEM((2, reach, rows, rows), F32),
                pltpu.VMEM((GROUP, HEAD_DIM, rows), F32),
                pltpu.VMEM((GROUP, rows), F32),
            ],
        ),
        out_shape=[
            jax.ShapeDtypeStruct(q_t.shape, F32),
            jax.ShapeDtypeStruct((blocks, KV_HEADS, HEAD_DIM, rows), F32),
            jax.ShapeDtypeStruct((blocks, KV_HEADS, HEAD_DIM, rows), F32),
        ],
        compiler_params=pltpu.CompilerParams(vmem_limit_bytes=48 * 2**20),
        cost_estimate=pl.CostEstimate(
            flops=40_000_000_000, bytes_accessed=16_000_000, transcendentals=0
        ),
    )(q_blocks, seg_q, seg_k, valid_k, q_t, kv_t, kv_t, o_t, do_t, lse)


def norm_forward(value_rows, gain):
    inverse = lax.rsqrt(jnp.mean(value_rows * value_rows, axis=-1, keepdims=True) + EPSILON)
    normed = value_rows * inverse
    return (normed * gain, normed, inverse)


def norm_backward(upstream, gain, normed, inverse):
    scaled = upstream * gain
    grad_in = inverse * (scaled - normed * jnp.mean(scaled * normed, axis=-1, keepdims=True))
    return (grad_in, jnp.sum(upstream * normed, axis=0))


def ein(spec, left, right):
    return jnp.einsum(spec, left, right, preferred_element_type=F32)


def turn(v, cosine, sine):
    half = HEAD_DIM // 2
    a, b = v[:, :, :half], v[:, :, half:]
    return jnp.concatenate([a * cosine - b * sine, a * sine + b * cosine], axis=2)


def order(n, own, other):
    k = lax.axis_index("fsdp") % 2
    return jnp.stack([jnp.where(k == 0, own, other), jnp.where(k == 0, other, own)])


def gather_rows(shard):
    n = lax.axis_size("fsdp")
    c = lax.axis_index("ctx")
    r, cols = shard.shape
    quarter = lax.dynamic_slice_in_dim(shard, c * (r // 4), r // 4, 0)
    mine = ctx_gather(z_gather(quarter), 1)
    other = core_swap(mine)
    k = lax.axis_index("fsdp") % 2
    whole = place([(k, mine), (k ^ 1, other)], 1)
    return whole.reshape(n * r, cols)


def scatter_rows(whole):
    n = lax.axis_size("fsdp")
    nz = n // 2
    k = lax.axis_index("fsdp") % 2
    rows, cols = whole.shape
    r = rows // n
    parts = whole.reshape(nz, 2, 4, r // 4, cols)
    got = core_swap(take(parts, k ^ 1, 1))
    pair = (take(parts, k, 1).astype(F32) + got.astype(F32)).astype(BF16)
    mine = z_scatter(ctx_scatter(pair, 1).astype(BF16))
    return ctx_gather(mine.astype(BF16), 0).reshape(r, cols).astype(F32)


def per_device(
    tokens, cotangent, segments, valid, norm_one, w_query, w_key, w_value, w_out,
    norm_two, w_gate, w_up, w_down,
):
    c = lax.axis_index("ctx")
    n = lax.axis_size("fsdp")
    nz = n // 2
    f = lax.axis_index("fsdp")
    k = f % 2
    row_count = tokens.shape[1]
    rows = row_count // 2
    width = tokens.shape[2]
    blocks = 8
    q_width, kv_width = w_query.shape[1], w_key.shape[1]
    ff = w_gate.shape[1]
    r = w_query.shape[0]
    r4 = r // 4

    q_blocks = jnp.stack([c, blocks - 1 - c]).astype(jnp.int32)
    seg_blocks = segments[0].reshape(blocks, rows)
    valid_blocks = valid[0].reshape(blocks, rows)
    seg_q = jnp.stack([take(seg_blocks, q_blocks[0], 0), take(seg_blocks, q_blocks[1], 0)])
    live = jnp.stack([take(valid_blocks, q_blocks[0], 0), take(valid_blocks, q_blocks[1], 0)])
    seg_q = seg_q[:, None, :]
    seg_k = seg_blocks[:, :, None]
    valid_k = valid_blocks[:, :, None]
    places = q_blocks[:, None] * rows + jnp.arange(rows, dtype=jnp.int32)[None, :]
    half = HEAD_DIM // 2
    freqs = jnp.exp(jnp.arange(half, dtype=F32) * (-math.log(ROPE_BASE) / half))
    angles = places.astype(F32)[:, None, None, :] * freqs[None, None, :, None]
    cosine, sine = jnp.cos(angles), jnp.sin(angles)

    gains = jnp.stack([norm_one, norm_two], axis=1)
    gains = jnp.concatenate([gains, jnp.zeros((r, 126), BF16)], axis=1)
    qkv_w = gather_rows(jnp.concatenate([w_query, w_key, w_value, gains], axis=1))
    out_w = gather_rows(w_out)
    gain_one = qkv_w[:, -128].astype(F32)
    gain_two = qkv_w[:, -127].astype(F32)

    d_rows = w_down.shape[0]
    d4 = d_rows // 4
    strip = d_rows // PARTS
    s4 = strip // 4

    def columns(shard):
        quarter = lax.dynamic_slice_in_dim(shard, c * r4, r4, 0)
        cut = quarter.reshape(r4, 2, nz, PARTS, strip).transpose(1, 3, 0, 2, 4)
        return cut.reshape(2, PARTS, r4, nz * strip)

    pairs = jnp.concatenate([columns(w_gate), columns(w_up)], axis=3)
    cut = nz * strip
    gu_w, down_w = [], []
    for part in range(PARTS):
        keep = take(pairs[:, part], k, 0)
        other = core_swap(take(pairs[:, part], k ^ 1, 0))
        both = order(n, keep, other)
        gu_w.append(ctx_gather(z_gather(both), 2).reshape(n * r, 2 * cut))
        piece = lax.dynamic_slice_in_dim(w_down, part * strip + c * s4, s4, 0)
        down_w.append(ctx_gather(half_gather(piece), 1).reshape(cut, width))

    inputs = tokens[0].astype(F32)
    normed_one, unit_one, inverse_one = norm_forward(inputs, gain_one)
    first_in = normed_one.astype(BF16)
    first_sides = first_in.reshape(2, rows, width)
    qkv_t = ein("if,bri->bfr", qkv_w[:, : q_width + 2 * kv_width], first_sides)
    q_t = turn(qkv_t[:, :q_width].reshape(2, HEADS, HEAD_DIM, rows), cosine, sine).astype(BF16)
    k_t = turn(
        qkv_t[:, q_width : q_width + kv_width].reshape(2, KV_HEADS, HEAD_DIM, rows), cosine, sine
    ).astype(BF16)
    v_t = qkv_t[:, q_width + kv_width :].reshape(2, KV_HEADS, HEAD_DIM, rows).astype(BF16)
    kv_own = jnp.concatenate([k_t, v_t], axis=1)
    kv_x, kv_y = swap_x(kv_own), swap_y(kv_own)
    kv_d = jnp.stack([swap_y(kv_x[0]), swap_x(kv_y[1])])
    kv_all = jnp.zeros((blocks,) + kv_own.shape[1:], BF16)
    for owner, piece in ((c, kv_own), (c ^ 1, kv_x), (c ^ 2, kv_y), (c ^ 3, kv_d)):
        kv_all = put(kv_all, piece[0], owner, 0)
        kv_all = put(kv_all, piece[1], blocks - 1 - owner, 0)
    o_t, lse = attention_forward(q_blocks, seg_q, seg_k, valid_k, q_t, kv_all)
    attended_t = o_t.reshape(2, width, rows)
    branch_attn = ein("bfr,fo->bro", attended_t, out_w).reshape(row_count, width)
    middle = inputs + branch_attn

    normed_two, unit_two, inverse_two = norm_forward(middle, gain_two)
    second_in = normed_two.astype(BF16)
    grad_output = cotangent[0]
    x2 = jnp.concatenate([second_in, core_swap(second_in)], axis=0)
    dy2 = jnp.concatenate([grad_output, core_swap(grad_output)], axis=0)
    ffn2 = 0.0
    d_second2 = 0.0
    grad_gu, grad_d = [], []
    for part in range(PARTS):
        gu = ein("ri,if->rf", x2, gu_w[part])
        gate_pre, up_pre = gu[:, :cut], gu[:, cut:]
        sig = jax.nn.sigmoid(gate_pre)
        swish = gate_pre * sig
        hidden = (swish * up_pre).astype(BF16)
        d_hidden = ein("ro,fo->rf", dy2, down_w[part])
        slope = sig * (1.0 + gate_pre * (1.0 - sig))
        d_gu = jnp.concatenate(
            [(d_hidden * up_pre * slope).astype(BF16), (d_hidden * swish).astype(BF16)], axis=1
        )
        grad_d.append(ein("rf,ro->fo", hidden, dy2).astype(BF16))
        grad_gu.append(ein("ri,rf->if", x2, d_gu).astype(BF16))
        ffn2 = ffn2 + ein("rf,fo->ro", hidden, down_w[part])
        d_second2 = d_second2 + ein("rf,if->ri", d_gu, gu_w[part])
    d_second = d_second2[:row_count] + core_swap(d_second2[row_count:].astype(BF16)).astype(F32)
    branch_ffn = ffn2[:row_count] + core_swap(ffn2[row_count:].astype(BF16)).astype(F32)
    result = middle + branch_ffn

    quarter_gu, shard_down = [], []
    for part in range(PARTS):
        whole = grad_gu[part].reshape(nz, 2, 4, r4, 2 * cut)
        mine = z_scatter(ctx_scatter(whole, 2).astype(BF16))
        own = take(mine, k, 0).astype(BF16)
        other = core_swap(take(mine, k ^ 1, 0).astype(BF16))
        quarter_gu.append(order(n, own, other))
        down = half_scatter(ctx_scatter(grad_d[part].reshape(nz, 4, s4, width), 1).astype(BF16))
        shard_down.append(ctx_gather(down.astype(BF16), 0).reshape(strip, width))
    quarters = jnp.stack(quarter_gu, axis=1).reshape(2, PARTS, r4, 2, nz, strip)
    quarters = quarters.transpose(3, 2, 0, 4, 1, 5).reshape(2, r4, ff)
    whole_gu = ctx_gather(quarters, 1).reshape(2, r, ff).astype(F32)
    grad_gate_w, grad_up_w = whole_gu[0], whole_gu[1]
    grad_down_w = jnp.concatenate(shard_down, axis=0).astype(F32)

    grad_mid_norm, grad_gain_two = norm_backward(d_second, gain_two, unit_two, inverse_two)
    grad_middle = grad_output.astype(F32) + grad_mid_norm
    d_branch = grad_middle.astype(BF16).reshape(2, rows, width)
    grad_out_w = scatter_rows(ein("bfr,bro->fo", attended_t, d_branch).astype(BF16))
    do_t = ein("fo,bro->bfr", out_w, d_branch).astype(BF16).reshape(2, HEADS, HEAD_DIM, rows)
    dq_t, dk_t, dv_t = attention_backward(
        q_blocks, seg_q, seg_k, valid_k, q_t, kv_all, o_t, do_t, lse
    )
    dkv = jnp.concatenate([dk_t, dv_t], axis=1).astype(BF16)

    def of(owner, side):
        return take(dkv, owner if side == 0 else blocks - 1 - owner, 0)

    low = swap_x(jnp.stack([of(c ^ 1, 0), of(c ^ 3, 0)])).astype(F32)
    high = swap_y(jnp.stack([of(c ^ 2, 1), of(c ^ 3, 1)])).astype(F32)
    low_own = of(c, 0).astype(F32) + low[0]
    low_pass = (of(c ^ 2, 0).astype(F32) + low[1]).astype(BF16)
    high_own = of(c, 1).astype(F32) + high[0]
    high_pass = (of(c ^ 1, 1).astype(F32) + high[1]).astype(BF16)
    dkv_own = jnp.stack(
        [low_own + swap_y(low_pass).astype(F32), high_own + swap_x(high_pass).astype(F32)]
    )
    d_q = turn(dq_t, cosine, -sine).astype(BF16)
    d_k = turn(dkv_own[:, :KV_HEADS], cosine, -sine).astype(BF16)
    d_v = dkv_own[:, KV_HEADS:].astype(BF16)
    d_qkv = jnp.concatenate([d_q, d_k, d_v], axis=1).reshape(2, q_width + 2 * kv_width, rows)
    grad_qkv = scatter_rows(ein("bri,bfr->if", first_sides, d_qkv).astype(BF16))
    d_first = ein("bfr,if->bri", d_qkv, qkv_w[:, : q_width + 2 * kv_width])
    grad_in_norm, grad_gain_one = norm_backward(
        d_first.reshape(row_count, width), gain_one, unit_one, inverse_one
    )
    grad_inputs = grad_middle + grad_in_norm

    live_rows = live.reshape(row_count, 1).astype(F32)
    squares = jnp.stack(
        [
            jnp.sum(live_rows * member * member)
            for member in (result, grad_inputs, branch_attn, branch_ffn, middle)
        ]
        + [jnp.sum(live_rows)]
    )
    small = lax.psum(jnp.concatenate([grad_gain_one, grad_gain_two, squares]), ("ctx", "fsdp"))
    gain_sums = lax.dynamic_slice_in_dim(small[: 2 * width].reshape(2, width), f * r, r, 1)
    squares = small[2 * width :]
    spreads = jnp.sqrt(squares[:5] / (squares[5] * width))
    return (
        result[None].astype(BF16),
        grad_inputs[None].astype(BF16),
        gain_sums[0],
        grad_qkv[:, :q_width],
        grad_qkv[:, q_width : q_width + kv_width],
        grad_qkv[:, q_width + kv_width :],
        grad_out_w,
        gain_sums[1],
        grad_gate_w,
        grad_up_w,
        grad_down_w,
        spreads,
    )


def solution(mesh):
    rows, shard, vector = P("fsdp", "ctx", None), P("fsdp", None), P("fsdp")
    return jax.shard_map(
        per_device,
        mesh=mesh,
        in_specs=(
            rows, rows, shard, shard, vector, shard, shard, shard, shard, vector,
            shard, shard, shard,
        ),
        out_specs=(
            rows, rows, vector, shard, shard, shard, shard, vector, shard, shard, shard, P(),
        ),
        check_vma=False,
    )
```

```python
import functools
import math

import jax
import jax.numpy as jnp
from jax import lax
from jax.experimental import pallas as pl
from jax.experimental.pallas import tpu as pltpu
from jax.sharding import PartitionSpec as P

HEADS = 20
KV_HEADS = 5
HEAD_DIM = 64
GROUP = HEADS // KV_HEADS
WINDOW = 1024
EPSILON = 1e-05
MASKED = -1e30
ROPE_BASE = 10000.0
BF16 = jnp.bfloat16
F32 = jnp.float32


def core_swap(v):
    n = lax.axis_size("fsdp")
    return lax.ppermute(v, "fsdp", [(i, i ^ 1) for i in range(n)])


def swap_x(v):
    return lax.ppermute(v, "ctx", [(i, i ^ 1) for i in range(4)])


def swap_y(v):
    return lax.ppermute(v, "ctx", [(i, i ^ 2) for i in range(4)])


def put(buffer, piece, index, axis):
    return lax.dynamic_update_slice_in_dim(
        buffer, jnp.expand_dims(piece, axis), index, axis
    )


def take(v, index, axis):
    return lax.dynamic_index_in_dim(v, index, axis, keepdims=False)


def place(pieces, axis):
    first = pieces[0][1]
    shape = first.shape[:axis] + (len(pieces),) + first.shape[axis:]
    buffer = jnp.zeros(shape, first.dtype)
    for index, piece in pieces:
        buffer = put(buffer, piece, index, axis)
    return buffer


def z_fetch(piece):
    n = lax.axis_size("fsdp")
    nz = n // 2
    if nz != 4:
        groups = [list(range(0, n, 2)), list(range(1, n, 2))]
        every = lax.all_gather(piece, "fsdp", axis=0, axis_index_groups=groups)
        z = lax.axis_index("fsdp") // 2
        return jnp.take(every, (z - jnp.arange(nz)) % nz, axis=0)
    pieces = [piece]
    for d in (1, 2, 3):
        pieces.append(lax.ppermute(piece, "fsdp", [(i, (i + 2 * d) % n) for i in range(n)]))
    return jnp.stack(pieces)


def z_scatter(pieces):
    n = lax.axis_size("fsdp")
    nz = n // 2
    if nz != 4:
        groups = [list(range(0, n, 2)), list(range(1, n, 2))]
        return lax.psum_scatter(
            pieces, "fsdp", scatter_dimension=0, axis_index_groups=groups
        ).astype(F32)
    z = lax.axis_index("fsdp") // 2
    total = take(pieces, z, 0).astype(F32)
    for d in (1, 2, 3):
        sent = take(pieces, (z + d) % nz, 0)
        got = lax.ppermute(sent, "fsdp", [(i, (i + 2 * d) % n) for i in range(n)])
        total = total + got.astype(F32)
    return total


def sync(*values):
    return lax.optimization_barrier(values)


def ctx_fetch(piece):
    half = piece.shape[0] // 2
    from_x = swap_x(piece)
    from_y = swap_y(piece)
    from_d = jnp.concatenate([swap_y(from_x[:half]), swap_x(from_y[half:])], axis=0)
    return [piece, from_x, from_y, from_d]


def after(v, *earlier):
    return lax.optimization_barrier((v, earlier))[0]


def ctx_fetch_direct(piece):
    diagonal = lax.ppermute(piece, "ctx", [(i, i ^ 3) for i in range(4)])
    return [piece, swap_x(piece), swap_y(piece), diagonal]


def ctx_gather(piece, axis):
    c = lax.axis_index("ctx")
    return place([(c ^ i, v) for i, v in enumerate(ctx_fetch(piece))], axis)


def scatter_first(parts):
    half = parts[0].shape[0] // 2
    low_got = swap_x(jnp.concatenate([parts[1][:half], parts[3][:half]]))
    high_got = swap_y(jnp.concatenate([parts[2][half:], parts[3][half:]]))
    return low_got, high_got


def scatter_pass(parts, got):
    half = parts[0].shape[0] // 2
    low_got, high_got = got[0].astype(F32), got[1].astype(F32)
    low_pass = (parts[2][:half].astype(F32) + low_got[half:]).astype(BF16)
    high_pass = (parts[1][half:].astype(F32) + high_got[half:]).astype(BF16)
    low_own = parts[0][:half].astype(F32) + low_got[:half]
    high_own = parts[0][half:].astype(F32) + high_got[:half]
    return low_own, high_own, low_pass, high_pass


def scatter_last(low_own, high_own, low_pass, high_pass):
    from_y, from_x = swap_y(low_pass), swap_x(high_pass)
    return jnp.concatenate([low_own + from_y.astype(F32), high_own + from_x.astype(F32)])


def exchange_first(parts):
    to_x = jnp.concatenate([parts[1], parts[3][:1]], axis=0)
    to_y = jnp.concatenate([parts[2], parts[3][1:]], axis=0)
    return swap_x(to_x), swap_y(to_y)


def exchange_second(parts, got_x, got_y):
    from_d = jnp.concatenate([swap_y(got_x[2:]), swap_x(got_y[2:])], axis=0)
    return [parts[0], got_x[:2], got_y[:2], from_d]


def small_sum(v):
    n = lax.axis_size("fsdp")
    bit = 1
    while bit < n:
        v = v + lax.ppermute(v, "fsdp", [(i, i ^ bit) for i in range(n)])
        bit *= 2
    v = v + swap_x(v)
    return v + swap_y(v)


def pick_columns(c, gate, up, count):
    r, ff = gate.shape
    group = ff // count
    strip = group // 4

    def kernel(c_ref, gate_ref, up_ref, out_ref):
        for own in range(4):

            @pl.when(c_ref[0] == own)
            def _():
                for j in range(count):
                    at = j * group + own * strip
                    out_ref[:, j * strip : (j + 1) * strip] = gate_ref[:, at : at + strip]
                    to = ff // 4 + j * strip
                    out_ref[:, to : to + strip] = up_ref[:, at : at + strip]

    whole = pl.BlockSpec((r, ff), lambda i, s: (0, 0))
    return pl.pallas_call(
        kernel,
        grid_spec=pltpu.PrefetchScalarGridSpec(
            num_scalar_prefetch=1,
            grid=(1,),
            in_specs=[whole, whole],
            out_specs=pl.BlockSpec((r, ff // 2), lambda i, s: (0, 0)),
        ),
        out_shape=jax.ShapeDtypeStruct((r, ff // 2), BF16),
        cost_estimate=pl.CostEstimate(flops=0, bytes_accessed=6 * r * ff, transcendentals=0),
    )(c, gate, up)


def unpick_columns(c, pieces, count):
    r, half = pieces[0].shape
    ff = 2 * half
    group = ff // count
    strip = group // 4

    def kernel(c_ref, *refs):
        gate_ref, up_ref = refs[4:]
        for own in range(4):

            @pl.when(c_ref[0] == own)
            def _():
                for step in range(4):
                    for j in range(count):
                        at = j * group + (own ^ step) * strip
                        piece = refs[step]
                        gate_ref[:, at : at + strip] = piece[
                            :, j * strip : (j + 1) * strip
                        ].astype(F32)
                        frm = ff // 4 + j * strip
                        up_ref[:, at : at + strip] = piece[:, frm : frm + strip].astype(F32)

    whole = pl.BlockSpec((r, ff), lambda i, s: (0, 0))
    return pl.pallas_call(
        kernel,
        grid_spec=pltpu.PrefetchScalarGridSpec(
            num_scalar_prefetch=1,
            grid=(1,),
            in_specs=[pl.BlockSpec((r, half), lambda i, s: (0, 0))] * 4,
            out_specs=[whole, whole],
        ),
        out_shape=[jax.ShapeDtypeStruct((r, ff), F32)] * 2,
        compiler_params=pltpu.CompilerParams(vmem_limit_bytes=40 * 2**20),
        cost_estimate=pl.CostEstimate(flops=0, bytes_accessed=12 * r * ff, transcendentals=0),
    )(c, *pieces)


def pair_bias(q_block, k_block, rows, seg_q, seg_k, valid_k):
    key_at = k_block * rows + lax.broadcasted_iota(jnp.int32, (rows, rows), 0)
    query_at = q_block * rows + lax.broadcasted_iota(jnp.int32, (rows, rows), 1)
    distance = query_at - key_at
    allowed = (
        (seg_q == seg_k)
        & (distance >= 0)
        & (distance < WINDOW)
        & ((valid_k == 1) | (distance == 0))
    )
    return jnp.where(allowed, 0.0, MASKED).astype(F32)


def first_block(q_block, rows):
    reach = (WINDOW + rows - 2) // rows
    return jnp.maximum(q_block - reach, 0)


def dot(a, b, dims):
    return lax.dot_general(a, b, (dims, ((), ())), preferred_element_type=F32)


def fill_bias(blocks_ref, seg_q_ref, seg_k_ref, valid_k_ref, bias_ref, rows):
    for side in range(2):
        b = blocks_ref[side]
        lo = first_block(b, rows)

        def body(kb, _):
            bias_ref[side, kb - lo] = pair_bias(
                b, kb, rows, seg_q_ref[side], seg_k_ref[kb], valid_k_ref[kb]
            )
            return 0

        lax.fori_loop(lo, b + 1, body, 0)


def forward_kernel(
    blocks_ref, slots_ref, seg_q_ref, seg_k_ref, valid_k_ref, q_ref, k_ref, v_ref,
    o_ref, lse_ref, bias_ref, acc_ref, peak_ref, total_ref,
):
    rows = q_ref.shape[-1]

    @pl.when(pl.program_id(0) == 0)
    def _():
        fill_bias(blocks_ref, seg_q_ref, seg_k_ref, valid_k_ref, bias_ref, rows)

    for side in range(2):
        b = blocks_ref[side]
        lo = first_block(b, rows)
        acc_ref[...] = jnp.zeros_like(acc_ref)
        total_ref[...] = jnp.zeros_like(total_ref)
        peak_ref[...] = jnp.full_like(peak_ref, -jnp.inf)

        def body(kb, _):
            slot = slots_ref[kb]
            keys = k_ref[slot, 0].T
            values_t = v_ref[slot, 0]
            bias = bias_ref[side, kb - lo]
            for h in range(GROUP):
                query = q_ref[side, h]
                s = dot(keys, query, ((1,), (0,))) + bias
                peak_old = peak_ref[h : h + 1]
                peak = jnp.maximum(peak_old, jnp.max(s, axis=0, keepdims=True))
                p = jnp.exp(s - peak)
                shrink = jnp.exp(peak_old - peak)
                peak_ref[h : h + 1] = peak
                total_ref[h : h + 1] = total_ref[h : h + 1] * shrink + jnp.sum(
                    p, axis=0, keepdims=True
                )
                acc_ref[h] = acc_ref[h] * shrink + dot(values_t, p.astype(BF16), ((1,), (0,)))
            return 0

        body(b, 0)
        lax.fori_loop(lo, b, body, 0)
        for h in range(GROUP):
            total = total_ref[h : h + 1]
            o_ref[side, h] = (acc_ref[h] / total).astype(BF16)
            lse_ref[side, 0, h : h + 1] = peak_ref[h : h + 1] + jnp.log(total)


def backward_kernel(
    blocks_ref, slots_ref, seg_q_ref, seg_k_ref, valid_k_ref, cos_ref, sin_ref, q_ref, k_ref, v_ref,
    o_ref, do_ref, lse_ref,
    dq_ref, dkv_ref, bias_ref, acc_ref, center_ref, dk_ref, dv_ref,
):
    rows = q_ref.shape[-1]

    @pl.when(pl.program_id(0) == 0)
    def _():
        fill_bias(blocks_ref, seg_q_ref, seg_k_ref, valid_k_ref, bias_ref, rows)

    dk_ref[...] = jnp.zeros_like(dk_ref)
    dv_ref[...] = jnp.zeros_like(dv_ref)
    for side in range(2):
        b = blocks_ref[side]
        lo = first_block(b, rows)
        acc_ref[...] = jnp.zeros_like(acc_ref)
        for h in range(GROUP):
            center_ref[h : h + 1] = jnp.sum(
                o_ref[side, h].astype(F32) * do_ref[side, h].astype(F32), axis=0, keepdims=True
            )

        def body(kb, _):
            slot = slots_ref[kb]
            keys_t = k_ref[slot, 0]
            keys = keys_t.T
            values = v_ref[slot, 0].T
            bias = bias_ref[side, kb - lo]
            for h in range(GROUP):
                query_t = q_ref[side, h]
                grad_t = do_ref[side, h]
                s = dot(keys, query_t, ((1,), (0,))) + bias
                p = jnp.exp(s - lse_ref[side, 0, h : h + 1])
                dp = dot(values, grad_t, ((1,), (0,)))
                ds = (p * (dp - center_ref[h : h + 1])).astype(BF16)
                dv_ref[slot] += dot(grad_t, p.astype(BF16), ((1,), (1,)))
                dk_ref[slot] += dot(query_t, ds, ((1,), (1,)))
                acc_ref[h] += dot(keys_t, ds, ((1,), (0,)))
            return 0

        lax.fori_loop(lo, b + 1, body, 0)
        half = HEAD_DIM // 2
        cos, sin = cos_ref[side], sin_ref[side]
        for h in range(GROUP):
            a, b = acc_ref[h, :half] * 0.125, acc_ref[h, half:] * 0.125
            turned = jnp.concatenate([a * cos + b * sin, b * cos - a * sin], axis=0)
            dq_ref[side, h] = turned.astype(BF16)
    dkv_ref[:, 0, 0] = dk_ref[...].astype(BF16)
    dkv_ref[:, 1, 0] = dv_ref[...].astype(BF16)


def project(c, f, tokens_all, mine, other, cosine, sine, q_width):
    blocks, rows, width = tokens_all.shape
    _, nz, r, cols = mine.shape
    half = HEAD_DIM // 2
    kv_heads = 2 * KV_HEADS
    gains_at = q_width + kv_heads * HEAD_DIM

    def turned(flat_t, at, cos, sin):
        a, b = flat_t[at : at + half], flat_t[at + half : at + HEAD_DIM]
        return jnp.concatenate([a * cos - b * sin, a * sin + b * cos], axis=0)

    def kernel(
        at_ref, x_ref, mine_ref, other_ref, cos_ref, sin_ref,
        first_ref, q_ref, kv_ref, w_ref, gain_ref,
    ):
        @pl.when(pl.program_id(0) == 0)
        def _():
            for core in range(2):

                @pl.when(at_ref[1] % 2 == core)
                def _():
                    for z in range(nz):
                        step = (at_ref[1] // 2 - z + nz) % nz
                        for q in range(4):
                            for kk in range(2):
                                source = mine_ref if kk == core else other_ref
                                at = (2 * z + kk) * r
                                w_ref[at : at + r, q * cols : (q + 1) * cols] = source[
                                    q ^ at_ref[0], step
                                ]

            gain_ref[...] = w_ref[:, gains_at:].astype(F32).T[:8]

        x = x_ref[0].astype(F32)
        inverse = lax.rsqrt(jnp.mean(x * x, axis=-1, keepdims=True) + EPSILON)
        first = (x * inverse * gain_ref[0:1]).astype(BF16)
        first_ref[0] = first
        cos, sin = cos_ref[0], sin_ref[0]
        kv = dot(first, w_ref[:, q_width:gains_at], ((1,), (0,))).T
        for h in range(kv_heads):
            at = h * HEAD_DIM
            if h < KV_HEADS:
                kv_ref[0, h] = turned(kv, at, cos, sin).astype(BF16)
            else:
                kv_ref[0, h] = kv[at : at + HEAD_DIM].astype(BF16)

        @pl.when(pl.program_id(0) < 2)
        def _():
            q = dot(first, w_ref[:, :q_width], ((1,), (0,))).T
            for h in range(HEADS):
                turned_q = turned(q, h * HEAD_DIM, cos, sin).astype(BF16)
                q_ref[0, h] = (turned_q.astype(F32) * 0.125).astype(BF16)

    table = pl.BlockSpec((1, half, rows), lambda i, s: (i, 0, 0))
    piece = pl.BlockSpec(mine.shape, lambda i, s: (0, 0, 0, 0))
    return pl.pallas_call(
        kernel,
        grid_spec=pltpu.PrefetchScalarGridSpec(
            num_scalar_prefetch=1,
            grid=(blocks,),
            in_specs=[
                pl.BlockSpec((1, rows, width), lambda i, s: (i, 0, 0)),
                piece,
                piece,
                table,
                table,
            ],
            out_specs=[
                pl.BlockSpec((1, rows, width), lambda i, s: (i, 0, 0)),
                pl.BlockSpec(
                    (1, HEADS, HEAD_DIM, rows), lambda i, s: (jnp.minimum(i, 1), 0, 0, 0)
                ),
                pl.BlockSpec((1, kv_heads, HEAD_DIM, rows), lambda i, s: (i, 0, 0, 0)),
                pl.BlockSpec((2 * nz * r, 4 * cols), lambda i, s: (0, 0)),
                pl.BlockSpec((8, width), lambda i, s: (0, 0)),
            ],
        ),
        out_shape=[
            jax.ShapeDtypeStruct((blocks, rows, width), BF16),
            jax.ShapeDtypeStruct((2, HEADS, HEAD_DIM, rows), BF16),
            jax.ShapeDtypeStruct((blocks, kv_heads, HEAD_DIM, rows), BF16),
            jax.ShapeDtypeStruct((2 * nz * r, 4 * cols), BF16),
            jax.ShapeDtypeStruct((8, width), F32),
        ],
        compiler_params=pltpu.CompilerParams(vmem_limit_bytes=56 * 2**20),
        cost_estimate=pl.CostEstimate(
            flops=8_000_000_000, bytes_accessed=25_000_000, transcendentals=0
        ),
    )(jnp.stack([c, f]).astype(jnp.int32), tokens_all, mine, other, cosine, sine)


def kernel_specs(blocks, rows):
    q_spec = pl.BlockSpec((2, GROUP, HEAD_DIM, rows), lambda g, *_: (0, g, 0, 0))
    k_spec = pl.BlockSpec((blocks, 1, HEAD_DIM, rows), lambda g, *_: (0, g, 0, 0))
    v_spec = pl.BlockSpec((blocks, 1, HEAD_DIM, rows), lambda g, *_: (0, KV_HEADS + g, 0, 0))
    stat_spec = pl.BlockSpec((2, 1, GROUP, rows), lambda g, *_: (0, g, 0, 0))
    seg_specs = [
        pl.BlockSpec((2, 1, rows), lambda g, *_: (0, 0, 0)),
        pl.BlockSpec((blocks, rows, 1), lambda g, *_: (0, 0, 0)),
        pl.BlockSpec((blocks, rows, 1), lambda g, *_: (0, 0, 0)),
    ]
    return q_spec, k_spec, v_spec, stat_spec, seg_specs


def attention_forward(q_blocks, slots, seg_q, seg_k, valid_k, q_t, kv_t):
    blocks, _, _, rows = kv_t.shape
    q_spec, k_spec, v_spec, stat_spec, seg_specs = kernel_specs(blocks, rows)
    reach = (WINDOW + rows - 2) // rows + 1
    return pl.pallas_call(
        forward_kernel,
        grid_spec=pltpu.PrefetchScalarGridSpec(
            num_scalar_prefetch=2,
            grid=(KV_HEADS,),
            in_specs=seg_specs + [q_spec, k_spec, v_spec],
            out_specs=[q_spec, stat_spec],
            scratch_shapes=[
                pltpu.VMEM((2, reach, rows, rows), F32),
                pltpu.VMEM((GROUP, HEAD_DIM, rows), F32),
                pltpu.VMEM((GROUP, rows), F32),
                pltpu.VMEM((GROUP, rows), F32),
            ],
        ),
        out_shape=[
            jax.ShapeDtypeStruct(q_t.shape, BF16),
            jax.ShapeDtypeStruct((2, KV_HEADS, GROUP, rows), F32),
        ],
        compiler_params=pltpu.CompilerParams(vmem_limit_bytes=40 * 2**20),
        cost_estimate=pl.CostEstimate(
            flops=20_000_000_000, bytes_accessed=6_000_000, transcendentals=0
        ),
    )(q_blocks, slots, seg_q, seg_k, valid_k, q_t, kv_t, kv_t)


def attention_backward(q_blocks, slots, seg_q, seg_k, valid_k, cos, sin, q_t, kv_t, o_t, do_t, lse):
    blocks, _, _, rows = kv_t.shape
    q_spec, k_spec, v_spec, stat_spec, seg_specs = kernel_specs(blocks, rows)
    reach = (WINDOW + rows - 2) // rows + 1
    table = pl.BlockSpec((2, HEAD_DIM // 2, rows), lambda g, *_: (0, 0, 0))
    dkv_spec = pl.BlockSpec((blocks, 2, 1, HEAD_DIM, rows), lambda g, *_: (0, 0, g, 0, 0))
    return pl.pallas_call(
        backward_kernel,
        grid_spec=pltpu.PrefetchScalarGridSpec(
            num_scalar_prefetch=2,
            grid=(KV_HEADS,),
            in_specs=seg_specs
            + [table, table, q_spec, k_spec, v_spec, q_spec, q_spec, stat_spec],
            out_specs=[q_spec, dkv_spec],
            scratch_shapes=[
                pltpu.VMEM((2, reach, rows, rows), F32),
                pltpu.VMEM((GROUP, HEAD_DIM, rows), F32),
                pltpu.VMEM((GROUP, rows), F32),
                pltpu.VMEM((blocks, HEAD_DIM, rows), F32),
                pltpu.VMEM((blocks, HEAD_DIM, rows), F32),
            ],
        ),
        out_shape=[
            jax.ShapeDtypeStruct(q_t.shape, BF16),
            jax.ShapeDtypeStruct((blocks, 2, KV_HEADS, HEAD_DIM, rows), BF16),
        ],
        compiler_params=pltpu.CompilerParams(vmem_limit_bytes=48 * 2**20),
        cost_estimate=pl.CostEstimate(
            flops=40_000_000_000, bytes_accessed=16_000_000, transcendentals=0
        ),
    )(q_blocks, slots, seg_q, seg_k, valid_k, cos, sin, q_t, kv_t, kv_t, o_t, do_t, lse)


def norm_forward(value_rows, gain):
    inverse = lax.rsqrt(jnp.mean(value_rows * value_rows, axis=-1, keepdims=True) + EPSILON)
    normed = value_rows * inverse
    return (normed * gain, normed, inverse)


def norm_backward(upstream, gain, normed, inverse):
    scaled = upstream * gain
    grad_in = inverse * (scaled - normed * jnp.mean(scaled * normed, axis=-1, keepdims=True))
    return (grad_in, jnp.sum(upstream * normed, axis=0))


def ein(spec, left, right):
    return jnp.einsum(spec, left, right, preferred_element_type=F32)


def turn(v, cosine, sine):
    half = HEAD_DIM // 2
    a, b = v[:, :, :half], v[:, :, half:]
    return jnp.concatenate([a * cosine - b * sine, a * sine + b * cosine], axis=2)


def per_device(
    tokens, cotangent, segments, valid, norm_one, w_query, w_key, w_value, w_out,
    norm_two, w_gate, w_up, w_down,
):
    c = lax.axis_index("ctx")
    n = lax.axis_size("fsdp")
    f = lax.axis_index("fsdp")
    row_count = tokens.shape[1]
    rows = row_count // 2
    width = tokens.shape[2]
    blocks = 8
    q_width, kv_width = w_query.shape[1], w_key.shape[1]
    ff = w_gate.shape[1]
    r = w_query.shape[0]
    c_ref = c.reshape(1).astype(jnp.int32)

    q_blocks = jnp.stack([c, blocks - 1 - c]).astype(jnp.int32)
    seg_blocks = segments[0].reshape(blocks, rows)
    valid_blocks = valid[0].reshape(blocks, rows)
    seg_q = jnp.stack([take(seg_blocks, q_blocks[0], 0), take(seg_blocks, q_blocks[1], 0)])
    live = jnp.stack([take(valid_blocks, q_blocks[0], 0), take(valid_blocks, q_blocks[1], 0)])
    seg_q = seg_q[:, None, :]
    seg_k = seg_blocks[:, :, None]
    valid_k = valid_blocks[:, :, None]
    owners = c ^ jnp.arange(4, dtype=jnp.int32)
    block_of = jnp.stack([owners, blocks - 1 - owners], axis=1)
    every = jnp.arange(blocks, dtype=jnp.int32)
    side = (every >= 4).astype(jnp.int32)
    slots = (c ^ jnp.where(every < 4, every, blocks - 1 - every)) * 2 + side
    slots = slots.astype(jnp.int32)
    places = block_of[:, :, None] * rows + jnp.arange(rows, dtype=jnp.int32)
    half = HEAD_DIM // 2
    freqs = jnp.exp(jnp.arange(half, dtype=F32) * (-math.log(ROPE_BASE) / half))
    angles = places.astype(F32).reshape(8, 1, rows) * freqs[None, :, None]
    cosine, sine = jnp.cos(angles), jnp.sin(angles)

    tokens_own = tokens[0].reshape(2, rows, width)
    tokens_x, tokens_y = swap_x(tokens_own), swap_y(tokens_own)
    gains = jnp.stack([norm_one, norm_two], axis=1)
    gains = jnp.concatenate([gains, jnp.zeros((r, 126), BF16)], axis=1)
    qkv_shard = jnp.concatenate([w_query, w_key, w_value, gains], axis=1)
    c4 = qkv_shard.shape[1] // 4
    qkv_z = z_fetch(lax.dynamic_slice_in_dim(qkv_shard, c * c4, c4, 1))
    out_w = lax.all_gather(w_out, "fsdp", axis=0, tiled=True)
    qkv_z, tokens_x, tokens_y = sync(qkv_z, tokens_x, tokens_y)
    qkv_x, qkv_y = swap_x(qkv_z), swap_y(qkv_z)
    gu_shard = after(pick_columns(c_ref, w_gate, w_up, n), qkv_z)
    gu_w = lax.all_gather(gu_shard, "fsdp", axis=0, tiled=True)
    d4 = w_down.shape[0] // 4
    down_shard = after(lax.dynamic_slice_in_dim(w_down, c * d4, d4, 0), gu_shard)
    down_w = lax.all_gather(down_shard, "fsdp", axis=0, tiled=True)
    cut = ff // 4
    qkv_x, qkv_y, tokens_x, tokens_y = sync(qkv_x, qkv_y, tokens_x, tokens_y)
    zh = qkv_z.shape[0] // 2
    qkv_d = jnp.concatenate([swap_y(qkv_x[:zh]), swap_x(qkv_y[zh:])])
    tokens_d = jnp.concatenate([swap_y(tokens_x[:1]), swap_x(tokens_y[1:])])
    qkv_mine = jnp.stack([qkv_z, qkv_x, qkv_y, qkv_d])
    qkv_other = core_swap(qkv_mine)
    tokens_all = jnp.stack([tokens_own, tokens_x, tokens_y, tokens_d])
    dy_own = cotangent[0].reshape(2, rows, width)
    dy_pieces = ctx_fetch_direct(after(dy_own, qkv_mine, tokens_d))

    first_all, q_t, kv_all, qkv_w, gain_rows = project(
        c, f, tokens_all.reshape(8, rows, width), qkv_mine, qkv_other, cosine, sine, q_width
    )
    gain_one, gain_two = gain_rows[0], gain_rows[1]
    first_all = first_all.reshape(4, 2, rows, width)
    qkv_w = qkv_w[:, : q_width + 2 * kv_width]
    inputs = tokens[0].astype(F32)
    _, unit_one, inverse_one = norm_forward(inputs, gain_one)
    o_t, lse = attention_forward(q_blocks, slots, seg_q, seg_k, valid_k, q_t, kv_all)
    o_t, out_w, dy_pieces, gu_w, down_w = sync(o_t, out_w, dy_pieces, gu_w, down_w)
    dy_all = jnp.stack(dy_pieces).reshape(-1, width)
    attended_t = o_t.reshape(2, width, rows)
    branch_attn = ein("bfr,fo->bro", attended_t, out_w).reshape(row_count, width)
    middle = inputs + branch_attn

    normed_two, unit_two, inverse_two = norm_forward(middle, gain_two)
    second_in = normed_two.astype(BF16)
    x_own = second_in.reshape(2, rows, width)
    x_x, x_y = swap_x(x_own), swap_y(x_own)
    d_hidden = ein("ro,fo->rf", dy_all, down_w)

    def gated(x, d_hidden):
        gu = ein("bri,if->brf", x, gu_w).reshape(-1, 2 * cut)
        gate_pre, up_pre = gu[:, :cut], gu[:, cut:]
        sig = jax.nn.sigmoid(gate_pre)
        swish = gate_pre * sig
        slope = sig * (1.0 + gate_pre * (1.0 - sig))
        d_gu = [(d_hidden * up_pre * slope).astype(BF16), (d_hidden * swish).astype(BF16)]
        return (swish * up_pre).astype(BF16), jnp.concatenate(d_gu, axis=1)

    def back(d_gu):
        return ein("rf,if->ri", d_gu, gu_w).astype(BF16).reshape(-1, 2, rows, width)

    hidden_0, d_gu_0 = gated(x_own, d_hidden[:row_count])
    x_x, x_y, hidden_0, d_gu_0 = lax.optimization_barrier((x_x, x_y, hidden_0, d_gu_0))
    x_d = jnp.concatenate([swap_y(x_x[:1]), swap_x(x_y[1:])])
    x_xy = jnp.concatenate([x_x, x_y])
    hidden_1, d_gu_1 = gated(x_xy, d_hidden[row_count : 3 * row_count])
    parts_1 = back(d_gu_1)
    x_d, parts_1 = lax.optimization_barrier((x_d, parts_1))
    hidden_2, d_gu_2 = gated(x_d, d_hidden[3 * row_count :])
    parts_2 = back(d_gu_2)
    d_gu_0 = after(d_gu_0, parts_2)
    parts_0 = back(d_gu_0)
    parts = [parts_0[0], parts_1[0], parts_1[1], parts_2[0]]
    got = scatter_first(parts)
    x_all = jnp.concatenate([x_own, x_xy, x_d]).reshape(-1, width)
    d_gu = jnp.concatenate([d_gu_0, d_gu_1, d_gu_2])
    hidden = jnp.concatenate([hidden_0, hidden_1, hidden_2])
    grad_gu = ein("ri,rf->if", x_all, d_gu).astype(BF16)
    got_low, got_high, grad_gu = lax.optimization_barrier((*got, grad_gu))
    d_second = scatter_last(*scatter_pass(parts, (got_low, got_high))).reshape(row_count, width)
    grad_d = ein("rf,ro->fo", after(hidden, grad_gu), dy_all).astype(BF16)
    ffn_parts = ein("rf,fo->ro", after(hidden, grad_d), down_w).astype(BF16)
    d_second, ffn_parts = lax.optimization_barrier((d_second, ffn_parts))
    ffn_parts = ffn_parts.reshape(4, 2, rows, width)
    ffn_parts = [ffn_parts[i] for i in range(4)]
    ffn_got = scatter_first(ffn_parts)
    own_gu = lax.psum_scatter(grad_gu, "fsdp", scatter_dimension=0, tiled=True)
    own_down = lax.psum_scatter(grad_d, "fsdp", scatter_dimension=0, tiled=True)

    k = f % 2
    nz = n // 2
    r4 = r // 4
    grad_output = cotangent[0].astype(F32)
    grad_mid_norm, grad_gain_two = norm_backward(d_second, gain_two, unit_two, inverse_two)
    grad_middle = grad_output + grad_mid_norm
    d_branch = grad_middle.astype(BF16).reshape(2, rows, width)
    do_t = ein("fo,bro->bfr", out_w, d_branch).astype(BF16).reshape(2, HEADS, HEAD_DIM, rows)
    whole_out = ein("bfr,bro->fo", attended_t, d_branch).astype(BF16).reshape(n, 4, r4, width)
    out_parts = [take(whole_out, c ^ i, 1) for i in range(4)]
    out_got = scatter_first(out_parts)
    d_q, dkv = attention_backward(
        q_blocks, slots, seg_q, seg_k, valid_k, cosine[:2], sine[:2], q_t, kv_all, o_t, do_t, lse
    )
    d_q, dkv, ffn_got, out_got = sync(d_q, dkv, ffn_got, out_got)
    dkv = dkv.reshape(4, 2, 2 * KV_HEADS, HEAD_DIM, rows)
    dkv = [dkv[i] for i in range(4)]
    dkv_got = scatter_first(dkv)
    q4, kv4 = q_width // 4, kv_width // 2

    def quarter(v, size, i):
        return lax.dynamic_slice_in_dim(v, (c ^ i) * size, size, 1)

    d_q = d_q.reshape(2, q_width, rows)
    dq_parts = [quarter(d_q, q4, i) for i in range(4)]
    out_sums = scatter_pass(out_parts, out_got)
    dkv_got, dq_parts, out_sums = sync(dkv_got, dq_parts, out_sums)
    dkv_own = scatter_last(*scatter_pass(dkv, dkv_got))
    dq_got = exchange_first(dq_parts)
    d_k = turn(dkv_own[:, :KV_HEADS], cosine[:2, None], -sine[:2, None]).astype(BF16)
    d_kv = jnp.concatenate([d_k, dkv_own[:, KV_HEADS:].astype(BF16)], axis=1)
    d_kv = d_kv.reshape(2, 2 * kv_width, rows)
    dkv_parts = [quarter(d_kv, kv4, i) for i in range(4)]
    dkv_parts, out_sums = sync(dkv_parts, out_sums)
    dkv_got = exchange_first(dkv_parts)
    own_out = scatter_last(*out_sums).astype(BF16)
    dq_got, dkv_got = sync(dq_got, dkv_got)
    dq_all = jnp.stack(exchange_second(dq_parts, *dq_got))
    dkv_all = jnp.stack(exchange_second(dkv_parts, *dkv_got))
    grad_q = ein("gbri,gbfr->if", first_all, dq_all).astype(BF16)
    grad_kv = ein("gbri,gbfr->if", first_all, dkv_all).astype(BF16)
    grad_qkv = jnp.concatenate([grad_q, grad_kv], axis=1).reshape(nz, 2, r, q4 + kv4)
    own_out = own_out.reshape(nz, 2, r4, width)
    grad_qkv, own_out, own_gu = sync(grad_qkv, own_out, own_gu)

    def pair_sum(v):
        got = core_swap(take(v, k ^ 1, 1))
        return (take(v, k, 1).astype(F32) + got.astype(F32)).astype(BF16)

    pair_qkv, pair_out = sync(pair_sum(grad_qkv), pair_sum(own_out))
    own_qkv = z_scatter(pair_qkv).astype(BF16)
    own_out = z_scatter(pair_out).astype(BF16)

    d_q, d_kv, ffn_got, own_gu, _ = sync(d_q, d_kv, ffn_got, own_gu, pair_qkv)
    branch_ffn = scatter_last(*scatter_pass(ffn_parts, ffn_got)).reshape(row_count, width)
    result = middle + branch_ffn
    gu_x, gu_y = swap_x(own_gu), swap_y(own_gu)
    d_first = ein("bfr,if->bri", d_q, qkv_w[:, :q_width]) + ein(
        "bfr,if->bri", d_kv, qkv_w[:, q_width:]
    )
    grad_in_norm, grad_gain_one = norm_backward(
        d_first.reshape(row_count, width), gain_one, unit_one, inverse_one
    )
    grad_inputs = grad_middle + grad_in_norm
    own_qkv, own_out, gu_x, gu_y, own_down = sync(own_qkv, own_out, gu_x, gu_y, own_down)
    hr = gu_x.shape[0] // 2
    gu_d = jnp.concatenate([swap_y(gu_x[:hr]), swap_x(gu_y[hr:])])
    grad_gate_w, grad_up_w = unpick_columns(c_ref, [own_gu, gu_x, gu_y, gu_d], n)
    grad_down_w = ctx_gather(own_down, 0).reshape(4 * d4, width).astype(F32)
    grad_out_w = ctx_gather(own_out, 0).reshape(r, width).astype(F32)
    grad_qkv = ctx_gather(own_qkv, 1).astype(F32)
    grad_q = grad_qkv[:, :, :q4].reshape(r, q_width)
    grad_kv = grad_qkv[:, :, q4:].reshape(r, 2 * kv_width)

    live_rows = live.reshape(row_count, 1).astype(F32)
    squares = jnp.stack(
        [
            jnp.sum(live_rows * member * member)
            for member in (result, grad_inputs, branch_attn, branch_ffn, middle)
        ]
        + [jnp.sum(live_rows)]
    )
    small = small_sum(jnp.concatenate([grad_gain_one, grad_gain_two, squares]))
    gain_sums = lax.dynamic_slice_in_dim(small[: 2 * width].reshape(2, width), f * r, r, 1)
    squares = small[2 * width :]
    spreads = jnp.sqrt(squares[:5] / (squares[5] * width))
    return (
        result[None].astype(BF16),
        grad_inputs[None].astype(BF16),
        gain_sums[0],
        grad_q,
        grad_kv[:, :kv_width],
        grad_kv[:, kv_width:],
        grad_out_w,
        gain_sums[1],
        grad_gate_w,
        grad_up_w,
        grad_down_w,
        spreads,
    )


def solution(mesh):
    rows, shard, vector = P("fsdp", "ctx", None), P("fsdp", None), P("fsdp")
    return jax.shard_map(
        per_device,
        mesh=mesh,
        in_specs=(
            rows, rows, shard, shard, vector, shard, shard, shard, shard, vector,
            shard, shard, shard,
        ),
        out_specs=(
            rows, rows, vector, shard, shard, shard, shard, vector, shard, shard, shard, P(),
        ),
        check_vma=False,
    )
```

```python
import functools
import math

import jax
import jax.numpy as jnp
from jax import lax
from jax.experimental import pallas as pl
from jax.experimental.pallas import tpu as pltpu
from jax.sharding import PartitionSpec as P

HEADS = 20
KV_HEADS = 5
HEAD_DIM = 64
GROUP = HEADS // KV_HEADS
WINDOW = 1024
EPSILON = 1e-05
MASKED = -1e30
ROPE_BASE = 10000.0
VMEM_LIMIT = 60 * 2**20
BF16 = jnp.bfloat16
F32 = jnp.float32


def core_swap(v):
    n = lax.axis_size("fsdp")
    return lax.ppermute(v, "fsdp", [(i, i ^ 1) for i in range(n)])


def swap_x(v):
    return lax.ppermute(v, "ctx", [(i, i ^ 1) for i in range(4)])


def swap_y(v):
    return lax.ppermute(v, "ctx", [(i, i ^ 2) for i in range(4)])


def put(buffer, piece, index, axis):
    return lax.dynamic_update_slice_in_dim(
        buffer, jnp.expand_dims(piece, axis), index, axis
    )


def take(v, index, axis):
    return lax.dynamic_index_in_dim(v, index, axis, keepdims=False)


def place(pieces, axis):
    first = pieces[0][1]
    shape = first.shape[:axis] + (len(pieces),) + first.shape[axis:]
    buffer = jnp.zeros(shape, first.dtype)
    for index, piece in pieces:
        buffer = put(buffer, piece, index, axis)
    return buffer


def z_fetch(piece):
    n = lax.axis_size("fsdp")
    nz = n // 2
    if nz != 4:
        groups = [list(range(0, n, 2)), list(range(1, n, 2))]
        every = lax.all_gather(piece, "fsdp", axis=0, axis_index_groups=groups)
        z = lax.axis_index("fsdp") // 2
        return jnp.take(every, (z - jnp.arange(nz)) % nz, axis=0)
    pieces = [piece]
    for d in (1, 2, 3):
        pieces.append(lax.ppermute(piece, "fsdp", [(i, (i + 2 * d) % n) for i in range(n)]))
    return jnp.stack(pieces)


def z_scatter(pieces):
    n = lax.axis_size("fsdp")
    nz = n // 2
    if nz != 4:
        groups = [list(range(0, n, 2)), list(range(1, n, 2))]
        return lax.psum_scatter(
            pieces, "fsdp", scatter_dimension=0, axis_index_groups=groups
        ).astype(F32)
    z = lax.axis_index("fsdp") // 2
    total = take(pieces, z, 0).astype(F32)
    for d in (1, 2, 3):
        sent = take(pieces, (z + d) % nz, 0)
        got = lax.ppermute(sent, "fsdp", [(i, (i + 2 * d) % n) for i in range(n)])
        total = total + got.astype(F32)
    return total


def sync(*values):
    return lax.optimization_barrier(values)


def ctx_fetch(piece):
    half = piece.shape[0] // 2
    from_x = swap_x(piece)
    from_y = swap_y(piece)
    from_d = jnp.concatenate([swap_y(from_x[:half]), swap_x(from_y[half:])], axis=0)
    return [piece, from_x, from_y, from_d]


def after(v, *earlier):
    return lax.optimization_barrier((v, earlier))[0]


def ctx_fetch_direct(piece):
    diagonal = lax.ppermute(piece, "ctx", [(i, i ^ 3) for i in range(4)])
    return [piece, swap_x(piece), swap_y(piece), diagonal]


def in_order(pieces, axis):
    c = lax.axis_index("ctx")
    return place([(c ^ i, v) for i, v in enumerate(pieces)], axis)


def scatter_first(parts):
    half = parts[0].shape[0] // 2
    low_got = swap_x(jnp.concatenate([parts[1][:half], parts[3][:half]]))
    high_got = swap_y(jnp.concatenate([parts[2][half:], parts[3][half:]]))
    return low_got, high_got


def scatter_pass(parts, got):
    half = parts[0].shape[0] // 2
    rest = parts[0].shape[0] - half
    low_got, high_got = got[0].astype(F32), got[1].astype(F32)
    low_pass = (parts[2][:half].astype(F32) + low_got[half:]).astype(BF16)
    high_pass = (parts[1][half:].astype(F32) + high_got[rest:]).astype(BF16)
    low_own = parts[0][:half].astype(F32) + low_got[:half]
    high_own = parts[0][half:].astype(F32) + high_got[:rest]
    return low_own, high_own, low_pass, high_pass


def scatter_last(low_own, high_own, low_pass, high_pass):
    from_y, from_x = swap_y(low_pass), swap_x(high_pass)
    return jnp.concatenate([low_own + from_y.astype(F32), high_own + from_x.astype(F32)])


def exchange_first(parts):
    to_x = jnp.concatenate([parts[1], parts[3][:1]], axis=0)
    to_y = jnp.concatenate([parts[2], parts[3][1:]], axis=0)
    return swap_x(to_x), swap_y(to_y)


def exchange_second(got_x, got_y):
    return swap_y(got_x[2:]), swap_x(got_y[2:])


def z_sum(v):
    n = lax.axis_size("fsdp")
    if n == 8:
        return v + sum(
            lax.ppermute(v, "fsdp", [(i, (i + 2 * d) % n) for i in range(n)]) for d in (1, 2, 3)
        )
    bit = 2
    while bit < n:
        v = v + lax.ppermute(v, "fsdp", [(i, i ^ bit) for i in range(n)])
        bit *= 2
    return v


def pick_columns(c, gate, up, count):
    r, ff = gate.shape
    group = ff // count
    strip = group // 4

    def kernel(c_ref, gate_ref, up_ref, out_ref):
        for own in range(4):

            @pl.when(c_ref[0] == own)
            def _():
                for j in range(count):
                    at = j * group + own * strip
                    out_ref[:, j * strip : (j + 1) * strip] = gate_ref[:, at : at + strip]
                    to = ff // 4 + j * strip
                    out_ref[:, to : to + strip] = up_ref[:, at : at + strip]

    whole = pl.BlockSpec((r, ff), lambda i, s: (0, 0))
    return pl.pallas_call(
        kernel,
        grid_spec=pltpu.PrefetchScalarGridSpec(
            num_scalar_prefetch=1,
            grid=(1,),
            in_specs=[whole, whole],
            out_specs=pl.BlockSpec((r, ff // 2), lambda i, s: (0, 0)),
        ),
        out_shape=jax.ShapeDtypeStruct((r, ff // 2), BF16),
        cost_estimate=pl.CostEstimate(flops=0, bytes_accessed=6 * r * ff, transcendentals=0),
    )(c, gate, up)


def unpick_columns(c, pieces, count):
    r, half = pieces[0].shape
    ff = 2 * half
    group = ff // count
    strip = group // 4

    def kernel(c_ref, *refs):
        gate_ref, up_ref = refs[4:]
        for own in range(4):

            @pl.when(c_ref[0] == own)
            def _():
                for step in range(4):
                    for j in range(count):
                        at = j * group + (own ^ step) * strip
                        piece = refs[step]
                        gate_ref[:, at : at + strip] = piece[
                            :, j * strip : (j + 1) * strip
                        ].astype(F32)
                        frm = ff // 4 + j * strip
                        up_ref[:, at : at + strip] = piece[:, frm : frm + strip].astype(F32)

    whole = pl.BlockSpec((r, ff), lambda i, s: (0, 0))
    return pl.pallas_call(
        kernel,
        grid_spec=pltpu.PrefetchScalarGridSpec(
            num_scalar_prefetch=1,
            grid=(1,),
            in_specs=[pl.BlockSpec((r, half), lambda i, s: (0, 0))] * 4,
            out_specs=[whole, whole],
        ),
        out_shape=[jax.ShapeDtypeStruct((r, ff), F32)] * 2,
        compiler_params=pltpu.CompilerParams(vmem_limit_bytes=VMEM_LIMIT),
        cost_estimate=pl.CostEstimate(flops=0, bytes_accessed=12 * r * ff, transcendentals=0),
    )(c, *pieces)


def join_columns(c, pieces, q4, kv4):
    r = pieces[0].shape[0]

    def kernel(c_ref, *refs):
        q_ref, k_ref, v_ref = refs[4:]
        for own in range(4):

            @pl.when(c_ref[0] == own)
            def _():
                for step in range(4):
                    to = own ^ step
                    piece = refs[step][...].astype(F32)
                    q_ref[:, to * q4 : (to + 1) * q4] = piece[:, :q4]
                    target = k_ref if to < 2 else v_ref
                    at = (to % 2) * kv4
                    target[:, at : at + kv4] = piece[:, q4:]

    def whole(cols):
        return pl.BlockSpec((r, cols), lambda i, s: (0, 0))

    return pl.pallas_call(
        kernel,
        grid_spec=pltpu.PrefetchScalarGridSpec(
            num_scalar_prefetch=1,
            grid=(1,),
            in_specs=[whole(q4 + kv4)] * 4,
            out_specs=[whole(4 * q4), whole(2 * kv4), whole(2 * kv4)],
        ),
        out_shape=[
            jax.ShapeDtypeStruct((r, cols), F32) for cols in (4 * q4, 2 * kv4, 2 * kv4)
        ],
        cost_estimate=pl.CostEstimate(
            flops=0, bytes_accessed=24 * r * (q4 + kv4), transcendentals=0
        ),
    )(c, *pieces)


def pair_bias(q_block, k_block, rows, seg_q, seg_k, valid_k):
    key_at = k_block * rows + lax.broadcasted_iota(jnp.int32, (rows, rows), 0)
    query_at = q_block * rows + lax.broadcasted_iota(jnp.int32, (rows, rows), 1)
    distance = query_at - key_at
    allowed = (
        (seg_q == seg_k)
        & (distance >= 0)
        & (distance < WINDOW)
        & ((valid_k == 1) | (distance == 0))
    )
    return jnp.where(allowed, 0.0, MASKED).astype(F32)


def first_block(q_block, rows):
    reach = (WINDOW + rows - 2) // rows
    return jnp.maximum(q_block - reach, 0)


def dot(a, b, dims):
    return lax.dot_general(a, b, (dims, ((), ())), preferred_element_type=F32)


def fill_bias(blocks_ref, seg_q_ref, seg_k_ref, valid_k_ref, bias_ref, rows):
    for side in range(2):
        b = blocks_ref[side]
        lo = first_block(b, rows)

        def body(kb, _):
            bias_ref[side, kb - lo] = pair_bias(
                b, kb, rows, seg_q_ref[side], seg_k_ref[kb], valid_k_ref[kb]
            )
            return 0

        lax.fori_loop(lo, b + 1, body, 0)


def forward_kernel(
    blocks_ref, slots_ref, seg_q_ref, seg_k_ref, valid_k_ref, q_ref, k_ref, v_ref,
    o_ref, lse_ref, bias_ref, scores_ref, acc_ref,
):
    rows = q_ref.shape[-1]

    @pl.when(pl.program_id(0) == 0)
    def _():
        fill_bias(blocks_ref, seg_q_ref, seg_k_ref, valid_k_ref, bias_ref, rows)

    for side in range(2):
        b = blocks_ref[side]
        lo = first_block(b, rows)

        def score(kb, peaks):
            keys = k_ref[slots_ref[kb], 0].T
            bias = bias_ref[side, kb - lo]
            higher = []
            for h in range(GROUP):
                s = dot(keys, q_ref[side, h], ((1,), (0,))) + bias
                scores_ref[kb - lo, h] = s
                higher.append(jnp.maximum(peaks[h], jnp.max(s, axis=0, keepdims=True)))
            return tuple(higher)

        peaks = lax.fori_loop(
            lo, b + 1, score, (jnp.full((1, rows), -jnp.inf, F32),) * GROUP
        )
        acc_ref[...] = jnp.zeros_like(acc_ref)

        def mix(kb, totals):
            values_t = v_ref[slots_ref[kb], 0]
            more = []
            for h in range(GROUP):
                p = jnp.exp(scores_ref[kb - lo, h] - peaks[h])
                more.append(totals[h] + jnp.sum(p, axis=0, keepdims=True))
                acc_ref[h] += dot(values_t, p.astype(BF16), ((1,), (0,)))
            return tuple(more)

        totals = lax.fori_loop(lo, b + 1, mix, (jnp.zeros((1, rows), F32),) * GROUP)
        for h in range(GROUP):
            o_ref[side, h] = (acc_ref[h] / totals[h]).astype(BF16)
            lse_ref[side, 0, h : h + 1] = peaks[h] + jnp.log(totals[h])


def backward_kernel(
    blocks_ref, slots_ref, seg_q_ref, seg_k_ref, valid_k_ref, cos_ref, sin_ref, q_ref, k_ref, v_ref,
    o_ref, do_ref, lse_ref,
    dq_ref, low_ref, high_ref, keep_ref,
    bias_ref, acc_ref, center_ref, dk_ref, dv_ref, p_ref, ds_ref,
):
    rows = q_ref.shape[-1]
    half = HEAD_DIM // 2

    @pl.when(pl.program_id(0) == 0)
    def _():
        fill_bias(blocks_ref, seg_q_ref, seg_k_ref, valid_k_ref, bias_ref, rows)

    dk_ref[...] = jnp.zeros_like(dk_ref)
    dv_ref[...] = jnp.zeros_like(dv_ref)
    for side in range(2):
        b = blocks_ref[side]
        lo = first_block(b, rows)
        acc_ref[...] = jnp.zeros_like(acc_ref)
        for h in range(GROUP):
            center_ref[h : h + 1] = jnp.sum(
                o_ref[side, h].astype(F32) * do_ref[side, h].astype(F32), axis=0, keepdims=True
            )

        def soft(kb, at):
            slot = slots_ref[kb]
            keys = k_ref[slot, 0].T
            values = v_ref[slot, 0].T
            bias = bias_ref[side, kb - lo]
            for h in range(GROUP):
                s = dot(keys, q_ref[side, h], ((1,), (0,))) + bias
                p = jnp.exp(s - lse_ref[side, 0, h : h + 1])
                dp = dot(values, do_ref[side, h], ((1,), (0,)))
                p_ref[at, h] = p.astype(BF16)
                ds_ref[at, h] = (p * (dp - center_ref[h : h + 1])).astype(BF16)

        def products(kb, at):
            slot = slots_ref[kb]
            dv = dot(do_ref[side, 0], p_ref[at, 0], ((1,), (1,)))
            dk = dot(q_ref[side, 0], ds_ref[at, 0], ((1,), (1,)))
            for h in range(1, GROUP):
                dv += dot(do_ref[side, h], p_ref[at, h], ((1,), (1,)))
                dk += dot(q_ref[side, h], ds_ref[at, h], ((1,), (1,)))
            dv_ref[slot] += dv
            dk_ref[slot] += dk
            for h in range(GROUP):
                acc_ref[h] += dot(k_ref[slot, 0], ds_ref[at, h], ((1,), (0,)))

        soft(lo, 0)

        def body(kb, _):
            products(kb - 1, (kb - 1 - lo) % 2)
            soft(kb, (kb - lo) % 2)
            return 0

        lax.fori_loop(lo + 1, b + 1, body, 0)
        products(b, (b - lo) % 2)
        cos, sin = cos_ref[side], sin_ref[side]
        for h in range(GROUP):
            a, b2 = acc_ref[h, :half] * 0.125, acc_ref[h, half:] * 0.125
            turned = jnp.concatenate([a * cos + b2 * sin, b2 * cos - a * sin], axis=0)
            dq_ref[side, h] = turned.astype(BF16)
    for target, slots in ((low_ref, (2, 6)), (high_ref, (5, 7)), (keep_ref, (0, 4, 1, 3))):
        for i, slot in enumerate(slots):
            target[i, 0, 0] = dk_ref[slot].astype(BF16)
            target[i, 1, 0] = dv_ref[slot].astype(BF16)


def project(c, f, tokens_all, mine, other, cosine, sine, q_width):
    blocks, rows, width = tokens_all.shape
    _, nz, r, cols = mine.shape
    half = HEAD_DIM // 2
    kv_heads = 2 * KV_HEADS
    gains_at = q_width + kv_heads * HEAD_DIM

    def turned(flat_t, at, cos, sin):
        a, b = flat_t[at : at + half], flat_t[at + half : at + HEAD_DIM]
        return jnp.concatenate([a * cos - b * sin, a * sin + b * cos], axis=0)

    def kernel(
        at_ref, x_ref, mine_ref, other_ref, cos_ref, sin_ref,
        first_ref, q_ref, kv_ref, w_ref, gain_ref,
    ):
        @pl.when(pl.program_id(0) == 0)
        def _():
            for core in range(2):

                @pl.when(at_ref[1] % 2 == core)
                def _():
                    for z in range(nz):
                        step = (at_ref[1] // 2 - z + nz) % nz
                        for q in range(4):
                            for kk in range(2):
                                source = mine_ref if kk == core else other_ref
                                at = (2 * z + kk) * r
                                w_ref[at : at + r, q * cols : (q + 1) * cols] = source[
                                    q ^ at_ref[0], step
                                ]

            gain_ref[...] = w_ref[:, gains_at:].astype(F32).T[:8]

        x = x_ref[...].astype(F32)
        inverse = lax.rsqrt(jnp.mean(x * x, axis=-1, keepdims=True) + EPSILON)
        scaled = x * inverse * gain_ref[0:1][None]
        first_ref[...] = scaled.astype(BF16)
        first = scaled.reshape(2 * rows, width).astype(BF16)
        both = dot(first, w_ref[:, q_width:gains_at], ((1,), (0,)))
        for i in range(2):
            cos, sin = cos_ref[i], sin_ref[i]
            kv = both[i * rows : (i + 1) * rows].T
            for h in range(kv_heads):
                at = h * HEAD_DIM
                if h < KV_HEADS:
                    kv_ref[i, h] = turned(kv, at, cos, sin).astype(BF16)
                else:
                    kv_ref[i, h] = kv[at : at + HEAD_DIM].astype(BF16)

        @pl.when(pl.program_id(0) == 0)
        def _():
            both = dot(first, w_ref[:, :q_width], ((1,), (0,)))
            for i in range(2):
                cos, sin = cos_ref[i], sin_ref[i]
                q = both[i * rows : (i + 1) * rows].T
                for h in range(HEADS):
                    turned_q = turned(q, h * HEAD_DIM, cos, sin).astype(BF16)
                    q_ref[i, h] = (turned_q.astype(F32) * 0.125).astype(BF16)

    table = pl.BlockSpec((2, half, rows), lambda i, s: (i, 0, 0))
    piece = pl.BlockSpec(mine.shape, lambda i, s: (0, 0, 0, 0))
    return pl.pallas_call(
        kernel,
        grid_spec=pltpu.PrefetchScalarGridSpec(
            num_scalar_prefetch=1,
            grid=(blocks // 2,),
            in_specs=[
                pl.BlockSpec((2, rows, width), lambda i, s: (i, 0, 0)),
                piece,
                piece,
                table,
                table,
            ],
            out_specs=[
                pl.BlockSpec((2, rows, width), lambda i, s: (i, 0, 0)),
                pl.BlockSpec((2, HEADS, HEAD_DIM, rows), lambda i, s: (0, 0, 0, 0)),
                pl.BlockSpec((2, kv_heads, HEAD_DIM, rows), lambda i, s: (i, 0, 0, 0)),
                pl.BlockSpec((2 * nz * r, 4 * cols), lambda i, s: (0, 0)),
                pl.BlockSpec((8, width), lambda i, s: (0, 0)),
            ],
        ),
        out_shape=[
            jax.ShapeDtypeStruct((blocks, rows, width), BF16),
            jax.ShapeDtypeStruct((2, HEADS, HEAD_DIM, rows), BF16),
            jax.ShapeDtypeStruct((blocks, kv_heads, HEAD_DIM, rows), BF16),
            jax.ShapeDtypeStruct((2 * nz * r, 4 * cols), BF16),
            jax.ShapeDtypeStruct((8, width), F32),
        ],
        compiler_params=pltpu.CompilerParams(vmem_limit_bytes=VMEM_LIMIT),
        cost_estimate=pl.CostEstimate(
            flops=8_000_000_000, bytes_accessed=25_000_000, transcendentals=0
        ),
    )(jnp.stack([c, f]).astype(jnp.int32), tokens_all, mine, other, cosine, sine)


def project_grad(first_all, dq_pieces, dkv_pieces):
    _, rows, width = first_all.shape
    q4, kv4 = dq_pieces[0].shape[1], dkv_pieces[0].shape[1]

    def kernel(first_ref, *refs):
        out_ref = refs[-1]
        total = None
        for i, (piece, at) in enumerate(
            ((0, 0), (0, 1), (1, 0), (1, 1), (2, 0), (2, 1), (3, 0), (4, 0))
        ):
            turned = jnp.concatenate([refs[piece][at], refs[5 + piece][at]], axis=0)
            term = dot(turned, first_ref[i], ((1,), (0,)))
            total = term if total is None else total + term
        out_ref[...] = total.T.astype(BF16)

    operands = [first_all, *dq_pieces, *dkv_pieces]
    return pl.pallas_call(
        kernel,
        grid=(1,),
        in_specs=[fixed(v.shape) for v in operands],
        out_specs=fixed((width, q4 + kv4)),
        out_shape=jax.ShapeDtypeStruct((width, q4 + kv4), BF16),
        compiler_params=pltpu.CompilerParams(vmem_limit_bytes=VMEM_LIMIT),
        cost_estimate=BESIDE,
    )(*operands)


def kernel_specs(blocks, rows):
    q_spec = pl.BlockSpec((2, GROUP, HEAD_DIM, rows), lambda g, *_: (0, g, 0, 0))
    k_spec = pl.BlockSpec((blocks, 1, HEAD_DIM, rows), lambda g, *_: (0, g, 0, 0))
    v_spec = pl.BlockSpec((blocks, 1, HEAD_DIM, rows), lambda g, *_: (0, KV_HEADS + g, 0, 0))
    stat_spec = pl.BlockSpec((2, 1, GROUP, rows), lambda g, *_: (0, g, 0, 0))
    seg_specs = [
        pl.BlockSpec((2, 1, rows), lambda g, *_: (0, 0, 0)),
        pl.BlockSpec((blocks, rows, 1), lambda g, *_: (0, 0, 0)),
        pl.BlockSpec((blocks, rows, 1), lambda g, *_: (0, 0, 0)),
    ]
    return q_spec, k_spec, v_spec, stat_spec, seg_specs


def attention_forward(q_blocks, slots, seg_q, seg_k, valid_k, q_t, kv_t):
    blocks, _, _, rows = kv_t.shape
    q_spec, k_spec, v_spec, stat_spec, seg_specs = kernel_specs(blocks, rows)
    reach = (WINDOW + rows - 2) // rows + 1
    return pl.pallas_call(
        forward_kernel,
        grid_spec=pltpu.PrefetchScalarGridSpec(
            num_scalar_prefetch=2,
            grid=(KV_HEADS,),
            in_specs=seg_specs + [q_spec, k_spec, v_spec],
            out_specs=[q_spec, stat_spec],
            scratch_shapes=[
                pltpu.VMEM((2, reach, rows, rows), F32),
                pltpu.VMEM((reach, GROUP, rows, rows), F32),
                pltpu.VMEM((GROUP, HEAD_DIM, rows), F32),
            ],
        ),
        out_shape=[
            jax.ShapeDtypeStruct(q_t.shape, BF16),
            jax.ShapeDtypeStruct((2, KV_HEADS, GROUP, rows), F32),
        ],
        compiler_params=pltpu.CompilerParams(vmem_limit_bytes=VMEM_LIMIT),
        cost_estimate=pl.CostEstimate(
            flops=20_000_000_000, bytes_accessed=6_000_000, transcendentals=0
        ),
    )(q_blocks, slots, seg_q, seg_k, valid_k, q_t, kv_t, kv_t)


def attention_backward(q_blocks, slots, seg_q, seg_k, valid_k, cos, sin, q_t, kv_t, o_t, do_t, lse):
    blocks, _, _, rows = kv_t.shape
    q_spec, k_spec, v_spec, stat_spec, seg_specs = kernel_specs(blocks, rows)
    reach = (WINDOW + rows - 2) // rows + 1
    table = pl.BlockSpec((2, HEAD_DIM // 2, rows), lambda g, *_: (0, 0, 0))

    def dkv_spec(count):
        return pl.BlockSpec((count, 2, 1, HEAD_DIM, rows), lambda g, *_: (0, 0, g, 0, 0))

    def dkv_shape(count):
        return jax.ShapeDtypeStruct((count, 2, KV_HEADS, HEAD_DIM, rows), BF16)

    return pl.pallas_call(
        backward_kernel,
        grid_spec=pltpu.PrefetchScalarGridSpec(
            num_scalar_prefetch=2,
            grid=(KV_HEADS,),
            in_specs=seg_specs
            + [table, table, q_spec, k_spec, v_spec, q_spec, q_spec, stat_spec],
            out_specs=[q_spec, dkv_spec(2), dkv_spec(2), dkv_spec(4)],
            scratch_shapes=[
                pltpu.VMEM((2, reach, rows, rows), F32),
                pltpu.VMEM((GROUP, HEAD_DIM, rows), F32),
                pltpu.VMEM((GROUP, rows), F32),
                pltpu.VMEM((blocks, HEAD_DIM, rows), F32),
                pltpu.VMEM((blocks, HEAD_DIM, rows), F32),
                pltpu.VMEM((2, GROUP, rows, rows), BF16),
                pltpu.VMEM((2, GROUP, rows, rows), BF16),
            ],
        ),
        out_shape=[
            jax.ShapeDtypeStruct(q_t.shape, BF16),
            dkv_shape(2),
            dkv_shape(2),
            dkv_shape(4),
        ],
        compiler_params=pltpu.CompilerParams(vmem_limit_bytes=VMEM_LIMIT),
        cost_estimate=BESIDE,
    )(q_blocks, slots, seg_q, seg_k, valid_k, cos, sin, q_t, kv_t, kv_t, o_t, do_t, lse)


def feed_forward(x, dy_all, gu_w, down_w, first, held):
    count, rows, width = x.shape
    cut = down_w.shape[0]

    def kernel(x_ref, dy_ref, gu_ref, down_ref, *refs):
        all_ref, hidden_ref, d_gu_ref, part_ref = refs[-4:]
        x_in = x_ref[0]
        all_ref[0] = x_in
        gu = dot(x_in, gu_ref[...], ((1,), (0,)))
        d_hidden = dot(dy_ref[0], down_ref[...], ((1,), (1,)))
        gate_pre, up_pre = gu[:, :cut], gu[:, cut:]
        sig = jax.nn.sigmoid(gate_pre)
        swish = gate_pre * sig
        slope = sig * (1.0 + gate_pre * (1.0 - sig))
        hidden_ref[0] = (swish * up_pre).astype(BF16)
        d_gu_ref[0, :, :cut] = (d_hidden * up_pre * slope).astype(BF16)
        d_gu_ref[0, :, cut:] = (d_hidden * swish).astype(BF16)
        part_ref[0] = dot(d_gu_ref[0], gu_ref[...], ((1,), (1,))).astype(BF16)

    def block(size):
        return pl.BlockSpec((1, rows, size), lambda i: (first + i, 0, 0))

    def own(size):
        return pl.BlockSpec((1, rows, size), lambda i: (i, 0, 0))

    held = () if held is None else held
    return pl.pallas_call(
        kernel,
        grid=(count,),
        in_specs=[
            own(width),
            block(width),
            pl.BlockSpec(gu_w.shape, lambda i: (0, 0)),
            pl.BlockSpec(down_w.shape, lambda i: (0, 0)),
        ]
        + [pl.BlockSpec(memory_space=pl.ANY)] * len(held),
        out_specs=[block(width), block(cut), block(2 * cut), own(width)],
        out_shape=[
            jax.ShapeDtypeStruct((4, rows, width), BF16),
            jax.ShapeDtypeStruct((4, rows, cut), BF16),
            jax.ShapeDtypeStruct((4, rows, 2 * cut), BF16),
            jax.ShapeDtypeStruct((count, rows, width), BF16),
        ],
        input_output_aliases={4 + i: i for i in range(len(held))},
        compiler_params=pltpu.CompilerParams(vmem_limit_bytes=VMEM_LIMIT),
        cost_estimate=pl.CostEstimate(
            flops=10 * count * rows * width * cut,
            bytes_accessed=2 * (gu_w.size + down_w.size + count * rows * (4 * width + 3 * cut)),
            transcendentals=0,
        ),
    )(x, dy_all, gu_w, down_w, *held)


BESIDE = pl.CostEstimate(flops=0, bytes_accessed=0, transcendentals=0)


def fixed(shape):
    return pl.BlockSpec(shape, lambda *_: (0,) * len(shape))


def transposed_product(left, right, tile):
    depth, rows = left.shape
    cols = right.shape[1]

    def kernel(left_ref, right_ref, out_ref):
        out_ref[...] = dot(left_ref[...], right_ref[...], ((0,), (0,))).astype(BF16)

    return pl.pallas_call(
        kernel,
        grid=(rows // tile,),
        in_specs=[pl.BlockSpec((depth, tile), lambda i: (0, i)), fixed(right.shape)],
        out_specs=pl.BlockSpec((tile, cols), lambda i: (i, 0)),
        out_shape=jax.ShapeDtypeStruct((rows, cols), BF16),
        compiler_params=pltpu.CompilerParams(vmem_limit_bytes=VMEM_LIMIT),
        cost_estimate=BESIDE,
    )(left, right)


def product(left, right, tile):
    rows, depth = left.shape
    cols = right.shape[1]

    def kernel(left_ref, right_ref, out_ref):
        out_ref[...] = dot(left_ref[...], right_ref[...], ((1,), (0,))).astype(BF16)

    return pl.pallas_call(
        kernel,
        grid=(rows // tile,),
        in_specs=[pl.BlockSpec((tile, depth), lambda i: (i, 0)), fixed(right.shape)],
        out_specs=pl.BlockSpec((tile, cols), lambda i: (i, 0)),
        out_shape=jax.ShapeDtypeStruct((rows, cols), BF16),
        compiler_params=pltpu.CompilerParams(vmem_limit_bytes=VMEM_LIMIT),
        cost_estimate=BESIDE,
    )(left, right)


def side_product(left_t, right):
    def kernel(left_ref, right_ref, out_ref):
        total = dot(left_ref[0], right_ref[0], ((1,), (0,)))
        out_ref[...] = (total + dot(left_ref[1], right_ref[1], ((1,), (0,)))).astype(BF16)

    shape = (left_t.shape[1], right.shape[2])
    return pl.pallas_call(
        kernel,
        grid=(1,),
        in_specs=[fixed(left_t.shape), fixed(right.shape)],
        out_specs=fixed(shape),
        out_shape=jax.ShapeDtypeStruct(shape, BF16),
        compiler_params=pltpu.CompilerParams(vmem_limit_bytes=VMEM_LIMIT),
        cost_estimate=BESIDE,
    )(left_t, right)


def add_sums(ref, first, sums):
    row = lax.broadcasted_iota(jnp.int32, (8, 128), 0)
    value = jnp.zeros((8, 128), F32)
    for i, v in enumerate(sums):
        value = jnp.where(row == i, v, value)

    @pl.when(first)
    def _():
        ref[...] = jnp.zeros_like(ref)

    ref[...] += value


def side_spec(*shape):
    return pl.BlockSpec((1, *shape), lambda i: (i, 0, 0))


def out_project(tokens, attended_t, weights, gain, live):
    sides, rows, width = tokens.shape

    def kernel(x_ref, att_ref, w_ref, gain_ref, live_ref, middle_ref, second_ref, sums_ref):
        branch = dot(att_ref[0], w_ref[...], ((0,), (0,)))
        middle = x_ref[0].astype(F32) + branch
        middle_ref[0] = middle
        inverse = lax.rsqrt(jnp.mean(middle * middle, axis=-1, keepdims=True) + EPSILON)
        second_ref[0] = (middle * inverse * gain_ref[...]).astype(BF16)
        mask = live_ref[0]
        sums = [jnp.sum(mask * branch * branch), jnp.sum(mask * middle * middle)]
        add_sums(sums_ref, pl.program_id(0) == 0, sums)

    return pl.pallas_call(
        kernel,
        grid=(sides,),
        in_specs=[
            side_spec(rows, width),
            side_spec(width, rows),
            fixed(weights.shape),
            fixed((1, width)),
            side_spec(rows, 1),
        ],
        out_specs=[side_spec(rows, width), side_spec(rows, width), fixed((8, 128))],
        out_shape=[
            jax.ShapeDtypeStruct(tokens.shape, F32),
            jax.ShapeDtypeStruct(tokens.shape, BF16),
            jax.ShapeDtypeStruct((8, 128), F32),
        ],
        compiler_params=pltpu.CompilerParams(vmem_limit_bytes=VMEM_LIMIT),
        cost_estimate=BESIDE,
    )(tokens, attended_t, weights, gain, live)


def norm_back(upstream, gain, value):
    inverse = lax.rsqrt(jnp.mean(value * value, axis=-1, keepdims=True) + EPSILON)
    normed = value * inverse
    scaled = upstream * gain
    grad = inverse * (scaled - normed * jnp.mean(scaled * normed, axis=-1, keepdims=True))
    return grad, jnp.sum(upstream * normed, axis=0, keepdims=True)


def add_row(ref, first, row):
    @pl.when(first)
    def _():
        ref[...] = jnp.zeros_like(ref)

    ref[...] += row


def middle_back(d_second, middle, cotangent, gain, weights):
    sides, rows, width = middle.shape

    def kernel(d_ref, m_ref, cot_ref, gain_ref, w_ref, gm_ref, branch_ref, do_ref, gain_grad_ref):
        grad, gain_grad = norm_back(d_ref[0], gain_ref[...], m_ref[0])
        grad_middle = cot_ref[0].astype(F32) + grad
        gm_ref[0] = grad_middle
        d_branch = grad_middle.astype(BF16)
        branch_ref[0] = d_branch
        do_ref[0] = dot(d_branch, w_ref[...], ((1,), (1,))).T.astype(BF16)
        add_row(gain_grad_ref, pl.program_id(0) == 0, gain_grad)

    return pl.pallas_call(
        kernel,
        grid=(sides,),
        in_specs=[
            side_spec(rows, width),
            side_spec(rows, width),
            side_spec(rows, width),
            fixed((1, width)),
            fixed(weights.shape),
        ],
        out_specs=[
            side_spec(rows, width),
            side_spec(rows, width),
            side_spec(width, rows),
            fixed((1, width)),
        ],
        out_shape=[
            jax.ShapeDtypeStruct(middle.shape, F32),
            jax.ShapeDtypeStruct(middle.shape, BF16),
            jax.ShapeDtypeStruct((sides, width, rows), BF16),
            jax.ShapeDtypeStruct((1, width), F32),
        ],
        compiler_params=pltpu.CompilerParams(vmem_limit_bytes=VMEM_LIMIT),
        cost_estimate=BESIDE,
    )(d_second, middle, cotangent, gain, weights)


def first_back(d_q, d_kv, weights, tokens, grad_middle, gain, live):
    sides, rows, width = tokens.shape
    q_width, kv_width = d_q.shape[1], d_kv.shape[1]

    def kernel(
        dq_ref, dkv_ref, w_ref, x_ref, gm_ref, gain_ref, live_ref, out_ref, gain_grad_ref, sums_ref
    ):
        d_first = dot(dq_ref[0].T, w_ref[:, :q_width], ((1,), (1,)))
        d_first += dot(dkv_ref[0].T, w_ref[:, q_width : q_width + kv_width], ((1,), (1,)))
        grad, gain_grad = norm_back(d_first, gain_ref[...], x_ref[0].astype(F32))
        total = gm_ref[0] + grad
        out_ref[0] = total.astype(BF16)
        add_row(gain_grad_ref, pl.program_id(0) == 0, gain_grad)
        add_sums(sums_ref, pl.program_id(0) == 0, [jnp.sum(live_ref[0] * total * total)])

    return pl.pallas_call(
        kernel,
        grid=(sides,),
        in_specs=[
            side_spec(q_width, rows),
            side_spec(kv_width, rows),
            fixed(weights.shape),
            side_spec(rows, width),
            side_spec(rows, width),
            fixed((1, width)),
            side_spec(rows, 1),
        ],
        out_specs=[side_spec(rows, width), fixed((1, width)), fixed((8, 128))],
        out_shape=[
            jax.ShapeDtypeStruct(tokens.shape, BF16),
            jax.ShapeDtypeStruct((1, width), F32),
            jax.ShapeDtypeStruct((8, 128), F32),
        ],
        compiler_params=pltpu.CompilerParams(vmem_limit_bytes=VMEM_LIMIT),
        cost_estimate=BESIDE,
    )(d_q, d_kv, weights, tokens, grad_middle, gain, live)


def finish(middle, branch_ffn, live, gain_one, gain_two, early_sums, late_sums):
    sides, rows, width = middle.shape

    def kernel(m_ref, f_ref, live_ref, one_ref, two_ref, early_ref, late_ref, out_ref, small_ref):
        result = m_ref[0] + f_ref[0]
        out_ref[0] = result.astype(BF16)
        mask = live_ref[0]
        own = [jnp.sum(mask * result * result), jnp.sum(mask * f_ref[0] * f_ref[0]), jnp.sum(mask)]
        first = pl.program_id(0) == 0
        row = lax.broadcasted_iota(jnp.int32, (8, width), 0)
        value = jnp.where(row == 2, own[0], 0.0)
        value = jnp.where(row == 5, own[1], value)
        value = jnp.where(row == 7, own[2], value)

        @pl.when(first)
        def _():
            start = jnp.where(row == 0, one_ref[...], 0.0)
            start = jnp.where(row == 1, two_ref[...], start)
            start = jnp.where(row == 3, late_ref[0:1, 0:1], start)
            start = jnp.where(row == 4, early_ref[0:1, 0:1], start)
            small_ref[...] = jnp.where(row == 6, early_ref[1:2, 0:1], start)

        small_ref[...] += value

    return pl.pallas_call(
        kernel,
        grid=(sides,),
        in_specs=[
            side_spec(rows, width),
            side_spec(rows, width),
            side_spec(rows, 1),
            fixed((1, width)),
            fixed((1, width)),
            fixed((8, 128)),
            fixed((8, 128)),
        ],
        out_specs=[side_spec(rows, width), fixed((8, width))],
        out_shape=[
            jax.ShapeDtypeStruct(middle.shape, BF16),
            jax.ShapeDtypeStruct((8, width), F32),
        ],
        compiler_params=pltpu.CompilerParams(vmem_limit_bytes=VMEM_LIMIT),
        cost_estimate=BESIDE,
    )(middle, branch_ffn, live, gain_one, gain_two, early_sums, late_sums)


def norm_forward(value_rows, gain):
    inverse = lax.rsqrt(jnp.mean(value_rows * value_rows, axis=-1, keepdims=True) + EPSILON)
    normed = value_rows * inverse
    return (normed * gain, normed, inverse)


def norm_backward(upstream, gain, normed, inverse):
    scaled = upstream * gain
    grad_in = inverse * (scaled - normed * jnp.mean(scaled * normed, axis=-1, keepdims=True))
    return (grad_in, jnp.sum(upstream * normed, axis=0))


def ein(spec, left, right):
    return jnp.einsum(spec, left, right, preferred_element_type=F32)


def turn(v, cosine, sine):
    half = HEAD_DIM // 2
    a, b = v[:, :, :half], v[:, :, half:]
    return jnp.concatenate([a * cosine - b * sine, a * sine + b * cosine], axis=2)


def per_device(
    tokens, cotangent, segments, valid, norm_one, w_query, w_key, w_value, w_out,
    norm_two, w_gate, w_up, w_down,
):
    c = lax.axis_index("ctx")
    n = lax.axis_size("fsdp")
    f = lax.axis_index("fsdp")
    row_count = tokens.shape[1]
    rows = row_count // 2
    width = tokens.shape[2]
    blocks = 8
    q_width, kv_width = w_query.shape[1], w_key.shape[1]
    ff = w_gate.shape[1]
    r = w_query.shape[0]
    c_ref = c.reshape(1).astype(jnp.int32)

    q_blocks = jnp.stack([c, blocks - 1 - c]).astype(jnp.int32)
    seg_blocks = segments[0].reshape(blocks, rows)
    valid_blocks = valid[0].reshape(blocks, rows)
    seg_q = jnp.stack([take(seg_blocks, q_blocks[0], 0), take(seg_blocks, q_blocks[1], 0)])
    live = jnp.stack([take(valid_blocks, q_blocks[0], 0), take(valid_blocks, q_blocks[1], 0)])
    seg_q = seg_q[:, None, :]
    seg_k = seg_blocks[:, :, None]
    valid_k = valid_blocks[:, :, None]
    owners = c ^ jnp.arange(4, dtype=jnp.int32)
    block_of = jnp.stack([owners, blocks - 1 - owners], axis=1)
    every = jnp.arange(blocks, dtype=jnp.int32)
    side = (every >= 4).astype(jnp.int32)
    slots = (c ^ jnp.where(every < 4, every, blocks - 1 - every)) * 2 + side
    slots = slots.astype(jnp.int32)
    places = block_of[:, :, None] * rows + jnp.arange(rows, dtype=jnp.int32)
    half = HEAD_DIM // 2
    freqs = jnp.exp(jnp.arange(half, dtype=F32) * (-math.log(ROPE_BASE) / half))
    angles = places.astype(F32).reshape(8, 1, rows) * freqs[None, :, None]
    cosine, sine = jnp.cos(angles), jnp.sin(angles)

    tokens_own = tokens[0].reshape(2, rows, width)
    tokens_x, tokens_y = swap_x(tokens_own), swap_y(tokens_own)
    gains = jnp.stack([norm_one, norm_two], axis=1)
    gains = jnp.concatenate([gains, jnp.zeros((r, 126), BF16)], axis=1)
    qkv_shard = jnp.concatenate([w_query, w_key, w_value, gains], axis=1)
    c4 = qkv_shard.shape[1] // 4
    qkv_z = z_fetch(lax.dynamic_slice_in_dim(qkv_shard, c * c4, c4, 1))
    d4 = w_down.shape[0] // 4
    down_shard = lax.dynamic_slice_in_dim(w_down, c * d4, d4, 0)
    out_down_shard = after(jnp.concatenate([w_out, down_shard]), qkv_z)
    out_down = lax.all_gather(out_down_shard, "fsdp", axis=0)
    qkv_z, tokens_x, tokens_y = sync(qkv_z, tokens_x, tokens_y)
    qkv_x, qkv_y = swap_x(qkv_z), swap_y(qkv_z)
    gu_shard = after(pick_columns(c_ref, w_gate, w_up, n), qkv_z)
    gu_w = lax.all_gather(gu_shard, "fsdp", axis=0, tiled=True)
    cut = ff // 4
    qkv_x, qkv_y, tokens_x, tokens_y = sync(qkv_x, qkv_y, tokens_x, tokens_y)
    zh = qkv_z.shape[0] // 2
    qkv_d = jnp.concatenate([swap_y(qkv_x[:zh]), swap_x(qkv_y[zh:])])
    tokens_d = jnp.concatenate([swap_y(tokens_x[:1]), swap_x(tokens_y[1:])])
    qkv_mine = jnp.stack([qkv_z, qkv_x, qkv_y, qkv_d])
    qkv_other = core_swap(qkv_mine)
    tokens_all = jnp.stack([tokens_own, tokens_x, tokens_y, tokens_d])
    dy_own = cotangent[0].reshape(2, rows, width)
    dy_pieces = ctx_fetch_direct(after(dy_own, qkv_mine, tokens_d))

    first_all, q_t, kv_all, qkv_w, gain_rows = project(
        c, f, tokens_all.reshape(8, rows, width), qkv_mine, qkv_other, cosine, sine, q_width
    )
    gain_one, gain_two = gain_rows[0:1], gain_rows[1:2]
    first_all = first_all.reshape(4, 2, rows, width)
    o_t, lse = attention_forward(q_blocks, slots, seg_q, seg_k, valid_k, q_t, kv_all)
    o_t, out_down, dy_pieces, gu_w = sync(o_t, out_down, dy_pieces, gu_w)
    out_w = out_down[:, :r].reshape(n * r, width)
    down_w = out_down[:, r:].reshape(cut, width)
    (dy_all,) = sync(jnp.stack(dy_pieces).reshape(4, row_count, width))
    attended_t = o_t.reshape(2, width, rows)
    live_rows = live.reshape(2, rows, 1).astype(F32)
    middle, x_own, early_sums = out_project(tokens_own, attended_t, out_w, gain_two, live_rows)

    x_x, x_y = swap_x(x_own), swap_y(x_own)
    held = feed_forward(x_own.reshape(1, row_count, width), dy_all, gu_w, down_w, 0, None)
    x_x, x_y, *held = sync(x_x, x_y, *held)
    parts_0 = held.pop()
    x_d = jnp.concatenate([swap_y(x_x[:1]), swap_x(x_y[1:])])
    x_xy = jnp.stack([x_x, x_y]).reshape(2, row_count, width)
    held = feed_forward(x_xy, dy_all, gu_w, down_w, 1, held)
    x_d, *held = sync(x_d, *held)
    parts_1 = held.pop()
    x_d = x_d.reshape(1, row_count, width)
    *held, parts_2 = feed_forward(x_d, dy_all, gu_w, down_w, 3, held)
    parts = [v.reshape(2, rows, width) for v in (parts_0[0], parts_1[0], parts_1[1], parts_2[0])]
    got = scatter_first(parts)
    x_all, hidden, d_gu = [v.reshape(4 * row_count, -1) for v in held]
    dy_all = dy_all.reshape(4 * row_count, width)
    grad_gu = transposed_product(x_all, d_gu, 256)
    ffn_parts = product(after(hidden, grad_gu), down_w, row_count)
    got_low, got_high, grad_gu, ffn_parts = sync(*got, grad_gu, ffn_parts)
    d_second = scatter_last(*scatter_pass(parts, (got_low, got_high)))
    grad_d = transposed_product(after(hidden, ffn_parts), dy_all, cut)
    d_second, grad_d = sync(d_second, grad_d)
    ffn_parts = ffn_parts.reshape(4, 2, rows, width)
    ffn_parts = [ffn_parts[i] for i in range(4)]
    own_gu = lax.psum_scatter(grad_gu, "fsdp", scatter_dimension=0, tiled=True)
    own_down = lax.psum_scatter(grad_d, "fsdp", scatter_dimension=0, tiled=True)

    k = f % 2
    nz = n // 2
    r4 = r // 4
    grad_middle, d_branch, do_t, grad_gain_two = middle_back(
        d_second, middle, dy_own, gain_two, out_w
    )
    do_t = do_t.reshape(2, HEADS, HEAD_DIM, rows)
    whole_out = side_product(attended_t, d_branch)
    do_t, ffn_parts, whole_out = sync(do_t, ffn_parts, whole_out)
    ffn_got = scatter_first(ffn_parts)
    d_q, dkv_low, dkv_high, dkv_keep = attention_backward(
        q_blocks, slots, seg_q, seg_k, valid_k, cosine[:2], sine[:2], q_t, kv_all, o_t, do_t, lse
    )
    d_q, dkv_low, dkv_high, dkv_keep, ffn_got = sync(d_q, dkv_low, dkv_high, dkv_keep, ffn_got)
    dkv_got = swap_x(dkv_low), swap_y(dkv_high)
    own_out = lax.psum_scatter(
        after(whole_out, dkv_low, own_gu), "fsdp", scatter_dimension=0, tiled=True
    )
    q4, kv4 = q_width // 4, kv_width // 2

    def quarter(v, size, i):
        return lax.dynamic_slice_in_dim(v, (c ^ i) * size, size, 1)

    d_q = d_q.reshape(2, q_width, rows)
    dq_parts = [quarter(d_q, q4, i) for i in range(4)]
    ffn_sums = scatter_pass(ffn_parts, ffn_got)
    dkv_got, dq_parts, ffn_sums = sync(dkv_got, dq_parts, ffn_sums)
    kept = dkv_keep.astype(F32)
    low_sums, high_sums = kept[:2] + dkv_got[0].astype(F32), kept[2:] + dkv_got[1].astype(F32)
    from_y, from_x = swap_y(low_sums[1].astype(BF16)), swap_x(high_sums[1].astype(BF16))
    dkv_own = jnp.stack([low_sums[0] + from_y.astype(F32), high_sums[0] + from_x.astype(F32)])
    dkv_own = dkv_own.reshape(2, 2 * KV_HEADS, HEAD_DIM, rows)
    dq_got = exchange_first(dq_parts)
    d_k = turn(dkv_own[:, :KV_HEADS], cosine[:2, None], -sine[:2, None]).astype(BF16)
    d_kv = jnp.concatenate([d_k, dkv_own[:, KV_HEADS:].astype(BF16)], axis=1)
    d_kv = d_kv.reshape(2, 2 * kv_width, rows)
    dkv_parts = [quarter(d_kv, kv4, i) for i in range(4)]
    dkv_got = exchange_first(dkv_parts)
    dq_got, dkv_got = sync(dq_got, dkv_got)
    dq_pieces = [dq_parts[0], *dq_got, *exchange_second(*dq_got)]
    dkv_pieces = [dkv_parts[0], *dkv_got, *exchange_second(*dkv_got)]
    dq_pieces, dkv_pieces, own_gu, own_out = sync(dq_pieces, dkv_pieces, own_gu, own_out)
    gu_x, gu_y = swap_x(own_gu), swap_y(own_gu)
    own_out = own_out.reshape(4, r4, width)
    out_parts = [take(own_out, c ^ i, 0) for i in range(4)]
    out_got = scatter_first(out_parts)
    grad_qkv = project_grad(first_all.reshape(8, rows, width), dq_pieces, dkv_pieces)
    grad_qkv = grad_qkv.reshape(nz, 2, r, q4 + kv4)
    got_half = core_swap(take(grad_qkv, k ^ 1, 1))
    pair_qkv = (take(grad_qkv, k, 1).astype(F32) + got_half.astype(F32)).astype(BF16)
    pair_qkv, d_q, d_kv, ffn_sums, gu_x, gu_y, out_got = sync(
        pair_qkv, d_q, d_kv, ffn_sums, gu_x, gu_y, out_got
    )
    own_qkv = z_scatter(pair_qkv).astype(BF16)

    branch_ffn = scatter_last(*ffn_sums)
    grad_tokens, grad_gain_one, late_sums = first_back(
        d_q, d_kv, qkv_w, tokens_own, grad_middle, gain_one, live_rows
    )
    out_sums = scatter_pass(out_parts, out_got)
    own_qkv, branch_ffn, out_sums, grad_tokens, grad_gain_one, late_sums = sync(
        own_qkv, branch_ffn, out_sums, grad_tokens, grad_gain_one, late_sums
    )

    qkv_pieces = ctx_fetch_direct(own_qkv)
    own_out = scatter_last(*out_sums).astype(BF16)
    result, small = finish(
        middle, branch_ffn, live_rows, grad_gain_one, grad_gain_two, early_sums, late_sums
    )
    small = small + core_swap(small)
    own_out, qkv_pieces, small, gu_x, gu_y = sync(own_out, qkv_pieces, small, gu_x, gu_y)
    hr = gu_x.shape[0] // 2
    gu_d = jnp.concatenate([swap_y(gu_x[:hr]), swap_x(gu_y[hr:])])
    small = z_sum(small)
    grad_q, grad_k, grad_v = join_columns(c_ref, qkv_pieces, q4, kv4)
    gu_d, small, own_down, own_out = sync(gu_d, small, own_down, own_out)
    small = sum(ctx_fetch_direct(small))
    out_pieces = ctx_fetch_direct(own_out)
    down_pieces = ctx_fetch_direct(own_down)
    grad_gate_w, grad_up_w = unpick_columns(c_ref, [own_gu, gu_x, gu_y, gu_d], n)
    grad_down_w = in_order(down_pieces, 0).reshape(4 * d4, width).astype(F32)
    grad_out_w = in_order(out_pieces, 0).reshape(r, width).astype(F32)
    gain_sums = lax.dynamic_slice_in_dim(small[:2], f * r, r, 1)
    squares = small[2:8, 0]
    spreads = jnp.sqrt(squares[:5] / (squares[5] * width))
    return (
        result.reshape(1, row_count, width),
        grad_tokens.reshape(1, row_count, width),
        gain_sums[0],
        grad_q,
        grad_k,
        grad_v,
        grad_out_w,
        gain_sums[1],
        grad_gate_w,
        grad_up_w,
        grad_down_w,
        spreads,
    )


def solution(mesh):
    rows, shard, vector = P("fsdp", "ctx", None), P("fsdp", None), P("fsdp")
    return jax.shard_map(
        per_device,
        mesh=mesh,
        in_specs=(
            rows, rows, shard, shard, vector, shard, shard, shard, shard, vector,
            shard, shard, shard,
        ),
        out_specs=(
            rows, rows, vector, shard, shard, shard, shard, vector, shard, shard, shard, P(),
        ),
        check_vma=False,
    )
```

```python
import functools
import math

import jax
import jax.numpy as jnp
from jax import lax
from jax.experimental import pallas as pl
from jax.experimental.pallas import tpu as pltpu
from jax.sharding import PartitionSpec as P

HEADS = 20
KV_HEADS = 5
HEAD_DIM = 64
GROUP = HEADS // KV_HEADS
WINDOW = 1024
EPSILON = 1e-05
MASKED = -1e30
ROPE_BASE = 10000.0
VMEM_LIMIT = 60 * 2**20
BF16 = jnp.bfloat16
F32 = jnp.float32


def core_swap(v):
    n = lax.axis_size("fsdp")
    return lax.ppermute(v, "fsdp", [(i, i ^ 1) for i in range(n)])


def swap_x(v):
    return lax.ppermute(v, "ctx", [(i, i ^ 1) for i in range(4)])


def swap_y(v):
    return lax.ppermute(v, "ctx", [(i, i ^ 2) for i in range(4)])


def put(buffer, piece, index, axis):
    return lax.dynamic_update_slice_in_dim(
        buffer, jnp.expand_dims(piece, axis), index, axis
    )


def take(v, index, axis):
    return lax.dynamic_index_in_dim(v, index, axis, keepdims=False)


def place(pieces, axis):
    first = pieces[0][1]
    shape = first.shape[:axis] + (len(pieces),) + first.shape[axis:]
    buffer = jnp.zeros(shape, first.dtype)
    for index, piece in pieces:
        buffer = put(buffer, piece, index, axis)
    return buffer


def z_fetch(piece):
    n = lax.axis_size("fsdp")
    nz = n // 2
    if nz != 4:
        groups = [list(range(0, n, 2)), list(range(1, n, 2))]
        every = lax.all_gather(piece, "fsdp", axis=0, axis_index_groups=groups)
        z = lax.axis_index("fsdp") // 2
        return jnp.take(every, (z - jnp.arange(nz)) % nz, axis=0)
    pieces = [piece]
    for d in (1, 2, 3):
        pieces.append(lax.ppermute(piece, "fsdp", [(i, (i + 2 * d) % n) for i in range(n)]))
    return jnp.stack(pieces)


def z_scatter(pieces):
    n = lax.axis_size("fsdp")
    nz = n // 2
    if nz != 4:
        groups = [list(range(0, n, 2)), list(range(1, n, 2))]
        return lax.psum_scatter(
            pieces, "fsdp", scatter_dimension=0, axis_index_groups=groups
        ).astype(F32)
    z = lax.axis_index("fsdp") // 2
    total = take(pieces, z, 0).astype(F32)
    for d in (1, 2, 3):
        sent = take(pieces, (z + d) % nz, 0)
        got = lax.ppermute(sent, "fsdp", [(i, (i + 2 * d) % n) for i in range(n)])
        total = total + got.astype(F32)
    return total


def sync(*values):
    return lax.optimization_barrier(values)


def ctx_fetch(piece):
    half = piece.shape[0] // 2
    from_x = swap_x(piece)
    from_y = swap_y(piece)
    from_d = jnp.concatenate([swap_y(from_x[:half]), swap_x(from_y[half:])], axis=0)
    return [piece, from_x, from_y, from_d]


def after(v, *earlier):
    return lax.optimization_barrier((v, earlier))[0]


def ctx_fetch_direct(piece):
    diagonal = lax.ppermute(piece, "ctx", [(i, i ^ 3) for i in range(4)])
    return [piece, swap_x(piece), swap_y(piece), diagonal]


def in_order(pieces, axis):
    c = lax.axis_index("ctx")
    return place([(c ^ i, v) for i, v in enumerate(pieces)], axis)


def scatter_first(parts):
    half = parts[0].shape[0] // 2
    low_got = swap_x(jnp.concatenate([parts[1][:half], parts[3][:half]]))
    high_got = swap_y(jnp.concatenate([parts[2][half:], parts[3][half:]]))
    return low_got, high_got


def scatter_pass(parts, got):
    half = parts[0].shape[0] // 2
    rest = parts[0].shape[0] - half
    low_got, high_got = got[0].astype(F32), got[1].astype(F32)
    low_pass = (parts[2][:half].astype(F32) + low_got[half:]).astype(BF16)
    high_pass = (parts[1][half:].astype(F32) + high_got[rest:]).astype(BF16)
    low_own = parts[0][:half].astype(F32) + low_got[:half]
    high_own = parts[0][half:].astype(F32) + high_got[:rest]
    return low_own, high_own, low_pass, high_pass


def scatter_last(low_own, high_own, low_pass, high_pass):
    from_y, from_x = swap_y(low_pass), swap_x(high_pass)
    return jnp.concatenate([low_own + from_y.astype(F32), high_own + from_x.astype(F32)])


def exchange_first(parts):
    to_x = jnp.concatenate([parts[1], parts[3][:1]], axis=0)
    to_y = jnp.concatenate([parts[2], parts[3][1:]], axis=0)
    return swap_x(to_x), swap_y(to_y)


def z_sum(v):
    n = lax.axis_size("fsdp")
    if n == 8:
        return v + sum(
            lax.ppermute(v, "fsdp", [(i, (i + 2 * d) % n) for i in range(n)]) for d in (1, 2, 3)
        )
    bit = 2
    while bit < n:
        v = v + lax.ppermute(v, "fsdp", [(i, i ^ bit) for i in range(n)])
        bit *= 2
    return v


def pick_columns(c, gate, up, count):
    r, ff = gate.shape
    group = ff // count
    strip = group // 4

    def kernel(c_ref, gate_ref, up_ref, out_ref):
        for own in range(4):

            @pl.when(c_ref[0] == own)
            def _():
                for j in range(count):
                    at = j * group + own * strip
                    out_ref[:, j * strip : (j + 1) * strip] = gate_ref[:, at : at + strip]
                    to = ff // 4 + j * strip
                    out_ref[:, to : to + strip] = up_ref[:, at : at + strip]

    whole = pl.BlockSpec((r, ff), lambda i, s: (0, 0))
    return pl.pallas_call(
        kernel,
        grid_spec=pltpu.PrefetchScalarGridSpec(
            num_scalar_prefetch=1,
            grid=(1,),
            in_specs=[whole, whole],
            out_specs=pl.BlockSpec((r, ff // 2), lambda i, s: (0, 0)),
        ),
        out_shape=jax.ShapeDtypeStruct((r, ff // 2), BF16),
        cost_estimate=pl.CostEstimate(flops=0, bytes_accessed=6 * r * ff, transcendentals=0),
    )(c, gate, up)


def unpick_columns(c, pieces, count):
    r, half = pieces[0].shape
    ff = 2 * half
    group = ff // count
    strip = group // 4

    def kernel(c_ref, *refs):
        gate_ref, up_ref = refs[4:]
        for own in range(4):

            @pl.when(c_ref[0] == own)
            def _():
                for step in range(4):
                    for j in range(count):
                        at = j * group + (own ^ step) * strip
                        piece = refs[step]
                        gate_ref[:, at : at + strip] = piece[
                            :, j * strip : (j + 1) * strip
                        ].astype(F32)
                        frm = ff // 4 + j * strip
                        up_ref[:, at : at + strip] = piece[:, frm : frm + strip].astype(F32)

    whole = pl.BlockSpec((r, ff), lambda i, s: (0, 0))
    return pl.pallas_call(
        kernel,
        grid_spec=pltpu.PrefetchScalarGridSpec(
            num_scalar_prefetch=1,
            grid=(1,),
            in_specs=[pl.BlockSpec((r, half), lambda i, s: (0, 0))] * 4,
            out_specs=[whole, whole],
        ),
        out_shape=[jax.ShapeDtypeStruct((r, ff), F32)] * 2,
        compiler_params=pltpu.CompilerParams(vmem_limit_bytes=VMEM_LIMIT),
        cost_estimate=pl.CostEstimate(flops=0, bytes_accessed=12 * r * ff, transcendentals=0),
    )(c, *pieces)


def join_columns(c, pieces, q4, kv4):
    r = pieces[0].shape[0]

    def kernel(c_ref, *refs):
        q_ref, k_ref, v_ref = refs[4:]
        for own in range(4):

            @pl.when(c_ref[0] == own)
            def _():
                for step in range(4):
                    to = own ^ step
                    piece = refs[step][...].astype(F32)
                    q_ref[:, to * q4 : (to + 1) * q4] = piece[:, :q4]
                    target = k_ref if to < 2 else v_ref
                    at = (to % 2) * kv4
                    target[:, at : at + kv4] = piece[:, q4:]

    def whole(cols):
        return pl.BlockSpec((r, cols), lambda i, s: (0, 0))

    return pl.pallas_call(
        kernel,
        grid_spec=pltpu.PrefetchScalarGridSpec(
            num_scalar_prefetch=1,
            grid=(1,),
            in_specs=[whole(q4 + kv4)] * 4,
            out_specs=[whole(4 * q4), whole(2 * kv4), whole(2 * kv4)],
        ),
        out_shape=[
            jax.ShapeDtypeStruct((r, cols), F32) for cols in (4 * q4, 2 * kv4, 2 * kv4)
        ],
        cost_estimate=pl.CostEstimate(
            flops=0, bytes_accessed=24 * r * (q4 + kv4), transcendentals=0
        ),
    )(c, *pieces)


def pair_bias(q_block, k_block, rows, seg_q, seg_k, valid_k):
    key_at = k_block * rows + lax.broadcasted_iota(jnp.int32, (rows, rows), 0)
    query_at = q_block * rows + lax.broadcasted_iota(jnp.int32, (rows, rows), 1)
    distance = query_at - key_at
    allowed = (
        (seg_q == seg_k)
        & (distance >= 0)
        & (distance < WINDOW)
        & ((valid_k == 1.0) | (distance == 0))
    )
    return jnp.where(allowed, 0.0, MASKED).astype(F32)


def first_block(q_block, rows):
    reach = (WINDOW + rows - 2) // rows
    return jnp.maximum(q_block - reach, 0)


def dot(a, b, dims):
    return lax.dot_general(a, b, (dims, ((), ())), preferred_element_type=F32)


def column(row):
    size = row.shape[1]
    return jnp.broadcast_to(row, (size, size)).T


def fill_bias(blocks_ref, seg_q_ref, seg_k_ref, valid_k_ref, bias_ref, rows):
    for side in range(2):
        b = blocks_ref[side]
        lo = first_block(b, rows)

        def body(kb, _):
            bias_ref[side, kb - lo] = pair_bias(
                b, kb, rows, seg_q_ref[side], column(seg_k_ref[kb]), column(valid_k_ref[kb])
            )
            return 0

        lax.fori_loop(lo, b + 1, body, 0)


def forward_kernel(
    blocks_ref, slots_ref, seg_q_ref, seg_k_ref, valid_k_ref, q_ref, k_ref, v_ref,
    o_ref, lse_ref, bias_ref, scores_ref, acc_ref,
):
    rows = q_ref.shape[-1]

    @pl.when(pl.program_id(0) == 0)
    def _():
        fill_bias(blocks_ref, seg_q_ref, seg_k_ref, valid_k_ref, bias_ref, rows)

    for side in range(2):
        b = blocks_ref[side]
        lo = first_block(b, rows)

        def score(kb, peaks):
            keys = k_ref[slots_ref[kb], 0].T
            bias = bias_ref[side, kb - lo]
            higher = []
            for h in range(GROUP):
                s = dot(keys, q_ref[side, h], ((1,), (0,))) + bias
                scores_ref[kb - lo, h] = s
                higher.append(jnp.maximum(peaks[h], jnp.max(s, axis=0, keepdims=True)))
            return tuple(higher)

        peaks = lax.fori_loop(
            lo, b + 1, score, (jnp.full((1, rows), -jnp.inf, F32),) * GROUP
        )
        acc_ref[...] = jnp.zeros_like(acc_ref)

        def mix(kb, totals):
            values_t = v_ref[slots_ref[kb], 0]
            more = []
            for h in range(GROUP):
                p = jnp.exp(scores_ref[kb - lo, h] - peaks[h])
                more.append(totals[h] + jnp.sum(p, axis=0, keepdims=True))
                acc_ref[h] += dot(values_t, p.astype(BF16), ((1,), (0,)))
            return tuple(more)

        totals = lax.fori_loop(lo, b + 1, mix, (jnp.zeros((1, rows), F32),) * GROUP)
        for h in range(GROUP):
            o_ref[side, h] = (acc_ref[h] / totals[h]).astype(BF16)
            lse_ref[side, 0, h : h + 1] = peaks[h] + jnp.log(totals[h])


def backward_kernel(
    blocks_ref, slots_ref, seg_q_ref, seg_k_ref, valid_k_ref, cos_ref, sin_ref, q_ref, k_ref, v_ref,
    o_ref, do_ref, lse_ref,
    dq_ref, low_ref, high_ref, keep_ref,
    bias_ref, acc_ref, center_ref, dk_ref, dv_ref, p_ref, ds_ref,
):
    rows = q_ref.shape[-1]
    half = HEAD_DIM // 2

    @pl.when(pl.program_id(0) == 0)
    def _():
        fill_bias(blocks_ref, seg_q_ref, seg_k_ref, valid_k_ref, bias_ref, rows)

    dk_ref[...] = jnp.zeros_like(dk_ref)
    dv_ref[...] = jnp.zeros_like(dv_ref)
    for side in range(2):
        b = blocks_ref[side]
        lo = first_block(b, rows)
        acc_ref[...] = jnp.zeros_like(acc_ref)
        for h in range(GROUP):
            center_ref[h : h + 1] = jnp.sum(
                o_ref[side, h].astype(F32) * do_ref[side, h].astype(F32), axis=0, keepdims=True
            )

        def soft(kb, at):
            slot = slots_ref[kb]
            keys = k_ref[slot, 0].T
            values = v_ref[slot, 0].T
            bias = bias_ref[side, kb - lo]
            for h in range(GROUP):
                s = dot(keys, q_ref[side, h], ((1,), (0,))) + bias
                p = jnp.exp(s - lse_ref[side, 0, h : h + 1])
                dp = dot(values, do_ref[side, h], ((1,), (0,)))
                p_ref[at, h] = p.astype(BF16)
                ds_ref[at, h] = (p * (dp - center_ref[h : h + 1])).astype(BF16)

        def products(kb, at):
            slot = slots_ref[kb]
            dv = dot(do_ref[side, 0], p_ref[at, 0], ((1,), (1,)))
            dk = dot(q_ref[side, 0], ds_ref[at, 0], ((1,), (1,)))
            for h in range(1, GROUP):
                dv += dot(do_ref[side, h], p_ref[at, h], ((1,), (1,)))
                dk += dot(q_ref[side, h], ds_ref[at, h], ((1,), (1,)))
            dv_ref[slot] += dv
            dk_ref[slot] += dk
            for h in range(GROUP):
                acc_ref[h] += dot(k_ref[slot, 0], ds_ref[at, h], ((1,), (0,)))

        soft(lo, 0)

        def body(kb, _):
            products(kb - 1, (kb - 1 - lo) % 2)
            soft(kb, (kb - lo) % 2)
            return 0

        lax.fori_loop(lo + 1, b + 1, body, 0)
        products(b, (b - lo) % 2)
        cos, sin = cos_ref[side], sin_ref[side]
        for h in range(GROUP):
            a, b2 = acc_ref[h, :half] * 0.125, acc_ref[h, half:] * 0.125
            turned = jnp.concatenate([a * cos + b2 * sin, b2 * cos - a * sin], axis=0)
            dq_ref[side, h] = turned.astype(BF16)
    for target, slots in ((low_ref, (2, 6)), (high_ref, (5, 7)), (keep_ref, (0, 4, 1, 3))):
        for i, slot in enumerate(slots):
            target[i, 0, 0] = dk_ref[slot].astype(BF16)
            target[i, 1, 0] = dv_ref[slot].astype(BF16)


def project(c, f, tokens, mine, other, cosine, sine, q_width):
    _, rows, width = tokens[0].shape
    blocks = 8
    _, nz, r, cols = mine[0].shape
    half = HEAD_DIM // 2
    kv_heads = 2 * KV_HEADS
    gains_at = q_width + kv_heads * HEAD_DIM

    def turned(flat_t, at, cos, sin):
        a, b = flat_t[at : at + half], flat_t[at + half : at + HEAD_DIM]
        return jnp.concatenate([a * cos - b * sin, a * sin + b * cos], axis=0)

    def kernel(at_ref, *refs):
        token_refs, mine_refs, other_refs = refs[:5], refs[5:7], refs[7:9]
        cos_ref, sin_ref, first_ref, q_ref, kv_ref, w_ref, gain_ref, x_ref = refs[9:]

        @pl.when(pl.program_id(0) == 0)
        def _():
            for core in range(2):
                for q in range(4):
                    step = q ^ at_ref[0]

                    def fill(index, which, core=core, q=q):
                        for z in range(nz):
                            z_step = (at_ref[1] // 2 - z + nz) % nz
                            for kk in range(2):
                                source = mine_refs if kk == core else other_refs
                                at = (2 * z + kk) * r
                                w_ref[at : at + r, q * cols : (q + 1) * cols] = source[which][
                                    index, z_step
                                ]

                    @pl.when((at_ref[1] % 2 == core) & (step < 3))
                    def _(step=step, fill=fill):
                        fill(step, 0)

                    @pl.when((at_ref[1] % 2 == core) & (step == 3))
                    def _(fill=fill):
                        fill(0, 1)

            gain_ref[...] = w_ref[:, gains_at:].astype(F32).T[:8]

        for i in range(3):

            @pl.when(pl.program_id(0) == i)
            def _(i=i):
                x_ref[...] = token_refs[i][...].astype(F32)

        @pl.when(pl.program_id(0) == 3)
        def _():
            x_ref[0] = token_refs[3][0].astype(F32)
            x_ref[1] = token_refs[4][0].astype(F32)

        x = x_ref[...]
        inverse = lax.rsqrt(jnp.mean(x * x, axis=-1, keepdims=True) + EPSILON)
        scaled = x * inverse * gain_ref[0:1][None]
        first_ref[...] = scaled.astype(BF16)
        first = scaled.reshape(2 * rows, width).astype(BF16)
        both = dot(first, w_ref[:, q_width:gains_at], ((1,), (0,)))
        for i in range(2):
            cos, sin = cos_ref[i], sin_ref[i]
            kv = both[i * rows : (i + 1) * rows].T
            for h in range(kv_heads):
                at = h * HEAD_DIM
                if h < KV_HEADS:
                    kv_ref[i, h] = turned(kv, at, cos, sin).astype(BF16)
                else:
                    kv_ref[i, h] = kv[at : at + HEAD_DIM].astype(BF16)

        @pl.when(pl.program_id(0) == 0)
        def _():
            both = dot(first, w_ref[:, :q_width], ((1,), (0,)))
            for i in range(2):
                cos, sin = cos_ref[i], sin_ref[i]
                q = both[i * rows : (i + 1) * rows].T
                for h in range(HEADS):
                    turned_q = turned(q, h * HEAD_DIM, cos, sin).astype(BF16)
                    q_ref[i, h] = (turned_q.astype(F32) * 0.125).astype(BF16)

    table = pl.BlockSpec((2, half, rows), lambda i, s: (i, 0, 0))
    operands = [*tokens, *mine, *other]
    return pl.pallas_call(
        kernel,
        grid_spec=pltpu.PrefetchScalarGridSpec(
            num_scalar_prefetch=1,
            grid=(blocks // 2,),
            in_specs=[fixed(v.shape) for v in operands] + [table, table],
            out_specs=[
                pl.BlockSpec((2, rows, width), lambda i, s: (i, 0, 0)),
                fixed((2, HEADS, HEAD_DIM, rows)),
                pl.BlockSpec((2, kv_heads, HEAD_DIM, rows), lambda i, s: (i, 0, 0, 0)),
                fixed((2 * nz * r, 4 * cols)),
                fixed((8, width)),
            ],
            scratch_shapes=[pltpu.VMEM((2, rows, width), F32)],
        ),
        out_shape=[
            jax.ShapeDtypeStruct((blocks, rows, width), BF16),
            jax.ShapeDtypeStruct((2, HEADS, HEAD_DIM, rows), BF16),
            jax.ShapeDtypeStruct((blocks, kv_heads, HEAD_DIM, rows), BF16),
            jax.ShapeDtypeStruct((2 * nz * r, 4 * cols), BF16),
            jax.ShapeDtypeStruct((8, width), F32),
        ],
        compiler_params=pltpu.CompilerParams(vmem_limit_bytes=VMEM_LIMIT),
        cost_estimate=pl.CostEstimate(
            flops=8_000_000_000, bytes_accessed=25_000_000, transcendentals=0
        ),
    )(jnp.stack([c, f]).astype(jnp.int32), *operands, cosine, sine)


def project_grad(first_all, dq_pieces, dkv_pieces, diagonal):
    _, rows, width = first_all.shape
    q4, kv4 = dq_pieces[0].shape[1], dkv_pieces[0].shape[1]

    def kernel(first_ref, *refs):
        out_ref = refs[-1]
        total = None
        for i in range(8):
            if i < 6:
                turned = jnp.concatenate([refs[i // 2][i % 2], refs[3 + i // 2][i % 2]], axis=0)
            else:
                turned = refs[i][0]
            term = dot(turned, first_ref[i], ((1,), (0,)))
            total = term if total is None else total + term
        out_ref[...] = total.T.astype(BF16)

    operands = [first_all, *dq_pieces, *dkv_pieces, *diagonal]
    return pl.pallas_call(
        kernel,
        grid=(1,),
        in_specs=[fixed(v.shape) for v in operands],
        out_specs=fixed((width, q4 + kv4)),
        out_shape=jax.ShapeDtypeStruct((width, q4 + kv4), BF16),
        compiler_params=pltpu.CompilerParams(vmem_limit_bytes=VMEM_LIMIT),
        cost_estimate=BESIDE,
    )(*operands)


def kernel_specs(blocks, rows):
    q_spec = pl.BlockSpec((2, GROUP, HEAD_DIM, rows), lambda g, *_: (0, g, 0, 0))
    k_spec = pl.BlockSpec((blocks, 1, HEAD_DIM, rows), lambda g, *_: (0, g, 0, 0))
    v_spec = pl.BlockSpec((blocks, 1, HEAD_DIM, rows), lambda g, *_: (0, KV_HEADS + g, 0, 0))
    stat_spec = pl.BlockSpec((2, 1, GROUP, rows), lambda g, *_: (0, g, 0, 0))
    seg_specs = [
        pl.BlockSpec((2, 1, rows), lambda g, *_: (0, 0, 0)),
        pl.BlockSpec((blocks, 1, rows), lambda g, *_: (0, 0, 0)),
        pl.BlockSpec((blocks, 1, rows), lambda g, *_: (0, 0, 0)),
    ]
    return q_spec, k_spec, v_spec, stat_spec, seg_specs


def attention_forward(q_blocks, slots, seg_q, seg_k, valid_k, q_t, kv_t):
    blocks, _, _, rows = kv_t.shape
    q_spec, k_spec, v_spec, stat_spec, seg_specs = kernel_specs(blocks, rows)
    reach = (WINDOW + rows - 2) // rows + 1
    return pl.pallas_call(
        forward_kernel,
        grid_spec=pltpu.PrefetchScalarGridSpec(
            num_scalar_prefetch=2,
            grid=(KV_HEADS,),
            in_specs=seg_specs + [q_spec, k_spec, v_spec],
            out_specs=[q_spec, stat_spec],
            scratch_shapes=[
                pltpu.VMEM((2, reach, rows, rows), F32),
                pltpu.VMEM((reach, GROUP, rows, rows), F32),
                pltpu.VMEM((GROUP, HEAD_DIM, rows), F32),
            ],
        ),
        out_shape=[
            jax.ShapeDtypeStruct(q_t.shape, BF16),
            jax.ShapeDtypeStruct((2, KV_HEADS, GROUP, rows), F32),
        ],
        compiler_params=pltpu.CompilerParams(vmem_limit_bytes=VMEM_LIMIT),
        cost_estimate=pl.CostEstimate(
            flops=20_000_000_000, bytes_accessed=6_000_000, transcendentals=0
        ),
    )(q_blocks, slots, seg_q, seg_k, valid_k, q_t, kv_t, kv_t)


def attention_backward(q_blocks, slots, seg_q, seg_k, valid_k, cos, sin, q_t, kv_t, o_t, do_t, lse):
    blocks, _, _, rows = kv_t.shape
    q_spec, k_spec, v_spec, stat_spec, seg_specs = kernel_specs(blocks, rows)
    reach = (WINDOW + rows - 2) // rows + 1
    table = pl.BlockSpec((2, HEAD_DIM // 2, rows), lambda g, *_: (0, 0, 0))

    def dkv_spec(count):
        return pl.BlockSpec((count, 2, 1, HEAD_DIM, rows), lambda g, *_: (0, 0, g, 0, 0))

    def dkv_shape(count):
        return jax.ShapeDtypeStruct((count, 2, KV_HEADS, HEAD_DIM, rows), BF16)

    return pl.pallas_call(
        backward_kernel,
        grid_spec=pltpu.PrefetchScalarGridSpec(
            num_scalar_prefetch=2,
            grid=(KV_HEADS,),
            in_specs=seg_specs
            + [table, table, q_spec, k_spec, v_spec, q_spec, q_spec, stat_spec],
            out_specs=[q_spec, dkv_spec(2), dkv_spec(2), dkv_spec(4)],
            scratch_shapes=[
                pltpu.VMEM((2, reach, rows, rows), F32),
                pltpu.VMEM((GROUP, HEAD_DIM, rows), F32),
                pltpu.VMEM((GROUP, rows), F32),
                pltpu.VMEM((blocks, HEAD_DIM, rows), F32),
                pltpu.VMEM((blocks, HEAD_DIM, rows), F32),
                pltpu.VMEM((2, GROUP, rows, rows), BF16),
                pltpu.VMEM((2, GROUP, rows, rows), BF16),
            ],
        ),
        out_shape=[
            jax.ShapeDtypeStruct(q_t.shape, BF16),
            dkv_shape(2),
            dkv_shape(2),
            dkv_shape(4),
        ],
        compiler_params=pltpu.CompilerParams(vmem_limit_bytes=VMEM_LIMIT),
        cost_estimate=BESIDE,
    )(q_blocks, slots, seg_q, seg_k, valid_k, cos, sin, q_t, kv_t, kv_t, o_t, do_t, lse)


def feed_forward(x, dy_all, gu_w, down_w, first, held):
    count, rows, width = x.shape
    cut = down_w.shape[0]

    def kernel(x_ref, dy_ref, gu_ref, down_ref, *refs):
        all_ref, hidden_ref, d_gu_ref, part_ref = refs[-4:]
        x_in = x_ref[0]
        all_ref[0] = x_in
        gu = dot(x_in, gu_ref[...], ((1,), (0,)))
        d_hidden = dot(dy_ref[0], down_ref[...], ((1,), (1,)))
        gate_pre, up_pre = gu[:, :cut], gu[:, cut:]
        sig = jax.nn.sigmoid(gate_pre)
        swish = gate_pre * sig
        slope = sig * (1.0 + gate_pre * (1.0 - sig))
        hidden_ref[0] = (swish * up_pre).astype(BF16)
        d_gu_ref[0, :, :cut] = (d_hidden * up_pre * slope).astype(BF16)
        d_gu_ref[0, :, cut:] = (d_hidden * swish).astype(BF16)
        part_ref[0] = dot(d_gu_ref[0], gu_ref[...], ((1,), (1,))).astype(BF16)

    def block(size):
        return pl.BlockSpec((1, rows, size), lambda i: (first + i, 0, 0))

    def own(size):
        return pl.BlockSpec((1, rows, size), lambda i: (i, 0, 0))

    held = () if held is None else held
    return pl.pallas_call(
        kernel,
        grid=(count,),
        in_specs=[
            own(width),
            block(width),
            pl.BlockSpec(gu_w.shape, lambda i: (0, 0)),
            pl.BlockSpec(down_w.shape, lambda i: (0, 0)),
        ]
        + [pl.BlockSpec(memory_space=pl.ANY)] * len(held),
        out_specs=[block(width), block(cut), block(2 * cut), own(width)],
        out_shape=[
            jax.ShapeDtypeStruct((4, rows, width), BF16),
            jax.ShapeDtypeStruct((4, rows, cut), BF16),
            jax.ShapeDtypeStruct((4, rows, 2 * cut), BF16),
            jax.ShapeDtypeStruct((count, rows, width), BF16),
        ],
        input_output_aliases={4 + i: i for i in range(len(held))},
        compiler_params=pltpu.CompilerParams(vmem_limit_bytes=VMEM_LIMIT),
        cost_estimate=pl.CostEstimate(
            flops=10 * count * rows * width * cut,
            bytes_accessed=2 * (gu_w.size + down_w.size + count * rows * (4 * width + 3 * cut)),
            transcendentals=0,
        ),
    )(x, dy_all, gu_w, down_w, *held)


BESIDE = pl.CostEstimate(flops=0, bytes_accessed=0, transcendentals=0)


def fixed(shape):
    return pl.BlockSpec(shape, lambda *_: (0,) * len(shape))


def transposed_product(left, right, tile):
    depth, rows = left.shape
    cols = right.shape[1]

    def kernel(left_ref, right_ref, out_ref):
        out_ref[...] = dot(left_ref[...], right_ref[...], ((0,), (0,))).astype(BF16)

    return pl.pallas_call(
        kernel,
        grid=(rows // tile,),
        in_specs=[pl.BlockSpec((depth, tile), lambda i: (0, i)), fixed(right.shape)],
        out_specs=pl.BlockSpec((tile, cols), lambda i: (i, 0)),
        out_shape=jax.ShapeDtypeStruct((rows, cols), BF16),
        compiler_params=pltpu.CompilerParams(vmem_limit_bytes=VMEM_LIMIT),
        cost_estimate=BESIDE,
    )(left, right)


def product(left, right, tile):
    rows, depth = left.shape
    cols = right.shape[1]

    def kernel(left_ref, right_ref, out_ref):
        out_ref[...] = dot(left_ref[...], right_ref[...], ((1,), (0,))).astype(BF16)

    return pl.pallas_call(
        kernel,
        grid=(rows // tile,),
        in_specs=[pl.BlockSpec((tile, depth), lambda i: (i, 0)), fixed(right.shape)],
        out_specs=pl.BlockSpec((tile, cols), lambda i: (i, 0)),
        out_shape=jax.ShapeDtypeStruct((rows, cols), BF16),
        compiler_params=pltpu.CompilerParams(vmem_limit_bytes=VMEM_LIMIT),
        cost_estimate=BESIDE,
    )(left, right)


def side_product(left_t, right):
    def kernel(left_ref, right_ref, out_ref):
        total = dot(left_ref[0], right_ref[0], ((1,), (0,)))
        out_ref[...] = (total + dot(left_ref[1], right_ref[1], ((1,), (0,)))).astype(BF16)

    shape = (left_t.shape[1], right.shape[2])
    return pl.pallas_call(
        kernel,
        grid=(1,),
        in_specs=[fixed(left_t.shape), fixed(right.shape)],
        out_specs=fixed(shape),
        out_shape=jax.ShapeDtypeStruct(shape, BF16),
        compiler_params=pltpu.CompilerParams(vmem_limit_bytes=VMEM_LIMIT),
        cost_estimate=BESIDE,
    )(left_t, right)


def add_sums(ref, first, sums):
    row = lax.broadcasted_iota(jnp.int32, (8, 128), 0)
    value = jnp.zeros((8, 128), F32)
    for i, v in enumerate(sums):
        value = jnp.where(row == i, v, value)

    @pl.when(first)
    def _():
        ref[...] = jnp.zeros_like(ref)

    ref[...] += value


def side_spec(*shape):
    return pl.BlockSpec((1, *shape), lambda i: (i, 0, 0))


def out_project(tokens, attended_t, weights, gain, live, r):
    sides, rows, width = tokens.shape

    def kernel(x_ref, att_ref, w_ref, gain_ref, live_ref, middle_ref, second_ref, sums_ref):
        w_out = w_ref[:, :r].reshape(width, width)
        branch = dot(att_ref[0], w_out, ((0,), (0,)))
        middle = x_ref[0].astype(F32) + branch
        middle_ref[0] = middle
        inverse = lax.rsqrt(jnp.mean(middle * middle, axis=-1, keepdims=True) + EPSILON)
        second_ref[0] = (middle * inverse * gain_ref[...]).astype(BF16)
        mask = live_ref[0]
        sums = [jnp.sum(mask * branch * branch), jnp.sum(mask * middle * middle)]
        add_sums(sums_ref, pl.program_id(0) == 0, sums)

    return pl.pallas_call(
        kernel,
        grid=(sides,),
        in_specs=[
            side_spec(rows, width),
            side_spec(width, rows),
            fixed(weights.shape),
            fixed((1, width)),
            side_spec(rows, 1),
        ],
        out_specs=[side_spec(rows, width), side_spec(rows, width), fixed((8, 128))],
        out_shape=[
            jax.ShapeDtypeStruct(tokens.shape, F32),
            jax.ShapeDtypeStruct(tokens.shape, BF16),
            jax.ShapeDtypeStruct((8, 128), F32),
        ],
        compiler_params=pltpu.CompilerParams(vmem_limit_bytes=VMEM_LIMIT),
        cost_estimate=BESIDE,
    )(tokens, attended_t, weights, gain, live)


def norm_back(upstream, gain, value):
    inverse = lax.rsqrt(jnp.mean(value * value, axis=-1, keepdims=True) + EPSILON)
    normed = value * inverse
    scaled = upstream * gain
    grad = inverse * (scaled - normed * jnp.mean(scaled * normed, axis=-1, keepdims=True))
    return grad, jnp.sum(upstream * normed, axis=0, keepdims=True)


def add_row(ref, first, row):
    @pl.when(first)
    def _():
        ref[...] = jnp.zeros_like(ref)

    ref[...] += row


def middle_back(d_second, middle, cotangent, gain, weights):
    sides, rows, width = middle.shape

    def kernel(d_ref, m_ref, cot_ref, gain_ref, w_ref, gm_ref, branch_ref, do_ref, gain_grad_ref):
        grad, gain_grad = norm_back(d_ref[0], gain_ref[...], m_ref[0])
        grad_middle = cot_ref[0].astype(F32) + grad
        gm_ref[0] = grad_middle
        d_branch = grad_middle.astype(BF16)
        branch_ref[0] = d_branch
        do_ref[0] = dot(d_branch, w_ref[...], ((1,), (1,))).T.astype(BF16)
        add_row(gain_grad_ref, pl.program_id(0) == 0, gain_grad)

    return pl.pallas_call(
        kernel,
        grid=(sides,),
        in_specs=[
            side_spec(rows, width),
            side_spec(rows, width),
            side_spec(rows, width),
            fixed((1, width)),
            fixed(weights.shape),
        ],
        out_specs=[
            side_spec(rows, width),
            side_spec(rows, width),
            side_spec(width, rows),
            fixed((1, width)),
        ],
        out_shape=[
            jax.ShapeDtypeStruct(middle.shape, F32),
            jax.ShapeDtypeStruct(middle.shape, BF16),
            jax.ShapeDtypeStruct((sides, width, rows), BF16),
            jax.ShapeDtypeStruct((1, width), F32),
        ],
        compiler_params=pltpu.CompilerParams(vmem_limit_bytes=VMEM_LIMIT),
        cost_estimate=BESIDE,
    )(d_second, middle, cotangent, gain, weights)


def first_back(d_q, d_kv, weights, tokens, grad_middle, gain, live):
    sides, rows, width = tokens.shape
    q_width, kv_width = d_q.shape[1], d_kv.shape[1]

    def kernel(
        dq_ref, dkv_ref, w_ref, x_ref, gm_ref, gain_ref, live_ref, out_ref, gain_grad_ref, sums_ref
    ):
        d_first = dot(dq_ref[0].T, w_ref[:, :q_width], ((1,), (1,)))
        d_first += dot(dkv_ref[0].T, w_ref[:, q_width : q_width + kv_width], ((1,), (1,)))
        grad, gain_grad = norm_back(d_first, gain_ref[...], x_ref[0].astype(F32))
        total = gm_ref[0] + grad
        out_ref[0] = total.astype(BF16)
        add_row(gain_grad_ref, pl.program_id(0) == 0, gain_grad)
        add_sums(sums_ref, pl.program_id(0) == 0, [jnp.sum(live_ref[0] * total * total)])

    return pl.pallas_call(
        kernel,
        grid=(sides,),
        in_specs=[
            side_spec(q_width, rows),
            side_spec(kv_width, rows),
            fixed(weights.shape),
            side_spec(rows, width),
            side_spec(rows, width),
            fixed((1, width)),
            side_spec(rows, 1),
        ],
        out_specs=[side_spec(rows, width), fixed((1, width)), fixed((8, 128))],
        out_shape=[
            jax.ShapeDtypeStruct(tokens.shape, BF16),
            jax.ShapeDtypeStruct((1, width), F32),
            jax.ShapeDtypeStruct((8, 128), F32),
        ],
        compiler_params=pltpu.CompilerParams(vmem_limit_bytes=VMEM_LIMIT),
        cost_estimate=BESIDE,
    )(d_q, d_kv, weights, tokens, grad_middle, gain, live)


def finish(middle, branch_ffn, live, gain_one, gain_two, early_sums, late_sums):
    sides, rows, width = middle.shape

    def kernel(m_ref, f_ref, live_ref, one_ref, two_ref, early_ref, late_ref, out_ref, small_ref):
        result = m_ref[0] + f_ref[0]
        out_ref[0] = result.astype(BF16)
        mask = live_ref[0]
        own = [jnp.sum(mask * result * result), jnp.sum(mask * f_ref[0] * f_ref[0]), jnp.sum(mask)]
        first = pl.program_id(0) == 0
        row = lax.broadcasted_iota(jnp.int32, (8, width), 0)
        value = jnp.where(row == 2, own[0], 0.0)
        value = jnp.where(row == 5, own[1], value)
        value = jnp.where(row == 7, own[2], value)

        @pl.when(first)
        def _():
            start = jnp.where(row == 0, one_ref[...], 0.0)
            start = jnp.where(row == 1, two_ref[...], start)
            start = jnp.where(row == 3, late_ref[0:1, 0:1], start)
            start = jnp.where(row == 4, early_ref[0:1, 0:1], start)
            small_ref[...] = jnp.where(row == 6, early_ref[1:2, 0:1], start)

        small_ref[...] += value

    return pl.pallas_call(
        kernel,
        grid=(sides,),
        in_specs=[
            side_spec(rows, width),
            side_spec(rows, width),
            side_spec(rows, 1),
            fixed((1, width)),
            fixed((1, width)),
            fixed((8, 128)),
            fixed((8, 128)),
        ],
        out_specs=[side_spec(rows, width), fixed((8, width))],
        out_shape=[
            jax.ShapeDtypeStruct(middle.shape, BF16),
            jax.ShapeDtypeStruct((8, width), F32),
        ],
        compiler_params=pltpu.CompilerParams(vmem_limit_bytes=VMEM_LIMIT),
        cost_estimate=BESIDE,
    )(middle, branch_ffn, live, gain_one, gain_two, early_sums, late_sums)


def norm_forward(value_rows, gain):
    inverse = lax.rsqrt(jnp.mean(value_rows * value_rows, axis=-1, keepdims=True) + EPSILON)
    normed = value_rows * inverse
    return (normed * gain, normed, inverse)


def norm_backward(upstream, gain, normed, inverse):
    scaled = upstream * gain
    grad_in = inverse * (scaled - normed * jnp.mean(scaled * normed, axis=-1, keepdims=True))
    return (grad_in, jnp.sum(upstream * normed, axis=0))


def ein(spec, left, right):
    return jnp.einsum(spec, left, right, preferred_element_type=F32)


def turn(v, cosine, sine):
    half = HEAD_DIM // 2
    a, b = v[:, :, :half], v[:, :, half:]
    return jnp.concatenate([a * cosine - b * sine, a * sine + b * cosine], axis=2)


def per_device(
    tokens, cotangent, segments, valid, norm_one, w_query, w_key, w_value, w_out,
    norm_two, w_gate, w_up, w_down,
):
    c = lax.axis_index("ctx")
    n = lax.axis_size("fsdp")
    f = lax.axis_index("fsdp")
    row_count = tokens.shape[1]
    rows = row_count // 2
    width = tokens.shape[2]
    blocks = 8
    q_width, kv_width = w_query.shape[1], w_key.shape[1]
    ff = w_gate.shape[1]
    r = w_query.shape[0]
    c_ref = c.reshape(1).astype(jnp.int32)

    q_blocks = jnp.stack([c, blocks - 1 - c]).astype(jnp.int32)
    seg_blocks = segments[0].reshape(blocks, rows)
    valid_blocks = valid[0].reshape(blocks, rows)
    seg_q = jnp.stack([take(seg_blocks, q_blocks[0], 0), take(seg_blocks, q_blocks[1], 0)])
    live = jnp.stack([take(valid_blocks, q_blocks[0], 0), take(valid_blocks, q_blocks[1], 0)])
    seg_q = seg_q[:, None, :].astype(F32)
    seg_k = seg_blocks[:, None, :].astype(F32)
    valid_k = valid_blocks[:, None, :].astype(F32)
    owners = c ^ jnp.arange(4, dtype=jnp.int32)
    block_of = jnp.stack([owners, blocks - 1 - owners], axis=1)
    every = jnp.arange(blocks, dtype=jnp.int32)
    side = (every >= 4).astype(jnp.int32)
    slots = (c ^ jnp.where(every < 4, every, blocks - 1 - every)) * 2 + side
    slots = slots.astype(jnp.int32)
    places = block_of[:, :, None] * rows + jnp.arange(rows, dtype=jnp.int32)
    half = HEAD_DIM // 2
    freqs = jnp.exp(jnp.arange(half, dtype=F32) * (-math.log(ROPE_BASE) / half))
    angles = places.astype(F32).reshape(8, 1, rows) * freqs[None, :, None]
    cosine, sine = jnp.cos(angles), jnp.sin(angles)

    tokens_own = tokens[0].reshape(2, rows, width)
    tokens_x, tokens_y = swap_x(tokens_own), swap_y(tokens_own)
    gains = jnp.stack([norm_one, norm_two], axis=1)
    gains = jnp.concatenate([gains, jnp.zeros((r, 126), BF16)], axis=1)
    qkv_shard = jnp.concatenate([w_query, w_key, w_value, gains], axis=1)
    c4 = qkv_shard.shape[1] // 4
    qkv_z = z_fetch(lax.dynamic_slice_in_dim(qkv_shard, c * c4, c4, 1))
    d4 = w_down.shape[0] // 4
    down_shard = lax.dynamic_slice_in_dim(w_down, c * d4, d4, 0)
    out_down_shard = after(jnp.concatenate([w_out, down_shard]), qkv_z)
    out_down = lax.all_gather(out_down_shard, "fsdp", axis=0)
    qkv_z, tokens_x, tokens_y = sync(qkv_z, tokens_x, tokens_y)
    qkv_x, qkv_y = swap_x(qkv_z), swap_y(qkv_z)
    gu_shard = after(pick_columns(c_ref, w_gate, w_up, n), qkv_z)
    gu_w = lax.all_gather(gu_shard, "fsdp", axis=0, tiled=True)
    cut = ff // 4
    live_rows = live.reshape(2, rows, 1).astype(F32)
    qkv_x, qkv_y, tokens_x, tokens_y, cosine, sine, live_rows = sync(
        qkv_x, qkv_y, tokens_x, tokens_y, cosine, sine, live_rows
    )
    zh = qkv_z.shape[0] // 2
    qkv_mine = jnp.stack([qkv_z, qkv_x, qkv_y])
    qkv_d = swap_y(qkv_x[:zh]), swap_x(qkv_y[zh:])
    tokens_d = swap_y(tokens_x[:1]), swap_x(tokens_y[1:])
    qkv_other = core_swap(qkv_mine)
    qkv_d, tokens_d, qkv_other = sync(qkv_d, tokens_d, qkv_other)
    qkv_d = jnp.concatenate(qkv_d)[None]
    qkv_other_d = core_swap(qkv_d)
    dy_own = cotangent[0].reshape(2, rows, width)
    dy_pieces = ctx_fetch_direct(after(dy_own, qkv_other_d))

    first_all, q_t, kv_all, qkv_w, gain_rows = project(
        c,
        f,
        (tokens_own, tokens_x, tokens_y, *tokens_d),
        (qkv_mine, qkv_d),
        (qkv_other, qkv_other_d),
        cosine,
        sine,
        q_width,
    )
    gain_one, gain_two = gain_rows[0:1], gain_rows[1:2]
    first_all = first_all.reshape(4, 2, rows, width)
    o_t, lse = attention_forward(q_blocks, slots, seg_q, seg_k, valid_k, q_t, kv_all)
    o_t, out_down, dy_pieces, gu_w = sync(o_t, out_down, dy_pieces, gu_w)
    out_w = out_down[:, :r].reshape(n * r, width)
    down_w = out_down[:, r:].reshape(cut, width)
    dy_all, out_w = sync(jnp.stack(dy_pieces).reshape(4, row_count, width), out_w)
    attended_t = o_t.reshape(2, width, rows)
    out_rows = out_down if r % 16 == 0 else out_w.reshape(n, r, width)
    middle, x_own, early_sums = out_project(
        tokens_own, attended_t, out_rows, gain_two, live_rows, r
    )

    x_x, x_y = swap_x(x_own), swap_y(x_own)
    held = feed_forward(x_own.reshape(1, row_count, width), dy_all, gu_w, down_w, 0, None)
    x_x, x_y, *held = sync(x_x, x_y, *held)
    parts_0 = held.pop()
    x_d = jnp.concatenate([swap_y(x_x[:1]), swap_x(x_y[1:])])
    x_xy = jnp.stack([x_x, x_y]).reshape(2, row_count, width)
    held = feed_forward(x_xy, dy_all, gu_w, down_w, 1, held)
    x_d, *held = sync(x_d, *held)
    parts_1 = held.pop()
    x_d = x_d.reshape(1, row_count, width)
    *held, parts_2 = feed_forward(x_d, dy_all, gu_w, down_w, 3, held)
    parts = [v.reshape(2, rows, width) for v in (parts_0[0], parts_1[0], parts_1[1], parts_2[0])]
    got = scatter_first(parts)
    x_all, hidden, d_gu = [v.reshape(4 * row_count, -1) for v in held]
    dy_all = dy_all.reshape(4 * row_count, width)
    grad_gu = transposed_product(x_all, d_gu, 256)
    ffn_parts = product(after(hidden, grad_gu), down_w, row_count)
    got_low, got_high, grad_gu, ffn_parts = sync(*got, grad_gu, ffn_parts)
    d_second = scatter_last(*scatter_pass(parts, (got_low, got_high)))
    grad_d = transposed_product(after(hidden, ffn_parts), dy_all, cut)
    d_second, grad_d = sync(d_second, grad_d)
    ffn_parts = ffn_parts.reshape(4, 2, rows, width)
    ffn_parts = [ffn_parts[i] for i in range(4)]
    own_gu = lax.psum_scatter(grad_gu, "fsdp", scatter_dimension=0, tiled=True)
    own_down = lax.psum_scatter(grad_d, "fsdp", scatter_dimension=0, tiled=True)

    k = f % 2
    nz = n // 2
    r4 = r // 4
    grad_middle, d_branch, do_t, grad_gain_two = middle_back(
        d_second, middle, dy_own, gain_two, out_w
    )
    do_t = do_t.reshape(2, HEADS, HEAD_DIM, rows)
    whole_out = side_product(attended_t, d_branch)
    do_t, ffn_parts, whole_out = sync(do_t, ffn_parts, whole_out)
    ffn_got = scatter_first(ffn_parts)
    d_q, dkv_low, dkv_high, dkv_keep = attention_backward(
        q_blocks, slots, seg_q, seg_k, valid_k, cosine[:2], sine[:2], q_t, kv_all, o_t, do_t, lse
    )
    d_q, dkv_low, dkv_high, dkv_keep, ffn_got = sync(d_q, dkv_low, dkv_high, dkv_keep, ffn_got)
    dkv_got = swap_x(dkv_low), swap_y(dkv_high)
    own_out = lax.psum_scatter(
        after(whole_out, dkv_low, own_gu), "fsdp", scatter_dimension=0, tiled=True
    )
    q4, kv4 = q_width // 4, kv_width // 2

    def quarter(v, size, i):
        return lax.dynamic_slice_in_dim(v, (c ^ i) * size, size, 1)

    d_q = d_q.reshape(2, q_width, rows)
    dq_parts = [quarter(d_q, q4, i) for i in range(4)]
    ffn_sums = scatter_pass(ffn_parts, ffn_got)
    dkv_got, dq_parts, ffn_sums = sync(dkv_got, dq_parts, ffn_sums)
    kept = dkv_keep.astype(F32)
    low_sums, high_sums = kept[:2] + dkv_got[0].astype(F32), kept[2:] + dkv_got[1].astype(F32)
    from_y, from_x = swap_y(low_sums[1].astype(BF16)), swap_x(high_sums[1].astype(BF16))
    dkv_own = jnp.stack([low_sums[0] + from_y.astype(F32), high_sums[0] + from_x.astype(F32)])
    dkv_own = dkv_own.reshape(2, 2 * KV_HEADS, HEAD_DIM, rows)
    dq_got = exchange_first(dq_parts)
    d_k = turn(dkv_own[:, :KV_HEADS], cosine[:2, None], -sine[:2, None]).astype(BF16)
    d_kv = jnp.concatenate([d_k, dkv_own[:, KV_HEADS:].astype(BF16)], axis=1)
    d_kv = d_kv.reshape(2, 2 * kv_width, rows)
    dkv_parts = [quarter(d_kv, kv4, i) for i in range(4)]
    dkv_got = exchange_first(dkv_parts)
    dq_got, dkv_got, ffn_sums = sync(dq_got, dkv_got, ffn_sums)
    diagonal = (
        swap_y(jnp.concatenate([dq_got[0][2:], dkv_got[0][2:]], axis=1)),
        swap_x(jnp.concatenate([dq_got[1][2:], dkv_got[1][2:]], axis=1)),
    )
    ffn_last = swap_y(ffn_sums[2]), swap_x(ffn_sums[3])
    dq_pieces = [dq_parts[0], *dq_got]
    dkv_pieces = [dkv_parts[0], *dkv_got]
    diagonal, own_out = sync(diagonal, own_out)
    own_out = own_out.reshape(4, r4, width)
    out_parts = [take(own_out, c ^ i, 0) for i in range(4)]
    out_got = scatter_first(out_parts)
    grad_qkv = project_grad(first_all.reshape(8, rows, width), dq_pieces, dkv_pieces, diagonal)
    grad_qkv = grad_qkv.reshape(nz, 2, r, q4 + kv4)
    got_half = core_swap(take(grad_qkv, k ^ 1, 1))
    pair_qkv = (take(grad_qkv, k, 1).astype(F32) + got_half.astype(F32)).astype(BF16)
    pair_qkv, d_q, d_kv, ffn_last, own_gu, out_got = sync(
        pair_qkv, d_q, d_kv, ffn_last, own_gu, out_got
    )
    branch_ffn = jnp.concatenate([v + g.astype(F32) for v, g in zip(ffn_sums[:2], ffn_last)])
    own_qkv = z_scatter(pair_qkv).astype(BF16)

    gu_x, gu_y = swap_x(own_gu), swap_y(own_gu)
    out_sums = scatter_pass(out_parts, out_got)
    grad_tokens, grad_gain_one, late_sums = first_back(
        d_q, d_kv, qkv_w, tokens_own, grad_middle, gain_one, live_rows
    )
    result, small = finish(
        middle, branch_ffn, live_rows, grad_gain_one, grad_gain_two, early_sums, late_sums
    )
    own_qkv, small, gu_x, gu_y, out_sums = sync(own_qkv, small, gu_x, gu_y, out_sums)

    small = small + core_swap(small)
    own_out = scatter_last(*out_sums).astype(BF16)
    qkv_pieces = ctx_fetch_direct(own_qkv)
    small, own_out, gu_x, gu_y = sync(small, own_out, gu_x, gu_y)
    small = z_sum(small)
    hr = gu_x.shape[0] // 2
    gu_d = jnp.concatenate([swap_y(gu_x[:hr]), swap_x(gu_y[hr:])])
    small, own_down, gu_d, own_out = sync(small, own_down, gu_d, own_out)
    small = sum(ctx_fetch_direct(small))
    down_pieces = ctx_fetch_direct(own_down)
    out_pieces = ctx_fetch_direct(own_out)
    grad_q, grad_k, grad_v = join_columns(c_ref, qkv_pieces, q4, kv4)
    grad_gate_w, grad_up_w = unpick_columns(c_ref, [own_gu, gu_x, gu_y, gu_d], n)
    grad_down_w = in_order(down_pieces, 0).reshape(4 * d4, width).astype(F32)
    grad_out_w = in_order(out_pieces, 0).reshape(r, width).astype(F32)
    gain_sums = lax.dynamic_slice_in_dim(small[:2], f * r, r, 1)
    squares = small[2:8, 0]
    spreads = jnp.sqrt(squares[:5] / (squares[5] * width))
    return (
        result.reshape(1, row_count, width),
        grad_tokens.reshape(1, row_count, width),
        gain_sums[0],
        grad_q,
        grad_k,
        grad_v,
        grad_out_w,
        gain_sums[1],
        grad_gate_w,
        grad_up_w,
        grad_down_w,
        spreads,
    )


def solution(mesh):
    rows, shard, vector = P("fsdp", "ctx", None), P("fsdp", None), P("fsdp")
    return jax.shard_map(
        per_device,
        mesh=mesh,
        in_specs=(
            rows, rows, shard, shard, vector, shard, shard, shard, shard, vector,
            shard, shard, shard,
        ),
        out_specs=(
            rows, rows, vector, shard, shard, shard, shard, vector, shard, shard, shard, P(),
        ),
        check_vma=False,
    )
```

```python
import functools
import math

import jax
import jax.numpy as jnp
from jax import lax
from jax.experimental import pallas as pl
from jax.experimental.pallas import tpu as pltpu
from jax.sharding import PartitionSpec as P

HEADS = 20
KV_HEADS = 5
HEAD_DIM = 64
GROUP = HEADS // KV_HEADS
WINDOW = 1024
EPSILON = 1e-05
MASKED = -1e30
ROPE_BASE = 10000.0
VMEM_LIMIT = 60 * 2**20
BF16 = jnp.bfloat16
F32 = jnp.float32


def core_swap(v):
    n = lax.axis_size("fsdp")
    return lax.ppermute(v, "fsdp", [(i, i ^ 1) for i in range(n)])


def swap_x(v):
    return lax.ppermute(v, "ctx", [(i, i ^ 1) for i in range(4)])


def swap_y(v):
    return lax.ppermute(v, "ctx", [(i, i ^ 2) for i in range(4)])


def put(buffer, piece, index, axis):
    return lax.dynamic_update_slice_in_dim(
        buffer, jnp.expand_dims(piece, axis), index, axis
    )


def take(v, index, axis):
    return lax.dynamic_index_in_dim(v, index, axis, keepdims=False)


def place(pieces, axis):
    first = pieces[0][1]
    shape = first.shape[:axis] + (len(pieces),) + first.shape[axis:]
    buffer = jnp.zeros(shape, first.dtype)
    for index, piece in pieces:
        buffer = put(buffer, piece, index, axis)
    return buffer


def z_fetch(piece):
    n = lax.axis_size("fsdp")
    nz = n // 2
    if nz != 4:
        groups = [list(range(0, n, 2)), list(range(1, n, 2))]
        every = lax.all_gather(piece, "fsdp", axis=0, axis_index_groups=groups)
        z = lax.axis_index("fsdp") // 2
        return jnp.take(every, (z - jnp.arange(nz)) % nz, axis=0)
    pieces = [piece]
    for d in (1, 2, 3):
        pieces.append(lax.ppermute(piece, "fsdp", [(i, (i + 2 * d) % n) for i in range(n)]))
    return jnp.stack(pieces)


def z_scatter(pieces):
    n = lax.axis_size("fsdp")
    nz = n // 2
    if nz != 4:
        groups = [list(range(0, n, 2)), list(range(1, n, 2))]
        return lax.psum_scatter(
            pieces, "fsdp", scatter_dimension=0, axis_index_groups=groups
        ).astype(F32)
    z = lax.axis_index("fsdp") // 2
    total = take(pieces, z, 0).astype(F32)
    for d in (1, 2, 3):
        sent = take(pieces, (z + d) % nz, 0)
        got = lax.ppermute(sent, "fsdp", [(i, (i + 2 * d) % n) for i in range(n)])
        total = total + got.astype(F32)
    return total


def sync(*values):
    return lax.optimization_barrier(values)


def ctx_fetch(piece):
    half = piece.shape[0] // 2
    from_x = swap_x(piece)
    from_y = swap_y(piece)
    from_d = jnp.concatenate([swap_y(from_x[:half]), swap_x(from_y[half:])], axis=0)
    return [piece, from_x, from_y, from_d]


def after(v, *earlier):
    return lax.optimization_barrier((v, earlier))[0]


def ctx_fetch_direct(piece):
    diagonal = lax.ppermute(piece, "ctx", [(i, i ^ 3) for i in range(4)])
    return [piece, swap_x(piece), swap_y(piece), diagonal]


def in_order(pieces, axis):
    c = lax.axis_index("ctx")
    return place([(c ^ i, v) for i, v in enumerate(pieces)], axis)


def scatter_first(parts):
    half = parts[0].shape[0] // 2
    low_got = swap_x(jnp.concatenate([parts[1][:half], parts[3][:half]]))
    high_got = swap_y(jnp.concatenate([parts[2][half:], parts[3][half:]]))
    return low_got, high_got


def scatter_pass(parts, got):
    half = parts[0].shape[0] // 2
    rest = parts[0].shape[0] - half
    low_got, high_got = got[0].astype(F32), got[1].astype(F32)
    low_pass = (parts[2][:half].astype(F32) + low_got[half:]).astype(BF16)
    high_pass = (parts[1][half:].astype(F32) + high_got[rest:]).astype(BF16)
    low_own = parts[0][:half].astype(F32) + low_got[:half]
    high_own = parts[0][half:].astype(F32) + high_got[:rest]
    return low_own, high_own, low_pass, high_pass


def scatter_last(low_own, high_own, low_pass, high_pass):
    from_y, from_x = swap_y(low_pass), swap_x(high_pass)
    return jnp.concatenate([low_own + from_y.astype(F32), high_own + from_x.astype(F32)])


def exchange_first(parts):
    to_x = jnp.concatenate([parts[1], parts[3][:1]], axis=0)
    to_y = jnp.concatenate([parts[2], parts[3][1:]], axis=0)
    return swap_x(to_x), swap_y(to_y)


def z_sum(v):
    n = lax.axis_size("fsdp")
    if n == 8:
        return v + sum(
            lax.ppermute(v, "fsdp", [(i, (i + 2 * d) % n) for i in range(n)]) for d in (1, 2, 3)
        )
    bit = 2
    while bit < n:
        v = v + lax.ppermute(v, "fsdp", [(i, i ^ bit) for i in range(n)])
        bit *= 2
    return v


def pick_columns(c, out, gate, up, count):
    r, ff = gate.shape
    width = out.shape[1]
    group = ff // count
    strip = group // 4

    def kernel(c_ref, w_ref, gate_ref, up_ref, out_ref):
        out_ref[:, :width] = w_ref[...]
        for own in range(4):

            @pl.when(c_ref[0] == own)
            def _():
                for j in range(count):
                    at = j * group + own * strip
                    to = width + j * strip
                    out_ref[:, to : to + strip] = gate_ref[:, at : at + strip]
                    to += ff // 4
                    out_ref[:, to : to + strip] = up_ref[:, at : at + strip]

    whole = pl.BlockSpec((r, ff), lambda i, s: (0, 0))
    return pl.pallas_call(
        kernel,
        grid_spec=pltpu.PrefetchScalarGridSpec(
            num_scalar_prefetch=1,
            grid=(1,),
            in_specs=[pl.BlockSpec((r, width), lambda i, s: (0, 0)), whole, whole],
            out_specs=pl.BlockSpec((r, width + ff // 2), lambda i, s: (0, 0)),
        ),
        out_shape=jax.ShapeDtypeStruct((r, width + ff // 2), BF16),
        cost_estimate=pl.CostEstimate(flops=0, bytes_accessed=6 * r * ff, transcendentals=0),
    )(c, out, gate, up)


def unpick_columns(c, pieces, count):
    r, half = pieces[0].shape
    ff = 2 * half
    group = ff // count
    strip = group // 4

    def kernel(c_ref, *refs):
        gate_ref, up_ref = refs[4:]
        for own in range(4):

            @pl.when(c_ref[0] == own)
            def _():
                for step in range(4):
                    for j in range(count):
                        at = j * group + (own ^ step) * strip
                        piece = refs[step]
                        gate_ref[:, at : at + strip] = piece[
                            :, j * strip : (j + 1) * strip
                        ].astype(F32)
                        frm = ff // 4 + j * strip
                        up_ref[:, at : at + strip] = piece[:, frm : frm + strip].astype(F32)

    whole = pl.BlockSpec((r, ff), lambda i, s: (0, 0))
    return pl.pallas_call(
        kernel,
        grid_spec=pltpu.PrefetchScalarGridSpec(
            num_scalar_prefetch=1,
            grid=(1,),
            in_specs=[pl.BlockSpec((r, half), lambda i, s: (0, 0))] * 4,
            out_specs=[whole, whole],
        ),
        out_shape=[jax.ShapeDtypeStruct((r, ff), F32)] * 2,
        compiler_params=pltpu.CompilerParams(vmem_limit_bytes=VMEM_LIMIT),
        cost_estimate=pl.CostEstimate(flops=0, bytes_accessed=12 * r * ff, transcendentals=0),
    )(c, *pieces)


def join_columns(c, pieces, q4, kv4):
    r = pieces[0].shape[0]

    def kernel(c_ref, *refs):
        q_ref, k_ref, v_ref = refs[4:]
        for own in range(4):

            @pl.when(c_ref[0] == own)
            def _():
                for step in range(4):
                    to = own ^ step
                    piece = refs[step][...].astype(F32)
                    q_ref[:, to * q4 : (to + 1) * q4] = piece[:, :q4]
                    target = k_ref if to < 2 else v_ref
                    at = (to % 2) * kv4
                    target[:, at : at + kv4] = piece[:, q4:]

    def whole(cols):
        return pl.BlockSpec((r, cols), lambda i, s: (0, 0))

    return pl.pallas_call(
        kernel,
        grid_spec=pltpu.PrefetchScalarGridSpec(
            num_scalar_prefetch=1,
            grid=(1,),
            in_specs=[whole(q4 + kv4)] * 4,
            out_specs=[whole(4 * q4), whole(2 * kv4), whole(2 * kv4)],
        ),
        out_shape=[
            jax.ShapeDtypeStruct((r, cols), F32) for cols in (4 * q4, 2 * kv4, 2 * kv4)
        ],
        cost_estimate=pl.CostEstimate(
            flops=0, bytes_accessed=24 * r * (q4 + kv4), transcendentals=0
        ),
    )(c, *pieces)


def pair_bias(q_block, k_block, rows, seg_q, seg_k, valid_k):
    key_at = k_block * rows + lax.broadcasted_iota(jnp.int32, (rows, rows), 0)
    query_at = q_block * rows + lax.broadcasted_iota(jnp.int32, (rows, rows), 1)
    distance = query_at - key_at
    allowed = (
        (seg_q == seg_k)
        & (distance >= 0)
        & (distance < WINDOW)
        & ((valid_k == 1.0) | (distance == 0))
    )
    return jnp.where(allowed, 0.0, MASKED).astype(F32)


def first_block(q_block, rows):
    reach = (WINDOW + rows - 2) // rows
    return jnp.maximum(q_block - reach, 0)


def dot(a, b, dims):
    return lax.dot_general(a, b, (dims, ((), ())), preferred_element_type=F32)


def column(row):
    size = row.shape[1]
    return jnp.broadcast_to(row, (size, size)).T


def fill_bias(blocks_ref, seg_q_ref, seg_k_ref, valid_k_ref, bias_ref, rows):
    for side in range(2):
        b = blocks_ref[side]
        lo = first_block(b, rows)

        def body(kb, _):
            bias_ref[side, kb - lo] = pair_bias(
                b, kb, rows, seg_q_ref[side], column(seg_k_ref[kb]), column(valid_k_ref[kb])
            )
            return 0

        lax.fori_loop(lo, b + 1, body, 0)


def forward_kernel(
    blocks_ref, slots_ref, seg_q_ref, seg_k_ref, valid_k_ref, q_ref, k_ref, v_ref,
    o_ref, lse_ref, bias_ref, scores_ref, acc_ref,
):
    rows = q_ref.shape[-1]

    @pl.when(pl.program_id(0) == 0)
    def _():
        fill_bias(blocks_ref, seg_q_ref, seg_k_ref, valid_k_ref, bias_ref, rows)

    for side in range(2):
        b = blocks_ref[side]
        lo = first_block(b, rows)

        def score(kb, peaks):
            keys = k_ref[slots_ref[kb], 0].T
            bias = bias_ref[side, kb - lo]
            higher = []
            for h in range(GROUP):
                s = dot(keys, q_ref[side, h], ((1,), (0,))) + bias
                scores_ref[kb - lo, h] = s
                higher.append(jnp.maximum(peaks[h], jnp.max(s, axis=0, keepdims=True)))
            return tuple(higher)

        peaks = lax.fori_loop(
            lo, b + 1, score, (jnp.full((1, rows), -jnp.inf, F32),) * GROUP
        )
        acc_ref[...] = jnp.zeros_like(acc_ref)

        def mix(kb, totals):
            values_t = v_ref[slots_ref[kb], 0]
            more = []
            for h in range(GROUP):
                p = jnp.exp(scores_ref[kb - lo, h] - peaks[h])
                more.append(totals[h] + jnp.sum(p, axis=0, keepdims=True))
                acc_ref[h] += dot(values_t, p.astype(BF16), ((1,), (0,)))
            return tuple(more)

        totals = lax.fori_loop(lo, b + 1, mix, (jnp.zeros((1, rows), F32),) * GROUP)
        for h in range(GROUP):
            o_ref[side, h] = (acc_ref[h] / totals[h]).astype(BF16)
            lse_ref[side, 0, h : h + 1] = peaks[h] + jnp.log(totals[h])


def backward_kernel(
    blocks_ref, slots_ref, seg_q_ref, seg_k_ref, valid_k_ref, cos_ref, sin_ref, q_ref, k_ref, v_ref,
    o_ref, do_ref, lse_ref,
    dq_ref, low_ref, high_ref, keep_ref,
    bias_ref, acc_ref, center_ref, dk_ref, dv_ref, p_ref, ds_ref,
):
    rows = q_ref.shape[-1]
    half = HEAD_DIM // 2

    @pl.when(pl.program_id(0) == 0)
    def _():
        fill_bias(blocks_ref, seg_q_ref, seg_k_ref, valid_k_ref, bias_ref, rows)

    dk_ref[...] = jnp.zeros_like(dk_ref)
    dv_ref[...] = jnp.zeros_like(dv_ref)
    for side in range(2):
        b = blocks_ref[side]
        lo = first_block(b, rows)
        acc_ref[...] = jnp.zeros_like(acc_ref)
        for h in range(GROUP):
            center_ref[h : h + 1] = jnp.sum(
                o_ref[side, h].astype(F32) * do_ref[side, h].astype(F32), axis=0, keepdims=True
            )

        def soft(kb, at):
            slot = slots_ref[kb]
            keys = k_ref[slot, 0].T
            values = v_ref[slot, 0].T
            bias = bias_ref[side, kb - lo]
            for h in range(GROUP):
                s = dot(keys, q_ref[side, h], ((1,), (0,))) + bias
                p = jnp.exp(s - lse_ref[side, 0, h : h + 1])
                dp = dot(values, do_ref[side, h], ((1,), (0,)))
                p_ref[at, h] = p.astype(BF16)
                ds_ref[at, h] = (p * (dp - center_ref[h : h + 1])).astype(BF16)

        def products(kb, at):
            slot = slots_ref[kb]
            dv = dot(do_ref[side, 0], p_ref[at, 0], ((1,), (1,)))
            dk = dot(q_ref[side, 0], ds_ref[at, 0], ((1,), (1,)))
            for h in range(1, GROUP):
                dv += dot(do_ref[side, h], p_ref[at, h], ((1,), (1,)))
                dk += dot(q_ref[side, h], ds_ref[at, h], ((1,), (1,)))
            dv_ref[slot] += dv
            dk_ref[slot] += dk
            for h in range(GROUP):
                acc_ref[h] += dot(k_ref[slot, 0], ds_ref[at, h], ((1,), (0,)))

        soft(lo, 0)

        def body(kb, _):
            products(kb - 1, (kb - 1 - lo) % 2)
            soft(kb, (kb - lo) % 2)
            return 0

        lax.fori_loop(lo + 1, b + 1, body, 0)
        products(b, (b - lo) % 2)
        cos, sin = cos_ref[side], sin_ref[side]
        for h in range(GROUP):
            a, b2 = acc_ref[h, :half] * 0.125, acc_ref[h, half:] * 0.125
            turned = jnp.concatenate([a * cos + b2 * sin, b2 * cos - a * sin], axis=0)
            dq_ref[side, h] = turned.astype(BF16)
    for target, slots in ((low_ref, (2, 6)), (high_ref, (5, 7)), (keep_ref, (0, 4, 1, 3))):
        for i, slot in enumerate(slots):
            target[i, 0, 0] = dk_ref[slot].astype(BF16)
            target[i, 1, 0] = dv_ref[slot].astype(BF16)


def project(c, f, tokens, mine, other, cosine, sine, q_width):
    _, rows, width = tokens[0].shape
    blocks = 8
    _, nz, r, cols = mine[0].shape
    half = HEAD_DIM // 2
    kv_heads = 2 * KV_HEADS
    gains_at = q_width + kv_heads * HEAD_DIM

    def turned(flat_t, at, cos, sin):
        a, b = flat_t[at : at + half], flat_t[at + half : at + HEAD_DIM]
        return jnp.concatenate([a * cos - b * sin, a * sin + b * cos], axis=0)

    def kernel(at_ref, *refs):
        token_refs, mine_refs, other_refs = refs[:5], refs[5:7], refs[7:9]
        cos_ref, sin_ref, first_ref, q_ref, kv_ref, w_ref, gain_ref, x_ref = refs[9:]

        @pl.when(pl.program_id(0) == 0)
        def _():
            for core in range(2):
                for q in range(4):
                    step = q ^ at_ref[0]

                    def fill(index, which, core=core, q=q):
                        for z in range(nz):
                            z_step = (at_ref[1] // 2 - z + nz) % nz
                            for kk in range(2):
                                source = mine_refs if kk == core else other_refs
                                at = (2 * z + kk) * r
                                w_ref[at : at + r, q * cols : (q + 1) * cols] = source[which][
                                    index, z_step
                                ]

                    @pl.when((at_ref[1] % 2 == core) & (step < 3))
                    def _(step=step, fill=fill):
                        fill(step, 0)

                    @pl.when((at_ref[1] % 2 == core) & (step == 3))
                    def _(fill=fill):
                        fill(0, 1)

            gain_ref[...] = w_ref[:, gains_at:].astype(F32).T[:8]

        for i in range(3):

            @pl.when(pl.program_id(0) == i)
            def _(i=i):
                x_ref[...] = token_refs[i][...].astype(F32)

        @pl.when(pl.program_id(0) == 3)
        def _():
            x_ref[0] = token_refs[3][0].astype(F32)
            x_ref[1] = token_refs[4][0].astype(F32)

        x = x_ref[...]
        inverse = lax.rsqrt(jnp.mean(x * x, axis=-1, keepdims=True) + EPSILON)
        scaled = x * inverse * gain_ref[0:1][None]
        first_ref[...] = scaled.astype(BF16)
        first = scaled.reshape(2 * rows, width).astype(BF16)
        both = dot(first, w_ref[:, q_width:gains_at], ((1,), (0,)))
        for i in range(2):
            cos, sin = cos_ref[i], sin_ref[i]
            kv = both[i * rows : (i + 1) * rows].T
            for h in range(kv_heads):
                at = h * HEAD_DIM
                if h < KV_HEADS:
                    kv_ref[i, h] = turned(kv, at, cos, sin).astype(BF16)
                else:
                    kv_ref[i, h] = kv[at : at + HEAD_DIM].astype(BF16)

        @pl.when(pl.program_id(0) == 0)
        def _():
            both = dot(first, w_ref[:, :q_width], ((1,), (0,)))
            for i in range(2):
                cos, sin = cos_ref[i], sin_ref[i]
                q = both[i * rows : (i + 1) * rows].T
                for h in range(HEADS):
                    turned_q = turned(q, h * HEAD_DIM, cos, sin).astype(BF16)
                    q_ref[i, h] = (turned_q.astype(F32) * 0.125).astype(BF16)

    table = pl.BlockSpec((2, half, rows), lambda i, s: (i, 0, 0))
    operands = [*tokens, *mine, *other]
    return pl.pallas_call(
        kernel,
        grid_spec=pltpu.PrefetchScalarGridSpec(
            num_scalar_prefetch=1,
            grid=(blocks // 2,),
            in_specs=[fixed(v.shape) for v in operands] + [table, table],
            out_specs=[
                pl.BlockSpec((2, rows, width), lambda i, s: (i, 0, 0)),
                fixed((2, HEADS, HEAD_DIM, rows)),
                pl.BlockSpec((2, kv_heads, HEAD_DIM, rows), lambda i, s: (i, 0, 0, 0)),
                fixed((2 * nz * r, 4 * cols)),
                fixed((8, width)),
            ],
            scratch_shapes=[pltpu.VMEM((2, rows, width), F32)],
        ),
        out_shape=[
            jax.ShapeDtypeStruct((blocks, rows, width), BF16),
            jax.ShapeDtypeStruct((2, HEADS, HEAD_DIM, rows), BF16),
            jax.ShapeDtypeStruct((blocks, kv_heads, HEAD_DIM, rows), BF16),
            jax.ShapeDtypeStruct((2 * nz * r, 4 * cols), BF16),
            jax.ShapeDtypeStruct((8, width), F32),
        ],
        compiler_params=pltpu.CompilerParams(vmem_limit_bytes=VMEM_LIMIT),
        cost_estimate=pl.CostEstimate(
            flops=8_000_000_000, bytes_accessed=25_000_000, transcendentals=0
        ),
    )(jnp.stack([c, f]).astype(jnp.int32), *operands, cosine, sine)


def project_grad(first_all, dq_pieces, dkv_pieces, diagonal):
    _, rows, width = first_all.shape
    q4, kv4 = dq_pieces[0].shape[1], dkv_pieces[0].shape[1]

    def kernel(first_ref, *refs):
        out_ref = refs[-1]
        total = None
        for i in range(8):
            if i < 6:
                turned = jnp.concatenate([refs[i // 2][i % 2], refs[3 + i // 2][i % 2]], axis=0)
            else:
                turned = refs[i][0]
            term = dot(turned, first_ref[i], ((1,), (0,)))
            total = term if total is None else total + term
        out_ref[...] = total.T.astype(BF16)

    operands = [first_all, *dq_pieces, *dkv_pieces, *diagonal]
    return pl.pallas_call(
        kernel,
        grid=(1,),
        in_specs=[fixed(v.shape) for v in operands],
        out_specs=fixed((width, q4 + kv4)),
        out_shape=jax.ShapeDtypeStruct((width, q4 + kv4), BF16),
        compiler_params=pltpu.CompilerParams(vmem_limit_bytes=VMEM_LIMIT),
        cost_estimate=BESIDE,
    )(*operands)


def kernel_specs(blocks, rows):
    q_spec = pl.BlockSpec((2, GROUP, HEAD_DIM, rows), lambda g, *_: (0, g, 0, 0))
    k_spec = pl.BlockSpec((blocks, 1, HEAD_DIM, rows), lambda g, *_: (0, g, 0, 0))
    v_spec = pl.BlockSpec((blocks, 1, HEAD_DIM, rows), lambda g, *_: (0, KV_HEADS + g, 0, 0))
    stat_spec = pl.BlockSpec((2, 1, GROUP, rows), lambda g, *_: (0, g, 0, 0))
    seg_specs = [
        pl.BlockSpec((2, 1, rows), lambda g, *_: (0, 0, 0)),
        pl.BlockSpec((blocks, 1, rows), lambda g, *_: (0, 0, 0)),
        pl.BlockSpec((blocks, 1, rows), lambda g, *_: (0, 0, 0)),
    ]
    return q_spec, k_spec, v_spec, stat_spec, seg_specs


def attention_forward(q_blocks, slots, seg_q, seg_k, valid_k, q_t, kv_t):
    blocks, _, _, rows = kv_t.shape
    q_spec, k_spec, v_spec, stat_spec, seg_specs = kernel_specs(blocks, rows)
    reach = (WINDOW + rows - 2) // rows + 1
    return pl.pallas_call(
        forward_kernel,
        grid_spec=pltpu.PrefetchScalarGridSpec(
            num_scalar_prefetch=2,
            grid=(KV_HEADS,),
            in_specs=seg_specs + [q_spec, k_spec, v_spec],
            out_specs=[q_spec, stat_spec],
            scratch_shapes=[
                pltpu.VMEM((2, reach, rows, rows), F32),
                pltpu.VMEM((reach, GROUP, rows, rows), F32),
                pltpu.VMEM((GROUP, HEAD_DIM, rows), F32),
            ],
        ),
        out_shape=[
            jax.ShapeDtypeStruct(q_t.shape, BF16),
            jax.ShapeDtypeStruct((2, KV_HEADS, GROUP, rows), F32),
        ],
        compiler_params=pltpu.CompilerParams(vmem_limit_bytes=VMEM_LIMIT),
        cost_estimate=pl.CostEstimate(
            flops=20_000_000_000, bytes_accessed=6_000_000, transcendentals=0
        ),
    )(q_blocks, slots, seg_q, seg_k, valid_k, q_t, kv_t, kv_t)


def attention_backward(q_blocks, slots, seg_q, seg_k, valid_k, cos, sin, q_t, kv_t, o_t, do_t, lse):
    blocks, _, _, rows = kv_t.shape
    q_spec, k_spec, v_spec, stat_spec, seg_specs = kernel_specs(blocks, rows)
    reach = (WINDOW + rows - 2) // rows + 1
    table = pl.BlockSpec((2, HEAD_DIM // 2, rows), lambda g, *_: (0, 0, 0))

    def dkv_spec(count):
        return pl.BlockSpec((count, 2, 1, HEAD_DIM, rows), lambda g, *_: (0, 0, g, 0, 0))

    def dkv_shape(count):
        return jax.ShapeDtypeStruct((count, 2, KV_HEADS, HEAD_DIM, rows), BF16)

    return pl.pallas_call(
        backward_kernel,
        grid_spec=pltpu.PrefetchScalarGridSpec(
            num_scalar_prefetch=2,
            grid=(KV_HEADS,),
            in_specs=seg_specs
            + [table, table, q_spec, k_spec, v_spec, q_spec, q_spec, stat_spec],
            out_specs=[q_spec, dkv_spec(2), dkv_spec(2), dkv_spec(4)],
            scratch_shapes=[
                pltpu.VMEM((2, reach, rows, rows), F32),
                pltpu.VMEM((GROUP, HEAD_DIM, rows), F32),
                pltpu.VMEM((GROUP, rows), F32),
                pltpu.VMEM((blocks, HEAD_DIM, rows), F32),
                pltpu.VMEM((blocks, HEAD_DIM, rows), F32),
                pltpu.VMEM((2, GROUP, rows, rows), BF16),
                pltpu.VMEM((2, GROUP, rows, rows), BF16),
            ],
        ),
        out_shape=[
            jax.ShapeDtypeStruct(q_t.shape, BF16),
            dkv_shape(2),
            dkv_shape(2),
            dkv_shape(4),
        ],
        compiler_params=pltpu.CompilerParams(vmem_limit_bytes=VMEM_LIMIT),
        cost_estimate=BESIDE,
    )(q_blocks, slots, seg_q, seg_k, valid_k, cos, sin, q_t, kv_t, kv_t, o_t, do_t, lse)


def feed_forward(x, dy_all, gu_w, down_w, first, held):
    count, rows, width = x.shape
    cut = down_w.shape[0]
    side = rows // 2
    held = () if held is None else tuple(held)

    def kernel(x_ref, dy_ref, gu_ref, down_ref, *refs):
        all_ref, hidden_ref, d_gu_ref, *part_refs = refs[len(held) :]
        x_in = x_ref[0]
        all_ref[0] = x_in
        gu = dot(x_in, gu_ref[...], ((1,), (0,)))
        d_hidden = dot(dy_ref[0], down_ref[...], ((1,), (1,)))
        gate_pre, up_pre = gu[:, :cut], gu[:, cut:]
        sig = jax.nn.sigmoid(gate_pre)
        swish = gate_pre * sig
        slope = sig * (1.0 + gate_pre * (1.0 - sig))
        hidden_ref[0] = (swish * up_pre).astype(BF16)
        d_gu_ref[0, :, :cut] = (d_hidden * up_pre * slope).astype(BF16)
        d_gu_ref[0, :, cut:] = (d_hidden * swish).astype(BF16)
        part = dot(d_gu_ref[0], gu_ref[...], ((1,), (1,)))
        low, high = part[:side].astype(BF16), part[side:].astype(BF16)
        if first == 0:
            part_refs[0][0] = low
            part_refs[0][1] = high
        elif first == 3:
            part_refs[0][0] = low
            part_refs[1][0] = high
        else:
            to_x, to_y, x_high, y_low = part_refs

            @pl.when(pl.program_id(0) == 0)
            def _():
                to_x[0] = low
                x_high[0] = high

            @pl.when(pl.program_id(0) == 1)
            def _():
                y_low[0] = low
                to_y[0] = high

    def block(size):
        return pl.BlockSpec((1, rows, size), lambda i: (first + i, 0, 0))

    def at(index):
        return pl.BlockSpec((1, side, width), lambda i: (index, 0, 0))

    def sums(size):
        return jax.ShapeDtypeStruct((size, side, width), BF16)

    if first == 0:
        part_specs, part_shapes = [fixed((2, side, width))], [sums(2)]
    elif first == 3:
        part_specs, part_shapes = [at(1), at(1)], [sums(2), sums(2)]
    else:
        part_specs, part_shapes = [at(0)] * 4, [sums(2), sums(2), sums(1), sums(1)]
    return pl.pallas_call(
        kernel,
        grid=(count,),
        in_specs=[
            pl.BlockSpec((1, rows, width), lambda i: (i, 0, 0)),
            block(width),
            fixed(gu_w.shape),
            fixed(down_w.shape),
        ]
        + [pl.BlockSpec(memory_space=pl.ANY)] * len(held),
        out_specs=[block(width), block(cut), block(2 * cut)] + part_specs,
        out_shape=[
            jax.ShapeDtypeStruct((4, rows, width), BF16),
            jax.ShapeDtypeStruct((4, rows, cut), BF16),
            jax.ShapeDtypeStruct((4, rows, 2 * cut), BF16),
        ]
        + part_shapes,
        input_output_aliases={4 + i: i for i in range(len(held))},
        compiler_params=pltpu.CompilerParams(vmem_limit_bytes=VMEM_LIMIT),
        cost_estimate=pl.CostEstimate(
            flops=10 * count * rows * width * cut,
            bytes_accessed=2 * (gu_w.size + down_w.size + count * rows * (4 * width + 3 * cut)),
            transcendentals=0,
        ),
    )(x, dy_all, gu_w, down_w, *held)


BESIDE = pl.CostEstimate(flops=0, bytes_accessed=0, transcendentals=0)


def fixed(shape):
    return pl.BlockSpec(shape, lambda *_: (0,) * len(shape))


def transposed_product(left, right, tile):
    depth, rows = left.shape
    cols = right.shape[1]

    def kernel(left_ref, right_ref, out_ref):
        out_ref[...] = dot(left_ref[...], right_ref[...], ((0,), (0,))).astype(BF16)

    return pl.pallas_call(
        kernel,
        grid=(rows // tile,),
        in_specs=[pl.BlockSpec((depth, tile), lambda i: (0, i)), fixed(right.shape)],
        out_specs=pl.BlockSpec((tile, cols), lambda i: (i, 0)),
        out_shape=jax.ShapeDtypeStruct((rows, cols), BF16),
        compiler_params=pltpu.CompilerParams(vmem_limit_bytes=VMEM_LIMIT),
        cost_estimate=BESIDE,
    )(left, right)


def ffn_product(hidden, down_w, side):
    rows, cut = hidden.shape
    width = down_w.shape[1]

    def kernel(left_ref, right_ref, to_x, to_y, keep):
        total = dot(left_ref[...], right_ref[...], ((1,), (0,)))
        low, high = total[:side].astype(BF16), total[side:].astype(BF16)
        places = (
            ((keep, 0), (keep, 1)), ((to_x, 0), (keep, 3)),
            ((keep, 2), (to_y, 0)), ((to_x, 1), (to_y, 1)),
        )
        for i, ((low_ref, low_at), (high_ref, high_at)) in enumerate(places):

            @pl.when(pl.program_id(0) == i)
            def _():
                low_ref[low_at] = low
                high_ref[high_at] = high

    sizes = (2, 2, 4)
    return pl.pallas_call(
        kernel,
        grid=(4,),
        in_specs=[pl.BlockSpec((rows // 4, cut), lambda i: (i, 0)), fixed(down_w.shape)],
        out_specs=[fixed((size, side, width)) for size in sizes],
        out_shape=[jax.ShapeDtypeStruct((size, side, width), BF16) for size in sizes],
        compiler_params=pltpu.CompilerParams(vmem_limit_bytes=VMEM_LIMIT),
        cost_estimate=BESIDE,
    )(hidden, down_w)


def side_product(left_t, right):
    def kernel(left_ref, right_ref, out_ref):
        total = dot(left_ref[0], right_ref[0], ((1,), (0,)))
        out_ref[...] = (total + dot(left_ref[1], right_ref[1], ((1,), (0,)))).astype(BF16)

    shape = (left_t.shape[1], right.shape[2])
    return pl.pallas_call(
        kernel,
        grid=(1,),
        in_specs=[fixed(left_t.shape), fixed(right.shape)],
        out_specs=fixed(shape),
        out_shape=jax.ShapeDtypeStruct(shape, BF16),
        compiler_params=pltpu.CompilerParams(vmem_limit_bytes=VMEM_LIMIT),
        cost_estimate=BESIDE,
    )(left_t, right)


def add_sums(ref, first, sums):
    row = lax.broadcasted_iota(jnp.int32, (8, 128), 0)
    value = jnp.zeros((8, 128), F32)
    for i, v in enumerate(sums):
        value = jnp.where(row == i, v, value)

    @pl.when(first)
    def _():
        ref[...] = jnp.zeros_like(ref)

    ref[...] += value


def side_spec(*shape):
    return pl.BlockSpec((1, *shape), lambda i: (i, 0, 0))


def out_project(tokens, attended_t, weights, gain, live):
    sides, rows, width = tokens.shape

    def kernel(x_ref, att_ref, w_ref, gain_ref, live_ref, middle_ref, second_ref, sums_ref):
        branch = dot(att_ref[0], w_ref[...], ((0,), (0,)))
        middle = x_ref[0].astype(F32) + branch
        middle_ref[0] = middle
        inverse = lax.rsqrt(jnp.mean(middle * middle, axis=-1, keepdims=True) + EPSILON)
        second_ref[0] = (middle * inverse * gain_ref[...]).astype(BF16)
        mask = live_ref[0]
        sums = [jnp.sum(mask * branch * branch), jnp.sum(mask * middle * middle)]
        add_sums(sums_ref, pl.program_id(0) == 0, sums)

    return pl.pallas_call(
        kernel,
        grid=(sides,),
        in_specs=[
            side_spec(rows, width),
            side_spec(width, rows),
            fixed((width, width)),
            fixed((1, width)),
            side_spec(rows, 1),
        ],
        out_specs=[side_spec(rows, width), side_spec(rows, width), fixed((8, 128))],
        out_shape=[
            jax.ShapeDtypeStruct(tokens.shape, F32),
            jax.ShapeDtypeStruct(tokens.shape, BF16),
            jax.ShapeDtypeStruct((8, 128), F32),
        ],
        compiler_params=pltpu.CompilerParams(vmem_limit_bytes=VMEM_LIMIT),
        cost_estimate=BESIDE,
    )(tokens, attended_t, weights, gain, live)


def norm_back(upstream, gain, value):
    inverse = lax.rsqrt(jnp.mean(value * value, axis=-1, keepdims=True) + EPSILON)
    normed = value * inverse
    scaled = upstream * gain
    grad = inverse * (scaled - normed * jnp.mean(scaled * normed, axis=-1, keepdims=True))
    return grad, jnp.sum(upstream * normed, axis=0, keepdims=True)


def add_row(ref, first, row):
    @pl.when(first)
    def _():
        ref[...] = jnp.zeros_like(ref)

    ref[...] += row


def middle_back(d_second, middle, cotangent, gain, weights):
    sides, rows, width = middle.shape

    def kernel(
        low_ref, from_y_ref, high_ref, from_x_ref, m_ref, cot_ref, gain_ref, w_ref,
        gm_ref, branch_ref, do_ref, gain_grad_ref, d_ref,
    ):
        @pl.when(pl.program_id(0) == 0)
        def _():
            d_ref[...] = low_ref[0] + from_y_ref[0].astype(F32)

        @pl.when(pl.program_id(0) == 1)
        def _():
            d_ref[...] = high_ref[0] + from_x_ref[0].astype(F32)

        grad, gain_grad = norm_back(d_ref[...], gain_ref[...], m_ref[0])
        grad_middle = cot_ref[0].astype(F32) + grad
        gm_ref[0] = grad_middle
        d_branch = grad_middle.astype(BF16)
        branch_ref[0] = d_branch
        do_ref[0] = dot(d_branch, w_ref[...], ((1,), (1,))).T.astype(BF16)
        add_row(gain_grad_ref, pl.program_id(0) == 0, gain_grad)

    return pl.pallas_call(
        kernel,
        grid=(sides,),
        in_specs=[fixed((1, rows, width))] * 4
        + [
            side_spec(rows, width),
            side_spec(rows, width),
            fixed((1, width)),
            fixed((width, width)),
        ],
        out_specs=[
            side_spec(rows, width),
            side_spec(rows, width),
            side_spec(width, rows),
            fixed((1, width)),
        ],
        out_shape=[
            jax.ShapeDtypeStruct(middle.shape, F32),
            jax.ShapeDtypeStruct(middle.shape, BF16),
            jax.ShapeDtypeStruct((sides, width, rows), BF16),
            jax.ShapeDtypeStruct((1, width), F32),
        ],
        scratch_shapes=[pltpu.VMEM((rows, width), F32)],
        compiler_params=pltpu.CompilerParams(vmem_limit_bytes=VMEM_LIMIT),
        cost_estimate=BESIDE,
    )(*d_second, middle, cotangent, gain, weights)


def first_back(d_q, d_kv, weights, tokens, grad_middle, gain, live):
    sides, rows, width = tokens.shape
    q_width, kv_width = d_q.shape[1], d_kv.shape[1]

    def kernel(
        dq_ref, dkv_ref, w_ref, x_ref, gm_ref, gain_ref, live_ref, out_ref, gain_grad_ref, sums_ref
    ):
        d_first = dot(dq_ref[0].T, w_ref[:, :q_width], ((1,), (1,)))
        d_first += dot(dkv_ref[0].T, w_ref[:, q_width : q_width + kv_width], ((1,), (1,)))
        grad, gain_grad = norm_back(d_first, gain_ref[...], x_ref[0].astype(F32))
        total = gm_ref[0] + grad
        out_ref[0] = total.astype(BF16)
        add_row(gain_grad_ref, pl.program_id(0) == 0, gain_grad)
        add_sums(sums_ref, pl.program_id(0) == 0, [jnp.sum(live_ref[0] * total * total)])

    return pl.pallas_call(
        kernel,
        grid=(sides,),
        in_specs=[
            side_spec(q_width, rows),
            side_spec(kv_width, rows),
            fixed(weights.shape),
            side_spec(rows, width),
            side_spec(rows, width),
            fixed((1, width)),
            side_spec(rows, 1),
        ],
        out_specs=[side_spec(rows, width), fixed((1, width)), fixed((8, 128))],
        out_shape=[
            jax.ShapeDtypeStruct(tokens.shape, BF16),
            jax.ShapeDtypeStruct((1, width), F32),
            jax.ShapeDtypeStruct((8, 128), F32),
        ],
        compiler_params=pltpu.CompilerParams(vmem_limit_bytes=VMEM_LIMIT),
        cost_estimate=BESIDE,
    )(d_q, d_kv, weights, tokens, grad_middle, gain, live)


def finish(middle, branch_ffn, live, gain_one, gain_two, early_sums, late_sums):
    sides, rows, width = middle.shape

    def kernel(m_ref, f_ref, live_ref, one_ref, two_ref, early_ref, late_ref, out_ref, small_ref):
        result = m_ref[0] + f_ref[0]
        out_ref[0] = result.astype(BF16)
        mask = live_ref[0]
        own = [jnp.sum(mask * result * result), jnp.sum(mask * f_ref[0] * f_ref[0]), jnp.sum(mask)]
        first = pl.program_id(0) == 0
        row = lax.broadcasted_iota(jnp.int32, (8, width), 0)
        value = jnp.where(row == 2, own[0], 0.0)
        value = jnp.where(row == 5, own[1], value)
        value = jnp.where(row == 7, own[2], value)

        @pl.when(first)
        def _():
            start = jnp.where(row == 0, one_ref[...], 0.0)
            start = jnp.where(row == 1, two_ref[...], start)
            start = jnp.where(row == 3, late_ref[0:1, 0:1], start)
            start = jnp.where(row == 4, early_ref[0:1, 0:1], start)
            small_ref[...] = jnp.where(row == 6, early_ref[1:2, 0:1], start)

        small_ref[...] += value

    return pl.pallas_call(
        kernel,
        grid=(sides,),
        in_specs=[
            side_spec(rows, width),
            side_spec(rows, width),
            side_spec(rows, 1),
            fixed((1, width)),
            fixed((1, width)),
            fixed((8, 128)),
            fixed((8, 128)),
        ],
        out_specs=[side_spec(rows, width), fixed((8, width))],
        out_shape=[
            jax.ShapeDtypeStruct(middle.shape, BF16),
            jax.ShapeDtypeStruct((8, width), F32),
        ],
        compiler_params=pltpu.CompilerParams(vmem_limit_bytes=VMEM_LIMIT),
        cost_estimate=BESIDE,
    )(middle, branch_ffn, live, gain_one, gain_two, early_sums, late_sums)


def norm_forward(value_rows, gain):
    inverse = lax.rsqrt(jnp.mean(value_rows * value_rows, axis=-1, keepdims=True) + EPSILON)
    normed = value_rows * inverse
    return (normed * gain, normed, inverse)


def norm_backward(upstream, gain, normed, inverse):
    scaled = upstream * gain
    grad_in = inverse * (scaled - normed * jnp.mean(scaled * normed, axis=-1, keepdims=True))
    return (grad_in, jnp.sum(upstream * normed, axis=0))


def ein(spec, left, right):
    return jnp.einsum(spec, left, right, preferred_element_type=F32)


def turn(v, cosine, sine):
    half = HEAD_DIM // 2
    a, b = v[:, :, :half], v[:, :, half:]
    return jnp.concatenate([a * cosine - b * sine, a * sine + b * cosine], axis=2)


def per_device(
    tokens, cotangent, segments, valid, norm_one, w_query, w_key, w_value, w_out,
    norm_two, w_gate, w_up, w_down,
):
    c = lax.axis_index("ctx")
    n = lax.axis_size("fsdp")
    f = lax.axis_index("fsdp")
    row_count = tokens.shape[1]
    rows = row_count // 2
    width = tokens.shape[2]
    blocks = 8
    q_width, kv_width = w_query.shape[1], w_key.shape[1]
    ff = w_gate.shape[1]
    r = w_query.shape[0]
    c_ref = c.reshape(1).astype(jnp.int32)

    q_blocks = jnp.stack([c, blocks - 1 - c]).astype(jnp.int32)
    seg_blocks = segments[0].reshape(blocks, rows)
    valid_blocks = valid[0].reshape(blocks, rows)
    seg_q = jnp.stack([take(seg_blocks, q_blocks[0], 0), take(seg_blocks, q_blocks[1], 0)])
    live = jnp.stack([take(valid_blocks, q_blocks[0], 0), take(valid_blocks, q_blocks[1], 0)])
    seg_q = seg_q[:, None, :].astype(F32)
    seg_k = seg_blocks[:, None, :].astype(F32)
    valid_k = valid_blocks[:, None, :].astype(F32)
    owners = c ^ jnp.arange(4, dtype=jnp.int32)
    block_of = jnp.stack([owners, blocks - 1 - owners], axis=1)
    every = jnp.arange(blocks, dtype=jnp.int32)
    side = (every >= 4).astype(jnp.int32)
    slots = (c ^ jnp.where(every < 4, every, blocks - 1 - every)) * 2 + side
    slots = slots.astype(jnp.int32)
    places = block_of[:, :, None] * rows + jnp.arange(rows, dtype=jnp.int32)
    half = HEAD_DIM // 2
    freqs = jnp.exp(jnp.arange(half, dtype=F32) * (-math.log(ROPE_BASE) / half))
    angles = places.astype(F32).reshape(8, 1, rows) * freqs[None, :, None]
    cosine, sine = jnp.cos(angles), jnp.sin(angles)

    tokens_own = tokens[0].reshape(2, rows, width)
    tokens_x, tokens_y = swap_x(tokens_own), swap_y(tokens_own)
    gains = jnp.stack([norm_one, norm_two], axis=1)
    gains = jnp.concatenate([gains, jnp.zeros((r, 126), BF16)], axis=1)
    qkv_shard = jnp.concatenate([w_query, w_key, w_value, gains], axis=1)
    c4 = qkv_shard.shape[1] // 4
    qkv_z = z_fetch(lax.dynamic_slice_in_dim(qkv_shard, c * c4, c4, 1))
    d4 = w_down.shape[0] // 4
    down_shard = lax.dynamic_slice_in_dim(w_down, c * d4, d4, 0)
    qkv_z, tokens_x, tokens_y = sync(qkv_z, tokens_x, tokens_y)
    qkv_x, qkv_y = swap_x(qkv_z), swap_y(qkv_z)
    picked = after(pick_columns(c_ref, w_out, w_gate, w_up, n), qkv_z)
    out_gu = lax.all_gather(picked, "fsdp", axis=0, tiled=True)
    down_w = lax.all_gather(after(down_shard, qkv_z), "fsdp", axis=0, tiled=True)
    cut = ff // 4
    live_rows = live.reshape(2, rows, 1).astype(F32)
    qkv_x, qkv_y, tokens_x, tokens_y, cosine, sine, live_rows = sync(
        qkv_x, qkv_y, tokens_x, tokens_y, cosine, sine, live_rows
    )
    zh = qkv_z.shape[0] // 2
    qkv_mine = jnp.stack([qkv_z, qkv_x, qkv_y])
    qkv_d = swap_y(qkv_x[:zh]), swap_x(qkv_y[zh:])
    tokens_d = swap_y(tokens_x[:1]), swap_x(tokens_y[1:])
    qkv_other = core_swap(qkv_mine)
    qkv_d, tokens_d, qkv_other = sync(qkv_d, tokens_d, qkv_other)
    qkv_d = jnp.concatenate(qkv_d)[None]
    qkv_other_d = core_swap(qkv_d)
    dy_own = cotangent[0].reshape(2, rows, width)
    dy_pieces = ctx_fetch_direct(after(dy_own, qkv_other_d))

    first_all, q_t, kv_all, qkv_w, gain_rows = project(
        c,
        f,
        (tokens_own, tokens_x, tokens_y, *tokens_d),
        (qkv_mine, qkv_d),
        (qkv_other, qkv_other_d),
        cosine,
        sine,
        q_width,
    )
    gain_one, gain_two = gain_rows[0:1], gain_rows[1:2]
    first_all = first_all.reshape(4, 2, rows, width)
    o_t, lse = attention_forward(q_blocks, slots, seg_q, seg_k, valid_k, q_t, kv_all)
    o_t, out_gu, dy_pieces, down_w = sync(o_t, out_gu, dy_pieces, down_w)
    dy_all, gu_w = sync(
        jnp.stack(dy_pieces).reshape(4, row_count, width), out_gu[:, width:]
    )
    attended_t = o_t.reshape(2, width, rows)
    middle, x_own, early_sums = out_project(tokens_own, attended_t, out_gu, gain_two, live_rows)

    x_x, x_y = swap_x(x_own), swap_y(x_own)
    held = feed_forward(x_own.reshape(1, row_count, width), dy_all, gu_w, down_w, 0, None)
    x_x, x_y, *held = sync(x_x, x_y, *held)
    own_part = held.pop()
    x_d = jnp.concatenate([swap_y(x_x[:1]), swap_x(x_y[1:])])
    x_xy = jnp.stack([x_x, x_y]).reshape(2, row_count, width)
    held = feed_forward(x_xy, dy_all, gu_w, down_w, 1, held)
    x_d, *held = sync(x_d, *held)
    y_low, x_high = held.pop(), held.pop()
    x_d = x_d.reshape(1, row_count, width)
    *held, to_x, to_y = feed_forward(x_d, dy_all, gu_w, down_w, 3, held)
    got = swap_x(to_x), swap_y(to_y)
    x_all, hidden, d_gu = [v.reshape(4 * row_count, -1) for v in held]
    dy_all = dy_all.reshape(4 * row_count, width)
    grad_gu = transposed_product(x_all, d_gu, 256)
    ffn_parts = ffn_product(after(hidden, grad_gu), down_w, rows)
    got_low, got_high, grad_gu, ffn_parts = sync(*got, grad_gu, ffn_parts)
    got_low, got_high = got_low.astype(F32), got_high.astype(F32)
    low_own = own_part[:1].astype(F32) + got_low[:1]
    high_own = own_part[1:].astype(F32) + got_high[:1]
    from_y = swap_y((y_low.astype(F32) + got_low[1:]).astype(BF16))
    from_x = swap_x((x_high.astype(F32) + got_high[1:]).astype(BF16))
    grad_d = transposed_product(after(hidden, ffn_parts), dy_all, cut)
    d_second = low_own, from_y, high_own, from_x
    d_second, grad_d = sync(d_second, grad_d)
    own_gu = lax.psum_scatter(grad_gu, "fsdp", scatter_dimension=0, tiled=True)
    own_down = lax.psum_scatter(grad_d, "fsdp", scatter_dimension=0, tiled=True)

    k = f % 2
    nz = n // 2
    r4 = r // 4
    grad_middle, d_branch, do_t, grad_gain_two = middle_back(
        d_second, middle, dy_own, gain_two, out_gu
    )
    do_t = do_t.reshape(2, HEADS, HEAD_DIM, rows)
    whole_out = side_product(attended_t, d_branch)
    do_t, ffn_parts, whole_out = sync(do_t, ffn_parts, whole_out)
    ffn_to_x, ffn_to_y, ffn_keep = ffn_parts
    ffn_got = swap_x(ffn_to_x), swap_y(ffn_to_y)
    d_q, dkv_low, dkv_high, dkv_keep = attention_backward(
        q_blocks, slots, seg_q, seg_k, valid_k, cosine[:2], sine[:2], q_t, kv_all, o_t, do_t, lse
    )
    d_q, dkv_low, dkv_high, dkv_keep, ffn_got = sync(d_q, dkv_low, dkv_high, dkv_keep, ffn_got)
    dkv_got = swap_x(dkv_low), swap_y(dkv_high)
    own_out = lax.psum_scatter(
        after(whole_out, dkv_low, own_gu), "fsdp", scatter_dimension=0, tiled=True
    )
    q4, kv4 = q_width // 4, kv_width // 2

    def quarter(v, size, i):
        return lax.dynamic_slice_in_dim(v, (c ^ i) * size, size, 1)

    d_q = d_q.reshape(2, q_width, rows)
    dq_parts = [quarter(d_q, q4, i) for i in range(4)]
    ffn_low, ffn_high = ffn_got[0].astype(F32), ffn_got[1].astype(F32)
    ffn_sums = (
        ffn_keep[:1].astype(F32) + ffn_low[:1],
        ffn_keep[1:2].astype(F32) + ffn_high[:1],
        (ffn_keep[2:3].astype(F32) + ffn_low[1:]).astype(BF16),
        (ffn_keep[3:].astype(F32) + ffn_high[1:]).astype(BF16),
    )
    dkv_got, dq_parts, ffn_sums = sync(dkv_got, dq_parts, ffn_sums)
    kept = dkv_keep.astype(F32)
    low_sums, high_sums = kept[:2] + dkv_got[0].astype(F32), kept[2:] + dkv_got[1].astype(F32)
    from_y, from_x = swap_y(low_sums[1].astype(BF16)), swap_x(high_sums[1].astype(BF16))
    dkv_own = jnp.stack([low_sums[0] + from_y.astype(F32), high_sums[0] + from_x.astype(F32)])
    dkv_own = dkv_own.reshape(2, 2 * KV_HEADS, HEAD_DIM, rows)
    dq_got = exchange_first(dq_parts)
    d_k = turn(dkv_own[:, :KV_HEADS], cosine[:2, None], -sine[:2, None]).astype(BF16)
    d_kv = jnp.concatenate([d_k, dkv_own[:, KV_HEADS:].astype(BF16)], axis=1)
    d_kv = d_kv.reshape(2, 2 * kv_width, rows)
    dkv_parts = [quarter(d_kv, kv4, i) for i in range(4)]
    dkv_got = exchange_first(dkv_parts)
    dq_got, dkv_got, ffn_sums = sync(dq_got, dkv_got, ffn_sums)
    diagonal = (
        swap_y(jnp.concatenate([dq_got[0][2:], dkv_got[0][2:]], axis=1)),
        swap_x(jnp.concatenate([dq_got[1][2:], dkv_got[1][2:]], axis=1)),
    )
    ffn_last = swap_y(ffn_sums[2]), swap_x(ffn_sums[3])
    dq_pieces = [dq_parts[0], *dq_got]
    dkv_pieces = [dkv_parts[0], *dkv_got]
    diagonal, own_out = sync(diagonal, own_out)
    own_out = own_out.reshape(4, r4, width)
    out_parts = [take(own_out, c ^ i, 0) for i in range(4)]
    out_got = scatter_first(out_parts)
    grad_qkv = project_grad(first_all.reshape(8, rows, width), dq_pieces, dkv_pieces, diagonal)
    grad_qkv = grad_qkv.reshape(nz, 2, r, q4 + kv4)
    got_half = core_swap(take(grad_qkv, k ^ 1, 1))
    pair_qkv = (take(grad_qkv, k, 1).astype(F32) + got_half.astype(F32)).astype(BF16)
    pair_qkv, d_q, d_kv, ffn_last, own_gu, out_got = sync(
        pair_qkv, d_q, d_kv, ffn_last, own_gu, out_got
    )
    branch_ffn = jnp.concatenate([v + g.astype(F32) for v, g in zip(ffn_sums[:2], ffn_last)])
    own_qkv = z_scatter(pair_qkv).astype(BF16)

    gu_x, gu_y = swap_x(own_gu), swap_y(own_gu)
    out_sums = scatter_pass(out_parts, out_got)
    grad_tokens, grad_gain_one, late_sums = first_back(
        d_q, d_kv, qkv_w, tokens_own, grad_middle, gain_one, live_rows
    )
    result, small = finish(
        middle, branch_ffn, live_rows, grad_gain_one, grad_gain_two, early_sums, late_sums
    )
    own_qkv, small, gu_x, gu_y, out_sums = sync(own_qkv, small, gu_x, gu_y, out_sums)

    small = small + core_swap(small)
    own_out = scatter_last(*out_sums).astype(BF16)
    qkv_pieces = ctx_fetch_direct(own_qkv)
    small, own_out, gu_x, gu_y = sync(small, own_out, gu_x, gu_y)
    small = z_sum(small)
    hr = gu_x.shape[0] // 2
    gu_d = jnp.concatenate([swap_y(gu_x[:hr]), swap_x(gu_y[hr:])])
    small, own_down, gu_d, own_out = sync(small, own_down, gu_d, own_out)
    small = sum(ctx_fetch_direct(small))
    down_pieces = ctx_fetch_direct(own_down)
    out_pieces = ctx_fetch_direct(own_out)
    grad_q, grad_k, grad_v = join_columns(c_ref, qkv_pieces, q4, kv4)
    grad_gate_w, grad_up_w = unpick_columns(c_ref, [own_gu, gu_x, gu_y, gu_d], n)
    grad_down_w = in_order(down_pieces, 0).reshape(4 * d4, width).astype(F32)
    grad_out_w = in_order(out_pieces, 0).reshape(r, width).astype(F32)
    gain_sums = lax.dynamic_slice_in_dim(small[:2], f * r, r, 1)
    squares = small[2:8, 0]
    spreads = jnp.sqrt(squares[:5] / (squares[5] * width))
    return (
        result.reshape(1, row_count, width),
        grad_tokens.reshape(1, row_count, width),
        gain_sums[0],
        grad_q,
        grad_k,
        grad_v,
        grad_out_w,
        gain_sums[1],
        grad_gate_w,
        grad_up_w,
        grad_down_w,
        spreads,
    )


def solution(mesh):
    rows, shard, vector = P("fsdp", "ctx", None), P("fsdp", None), P("fsdp")
    return jax.shard_map(
        per_device,
        mesh=mesh,
        in_specs=(
            rows, rows, shard, shard, vector, shard, shard, shard, shard, vector,
            shard, shard, shard,
        ),
        out_specs=(
            rows, rows, vector, shard, shard, shard, shard, vector, shard, shard, shard, P(),
        ),
        check_vma=False,
    )
```

```python
import functools
import math

import jax
import jax.numpy as jnp
from jax import lax
from jax.experimental import pallas as pl
from jax.experimental.pallas import tpu as pltpu
from jax.sharding import PartitionSpec as P

HEADS = 20
KV_HEADS = 5
HEAD_DIM = 64
GROUP = HEADS // KV_HEADS
WINDOW = 1024
EPSILON = 1e-05
MASKED = -1e30
ROPE_BASE = 10000.0
VMEM_LIMIT = 60 * 2**20
BF16 = jnp.bfloat16
F32 = jnp.float32


def core_swap(v):
    n = lax.axis_size("fsdp")
    return lax.ppermute(v, "fsdp", [(i, i ^ 1) for i in range(n)])


def swap_x(v):
    return lax.ppermute(v, "ctx", [(i, i ^ 1) for i in range(4)])


def swap_y(v):
    return lax.ppermute(v, "ctx", [(i, i ^ 2) for i in range(4)])


def put(buffer, piece, index, axis):
    return lax.dynamic_update_slice_in_dim(
        buffer, jnp.expand_dims(piece, axis), index, axis
    )


def take(v, index, axis):
    return lax.dynamic_index_in_dim(v, index, axis, keepdims=False)


def place(pieces, axis):
    first = pieces[0][1]
    shape = first.shape[:axis] + (len(pieces),) + first.shape[axis:]
    buffer = jnp.zeros(shape, first.dtype)
    for index, piece in pieces:
        buffer = put(buffer, piece, index, axis)
    return buffer


def z_fetch(piece):
    n = lax.axis_size("fsdp")
    nz = n // 2
    if nz != 4:
        groups = [list(range(0, n, 2)), list(range(1, n, 2))]
        every = lax.all_gather(piece, "fsdp", axis=0, axis_index_groups=groups)
        z = lax.axis_index("fsdp") // 2
        return jnp.take(every, (z - jnp.arange(nz)) % nz, axis=0)
    pieces = [piece]
    for d in (1, 2, 3):
        pieces.append(lax.ppermute(piece, "fsdp", [(i, (i + 2 * d) % n) for i in range(n)]))
    return jnp.stack(pieces)


def z_scatter(pieces):
    n = lax.axis_size("fsdp")
    nz = n // 2
    if nz != 4:
        groups = [list(range(0, n, 2)), list(range(1, n, 2))]
        return lax.psum_scatter(
            pieces, "fsdp", scatter_dimension=0, axis_index_groups=groups
        ).astype(F32)
    z = lax.axis_index("fsdp") // 2
    total = take(pieces, z, 0).astype(F32)
    for d in (1, 2, 3):
        sent = take(pieces, (z + d) % nz, 0)
        got = lax.ppermute(sent, "fsdp", [(i, (i + 2 * d) % n) for i in range(n)])
        total = total + got.astype(F32)
    return total


def sync(*values):
    return lax.optimization_barrier(values)


def ctx_fetch(piece):
    half = piece.shape[0] // 2
    from_x = swap_x(piece)
    from_y = swap_y(piece)
    from_d = jnp.concatenate([swap_y(from_x[:half]), swap_x(from_y[half:])], axis=0)
    return [piece, from_x, from_y, from_d]


def after(v, *earlier):
    return lax.optimization_barrier((v, earlier))[0]


def ctx_fetch_direct(piece):
    diagonal = lax.ppermute(piece, "ctx", [(i, i ^ 3) for i in range(4)])
    return [piece, swap_x(piece), swap_y(piece), diagonal]


def in_order(pieces, axis):
    c = lax.axis_index("ctx")
    return place([(c ^ i, v) for i, v in enumerate(pieces)], axis)


def scatter_first(parts):
    half = parts[0].shape[0] // 2
    low_got = swap_x(jnp.concatenate([parts[1][:half], parts[3][:half]]))
    high_got = swap_y(jnp.concatenate([parts[2][half:], parts[3][half:]]))
    return low_got, high_got


def scatter_pass(parts, got):
    half = parts[0].shape[0] // 2
    rest = parts[0].shape[0] - half
    low_got, high_got = got[0].astype(F32), got[1].astype(F32)
    low_pass = (parts[2][:half].astype(F32) + low_got[half:]).astype(BF16)
    high_pass = (parts[1][half:].astype(F32) + high_got[rest:]).astype(BF16)
    low_own = parts[0][:half].astype(F32) + low_got[:half]
    high_own = parts[0][half:].astype(F32) + high_got[:rest]
    return low_own, high_own, low_pass, high_pass


def scatter_last(low_own, high_own, low_pass, high_pass):
    from_y, from_x = swap_y(low_pass), swap_x(high_pass)
    return jnp.concatenate([low_own + from_y.astype(F32), high_own + from_x.astype(F32)])


def exchange_first(parts):
    to_x = jnp.concatenate([parts[1], parts[3][:1]], axis=0)
    to_y = jnp.concatenate([parts[2], parts[3][1:]], axis=0)
    return swap_x(to_x), swap_y(to_y)


def z_sum(v):
    n = lax.axis_size("fsdp")
    if n == 8:
        return v + sum(
            lax.ppermute(v, "fsdp", [(i, (i + 2 * d) % n) for i in range(n)]) for d in (1, 2, 3)
        )
    bit = 2
    while bit < n:
        v = v + lax.ppermute(v, "fsdp", [(i, i ^ bit) for i in range(n)])
        bit *= 2
    return v


def pick_columns(c, out, gate, up, count):
    r, ff = gate.shape
    width = out.shape[1]
    group = ff // count
    strip = group // 4

    def kernel(c_ref, w_ref, gate_ref, up_ref, out_ref):
        out_ref[:, :width] = w_ref[...]
        for own in range(4):

            @pl.when(c_ref[0] == own)
            def _():
                for j in range(count):
                    at = j * group + own * strip
                    to = width + j * strip
                    out_ref[:, to : to + strip] = gate_ref[:, at : at + strip]
                    to += ff // 4
                    out_ref[:, to : to + strip] = up_ref[:, at : at + strip]

    whole = pl.BlockSpec((r, ff), lambda i, s: (0, 0))
    return pl.pallas_call(
        kernel,
        grid_spec=pltpu.PrefetchScalarGridSpec(
            num_scalar_prefetch=1,
            grid=(1,),
            in_specs=[pl.BlockSpec((r, width), lambda i, s: (0, 0)), whole, whole],
            out_specs=pl.BlockSpec((r, width + ff // 2), lambda i, s: (0, 0)),
        ),
        out_shape=jax.ShapeDtypeStruct((r, width + ff // 2), BF16),
        cost_estimate=pl.CostEstimate(flops=0, bytes_accessed=6 * r * ff, transcendentals=0),
    )(c, out, gate, up)


def unpick_columns(c, pieces, count):
    r, half = pieces[0].shape
    ff = 2 * half
    group = ff // count
    strip = group // 4

    def kernel(c_ref, *refs):
        gate_ref, up_ref = refs[4:]
        for own in range(4):

            @pl.when(c_ref[0] == own)
            def _():
                for step in range(4):
                    for j in range(count):
                        at = j * group + (own ^ step) * strip
                        piece = refs[step]
                        gate_ref[:, at : at + strip] = piece[
                            :, j * strip : (j + 1) * strip
                        ].astype(F32)
                        frm = ff // 4 + j * strip
                        up_ref[:, at : at + strip] = piece[:, frm : frm + strip].astype(F32)

    whole = pl.BlockSpec((r, ff), lambda i, s: (0, 0))
    return pl.pallas_call(
        kernel,
        grid_spec=pltpu.PrefetchScalarGridSpec(
            num_scalar_prefetch=1,
            grid=(1,),
            in_specs=[pl.BlockSpec((r, half), lambda i, s: (0, 0))] * 4,
            out_specs=[whole, whole],
        ),
        out_shape=[jax.ShapeDtypeStruct((r, ff), F32)] * 2,
        compiler_params=pltpu.CompilerParams(vmem_limit_bytes=VMEM_LIMIT),
        cost_estimate=pl.CostEstimate(flops=0, bytes_accessed=12 * r * ff, transcendentals=0),
    )(c, *pieces)


def join_columns(c, pieces, q4, kv4):
    r = pieces[0].shape[0]

    def kernel(c_ref, *refs):
        q_ref, k_ref, v_ref = refs[4:]
        for own in range(4):

            @pl.when(c_ref[0] == own)
            def _():
                for step in range(4):
                    to = own ^ step
                    piece = refs[step][...].astype(F32)
                    q_ref[:, to * q4 : (to + 1) * q4] = piece[:, :q4]
                    target = k_ref if to < 2 else v_ref
                    at = (to % 2) * kv4
                    target[:, at : at + kv4] = piece[:, q4:]

    def whole(cols):
        return pl.BlockSpec((r, cols), lambda i, s: (0, 0))

    return pl.pallas_call(
        kernel,
        grid_spec=pltpu.PrefetchScalarGridSpec(
            num_scalar_prefetch=1,
            grid=(1,),
            in_specs=[whole(q4 + kv4)] * 4,
            out_specs=[whole(4 * q4), whole(2 * kv4), whole(2 * kv4)],
        ),
        out_shape=[
            jax.ShapeDtypeStruct((r, cols), F32) for cols in (4 * q4, 2 * kv4, 2 * kv4)
        ],
        cost_estimate=pl.CostEstimate(
            flops=0, bytes_accessed=24 * r * (q4 + kv4), transcendentals=0
        ),
    )(c, *pieces)


def pair_bias(q_block, k_block, rows, seg_q, seg_k, valid_k):
    key_at = k_block * rows + lax.broadcasted_iota(jnp.int32, (rows, rows), 0)
    query_at = q_block * rows + lax.broadcasted_iota(jnp.int32, (rows, rows), 1)
    distance = query_at - key_at
    allowed = (
        (seg_q == seg_k)
        & (distance >= 0)
        & (distance < WINDOW)
        & ((valid_k == 1.0) | (distance == 0))
    )
    return jnp.where(allowed, 0.0, MASKED).astype(F32)


def first_block(q_block, rows):
    reach = (WINDOW + rows - 2) // rows
    return jnp.maximum(q_block - reach, 0)


def dot(a, b, dims):
    return lax.dot_general(a, b, (dims, ((), ())), preferred_element_type=F32)


def column(row):
    size = row.shape[1]
    return jnp.broadcast_to(row, (size, size)).T


def fill_bias(blocks_ref, seg_q_ref, seg_k_ref, valid_k_ref, bias_ref, rows):
    for side in range(2):
        b = blocks_ref[side]
        lo = first_block(b, rows)

        def body(kb, _):
            bias_ref[side, kb - lo] = pair_bias(
                b, kb, rows, seg_q_ref[side], column(seg_k_ref[kb]), column(valid_k_ref[kb])
            )
            return 0

        lax.fori_loop(lo, b + 1, body, 0)


def forward_kernel(
    blocks_ref, slots_ref, seg_q_ref, seg_k_ref, valid_k_ref, q_ref, k_ref, v_ref,
    o_ref, lse_ref, bias_ref, scores_ref, acc_ref,
):
    rows = q_ref.shape[-1]

    @pl.when(pl.program_id(0) == 0)
    def _():
        fill_bias(blocks_ref, seg_q_ref, seg_k_ref, valid_k_ref, bias_ref, rows)

    for side in range(2):
        b = blocks_ref[side]
        lo = first_block(b, rows)

        def score(kb, peaks):
            keys = k_ref[slots_ref[kb], 0].T
            bias = bias_ref[side, kb - lo]
            higher = []
            for h in range(GROUP):
                s = dot(keys, q_ref[side, h], ((1,), (0,))) + bias
                scores_ref[kb - lo, h] = s
                higher.append(jnp.maximum(peaks[h], jnp.max(s, axis=0, keepdims=True)))
            return tuple(higher)

        peaks = lax.fori_loop(
            lo, b + 1, score, (jnp.full((1, rows), -jnp.inf, F32),) * GROUP
        )
        acc_ref[...] = jnp.zeros_like(acc_ref)

        def mix(kb, totals):
            values_t = v_ref[slots_ref[kb], 0]
            more = []
            for h in range(GROUP):
                p = jnp.exp(scores_ref[kb - lo, h] - peaks[h])
                more.append(totals[h] + jnp.sum(p, axis=0, keepdims=True))
                acc_ref[h] += dot(values_t, p.astype(BF16), ((1,), (0,)))
            return tuple(more)

        totals = lax.fori_loop(lo, b + 1, mix, (jnp.zeros((1, rows), F32),) * GROUP)
        for h in range(GROUP):
            o_ref[side, h] = (acc_ref[h] / totals[h]).astype(BF16)
            lse_ref[side, 0, h : h + 1] = peaks[h] + jnp.log(totals[h])


def backward_kernel(
    blocks_ref, slots_ref, seg_q_ref, seg_k_ref, valid_k_ref, cos_ref, sin_ref, q_ref, k_ref, v_ref,
    o_ref, do_ref, lse_ref,
    dq_ref, low_ref, high_ref, keep_ref,
    bias_ref, acc_ref, center_ref, dk_ref, dv_ref, p_ref, ds_ref,
):
    rows = q_ref.shape[-1]
    half = HEAD_DIM // 2

    @pl.when(pl.program_id(0) == 0)
    def _():
        fill_bias(blocks_ref, seg_q_ref, seg_k_ref, valid_k_ref, bias_ref, rows)

    dk_ref[...] = jnp.zeros_like(dk_ref)
    dv_ref[...] = jnp.zeros_like(dv_ref)
    for side in range(2):
        b = blocks_ref[side]
        lo = first_block(b, rows)
        acc_ref[...] = jnp.zeros_like(acc_ref)
        for h in range(GROUP):
            center_ref[h : h + 1] = jnp.sum(
                o_ref[side, h].astype(F32) * do_ref[side, h].astype(F32), axis=0, keepdims=True
            )

        def soft(kb, at):
            slot = slots_ref[kb]
            keys = k_ref[slot, 0].T
            values = v_ref[slot, 0].T
            bias = bias_ref[side, kb - lo]
            for h in range(GROUP):
                s = dot(keys, q_ref[side, h], ((1,), (0,))) + bias
                p = jnp.exp(s - lse_ref[side, 0, h : h + 1])
                dp = dot(values, do_ref[side, h], ((1,), (0,)))
                p_ref[at, h] = p.astype(BF16)
                ds_ref[at, h] = (p * (dp - center_ref[h : h + 1])).astype(BF16)

        def products(kb, at):
            slot = slots_ref[kb]
            dv = dot(do_ref[side, 0], p_ref[at, 0], ((1,), (1,)))
            dk = dot(q_ref[side, 0], ds_ref[at, 0], ((1,), (1,)))
            for h in range(1, GROUP):
                dv += dot(do_ref[side, h], p_ref[at, h], ((1,), (1,)))
                dk += dot(q_ref[side, h], ds_ref[at, h], ((1,), (1,)))
            dv_ref[slot] += dv
            dk_ref[slot] += dk
            for h in range(GROUP):
                acc_ref[h] += dot(k_ref[slot, 0], ds_ref[at, h], ((1,), (0,)))

        soft(lo, 0)

        def body(kb, _):
            products(kb - 1, (kb - 1 - lo) % 2)
            soft(kb, (kb - lo) % 2)
            return 0

        lax.fori_loop(lo + 1, b + 1, body, 0)
        products(b, (b - lo) % 2)
        cos, sin = cos_ref[side], sin_ref[side]
        for h in range(GROUP):
            a, b2 = acc_ref[h, :half] * 0.125, acc_ref[h, half:] * 0.125
            turned = jnp.concatenate([a * cos + b2 * sin, b2 * cos - a * sin], axis=0)
            dq_ref[side, h] = turned.astype(BF16)
    for target, slots in ((low_ref, (2, 6)), (high_ref, (5, 7)), (keep_ref, (0, 4, 1, 3))):
        for i, slot in enumerate(slots):
            target[i, 0, 0] = dk_ref[slot].astype(BF16)
            target[i, 1, 0] = dv_ref[slot].astype(BF16)


def project(c, f, tokens, mine, other, cosine, sine, q_width):
    _, rows, width = tokens[0].shape
    blocks = 8
    _, nz, r, cols = mine[0].shape
    half = HEAD_DIM // 2
    kv_heads = 2 * KV_HEADS
    gains_at = q_width + kv_heads * HEAD_DIM

    def turned(flat_t, at, cos, sin):
        a, b = flat_t[at : at + half], flat_t[at + half : at + HEAD_DIM]
        return jnp.concatenate([a * cos - b * sin, a * sin + b * cos], axis=0)

    def kernel(at_ref, *refs):
        token_refs, mine_refs, other_refs = refs[:5], refs[5:7], refs[7:9]
        cos_ref, sin_ref, first_ref, q_ref, kv_ref, w_ref, gain_ref, x_ref = refs[9:]

        @pl.when(pl.program_id(0) == 0)
        def _():
            for core in range(2):
                for q in range(4):
                    step = q ^ at_ref[0]

                    def fill(index, which, core=core, q=q):
                        for z in range(nz):
                            z_step = (at_ref[1] // 2 - z + nz) % nz
                            for kk in range(2):
                                source = mine_refs if kk == core else other_refs
                                at = (2 * z + kk) * r
                                w_ref[at : at + r, q * cols : (q + 1) * cols] = source[which][
                                    index, z_step
                                ]

                    @pl.when((at_ref[1] % 2 == core) & (step < 3))
                    def _(step=step, fill=fill):
                        fill(step, 0)

                    @pl.when((at_ref[1] % 2 == core) & (step == 3))
                    def _(fill=fill):
                        fill(0, 1)

            gain_ref[...] = w_ref[:, gains_at:].astype(F32).T[:8]

        for i in range(3):

            @pl.when(pl.program_id(0) == i)
            def _(i=i):
                x_ref[...] = token_refs[i][...].astype(F32)

        @pl.when(pl.program_id(0) == 3)
        def _():
            x_ref[0] = token_refs[3][0].astype(F32)
            x_ref[1] = token_refs[4][0].astype(F32)

        x = x_ref[...]
        inverse = lax.rsqrt(jnp.mean(x * x, axis=-1, keepdims=True) + EPSILON)
        scaled = x * inverse * gain_ref[0:1][None]
        first_ref[...] = scaled.astype(BF16)
        first = scaled.reshape(2 * rows, width).astype(BF16)
        both = dot(first, w_ref[:, q_width:gains_at], ((1,), (0,)))
        for i in range(2):
            cos, sin = cos_ref[i], sin_ref[i]
            kv = both[i * rows : (i + 1) * rows].T
            for h in range(kv_heads):
                at = h * HEAD_DIM
                if h < KV_HEADS:
                    kv_ref[i, h] = turned(kv, at, cos, sin).astype(BF16)
                else:
                    kv_ref[i, h] = kv[at : at + HEAD_DIM].astype(BF16)

        @pl.when(pl.program_id(0) == 0)
        def _():
            both = dot(first, w_ref[:, :q_width], ((1,), (0,)))
            for i in range(2):
                cos, sin = cos_ref[i], sin_ref[i]
                q = both[i * rows : (i + 1) * rows].T
                for h in range(HEADS):
                    turned_q = turned(q, h * HEAD_DIM, cos, sin).astype(BF16)
                    q_ref[i, h] = (turned_q.astype(F32) * 0.125).astype(BF16)

    table = pl.BlockSpec((2, half, rows), lambda i, s: (i, 0, 0))
    operands = [*tokens, *mine, *other]
    return pl.pallas_call(
        kernel,
        grid_spec=pltpu.PrefetchScalarGridSpec(
            num_scalar_prefetch=1,
            grid=(blocks // 2,),
            in_specs=[fixed(v.shape) for v in operands] + [table, table],
            out_specs=[
                pl.BlockSpec((2, rows, width), lambda i, s: (i, 0, 0)),
                fixed((2, HEADS, HEAD_DIM, rows)),
                pl.BlockSpec((2, kv_heads, HEAD_DIM, rows), lambda i, s: (i, 0, 0, 0)),
                fixed((2 * nz * r, 4 * cols)),
                fixed((8, width)),
            ],
            scratch_shapes=[pltpu.VMEM((2, rows, width), F32)],
        ),
        out_shape=[
            jax.ShapeDtypeStruct((blocks, rows, width), BF16),
            jax.ShapeDtypeStruct((2, HEADS, HEAD_DIM, rows), BF16),
            jax.ShapeDtypeStruct((blocks, kv_heads, HEAD_DIM, rows), BF16),
            jax.ShapeDtypeStruct((2 * nz * r, 4 * cols), BF16),
            jax.ShapeDtypeStruct((8, width), F32),
        ],
        compiler_params=pltpu.CompilerParams(vmem_limit_bytes=VMEM_LIMIT),
        cost_estimate=pl.CostEstimate(
            flops=8_000_000_000, bytes_accessed=25_000_000, transcendentals=0
        ),
    )(jnp.stack([c, f]).astype(jnp.int32), *operands, cosine, sine)


def project_grad(first_all, dq_pieces, dkv_pieces, diagonal):
    _, rows, width = first_all.shape
    q4, kv4 = dq_pieces[0].shape[1], dkv_pieces[0].shape[1]

    def kernel(first_ref, *refs):
        out_ref = refs[-1]
        total = None
        for i in range(8):
            if i < 6:
                turned = jnp.concatenate([refs[i // 2][i % 2], refs[3 + i // 2][i % 2]], axis=0)
            else:
                turned = refs[i][0]
            term = dot(turned, first_ref[i], ((1,), (0,)))
            total = term if total is None else total + term
        out_ref[...] = total.T.astype(BF16)

    operands = [first_all, *dq_pieces, *dkv_pieces, *diagonal]
    return pl.pallas_call(
        kernel,
        grid=(1,),
        in_specs=[fixed(v.shape) for v in operands],
        out_specs=fixed((width, q4 + kv4)),
        out_shape=jax.ShapeDtypeStruct((width, q4 + kv4), BF16),
        compiler_params=pltpu.CompilerParams(vmem_limit_bytes=VMEM_LIMIT),
        cost_estimate=BESIDE,
    )(*operands)


def kernel_specs(blocks, rows):
    q_spec = pl.BlockSpec((2, GROUP, HEAD_DIM, rows), lambda g, *_: (0, g, 0, 0))
    k_spec = pl.BlockSpec((blocks, 1, HEAD_DIM, rows), lambda g, *_: (0, g, 0, 0))
    v_spec = pl.BlockSpec((blocks, 1, HEAD_DIM, rows), lambda g, *_: (0, KV_HEADS + g, 0, 0))
    stat_spec = pl.BlockSpec((2, 1, GROUP, rows), lambda g, *_: (0, g, 0, 0))
    seg_specs = [
        pl.BlockSpec((2, 1, rows), lambda g, *_: (0, 0, 0)),
        pl.BlockSpec((blocks, 1, rows), lambda g, *_: (0, 0, 0)),
        pl.BlockSpec((blocks, 1, rows), lambda g, *_: (0, 0, 0)),
    ]
    return q_spec, k_spec, v_spec, stat_spec, seg_specs


def attention_forward(q_blocks, slots, seg_q, seg_k, valid_k, q_t, kv_t):
    blocks, _, _, rows = kv_t.shape
    q_spec, k_spec, v_spec, stat_spec, seg_specs = kernel_specs(blocks, rows)
    reach = (WINDOW + rows - 2) // rows + 1
    return pl.pallas_call(
        forward_kernel,
        grid_spec=pltpu.PrefetchScalarGridSpec(
            num_scalar_prefetch=2,
            grid=(KV_HEADS,),
            in_specs=seg_specs + [q_spec, k_spec, v_spec],
            out_specs=[q_spec, stat_spec],
            scratch_shapes=[
                pltpu.VMEM((2, reach, rows, rows), F32),
                pltpu.VMEM((reach, GROUP, rows, rows), F32),
                pltpu.VMEM((GROUP, HEAD_DIM, rows), F32),
            ],
        ),
        out_shape=[
            jax.ShapeDtypeStruct(q_t.shape, BF16),
            jax.ShapeDtypeStruct((2, KV_HEADS, GROUP, rows), F32),
        ],
        compiler_params=pltpu.CompilerParams(vmem_limit_bytes=VMEM_LIMIT),
        cost_estimate=pl.CostEstimate(
            flops=20_000_000_000, bytes_accessed=6_000_000, transcendentals=0
        ),
    )(q_blocks, slots, seg_q, seg_k, valid_k, q_t, kv_t, kv_t)


def attention_backward(q_blocks, slots, seg_q, seg_k, valid_k, cos, sin, q_t, kv_t, o_t, do_t, lse):
    blocks, _, _, rows = kv_t.shape
    q_spec, k_spec, v_spec, stat_spec, seg_specs = kernel_specs(blocks, rows)
    reach = (WINDOW + rows - 2) // rows + 1
    table = pl.BlockSpec((2, HEAD_DIM // 2, rows), lambda g, *_: (0, 0, 0))

    def dkv_spec(count):
        return pl.BlockSpec((count, 2, 1, HEAD_DIM, rows), lambda g, *_: (0, 0, g, 0, 0))

    def dkv_shape(count):
        return jax.ShapeDtypeStruct((count, 2, KV_HEADS, HEAD_DIM, rows), BF16)

    return pl.pallas_call(
        backward_kernel,
        grid_spec=pltpu.PrefetchScalarGridSpec(
            num_scalar_prefetch=2,
            grid=(KV_HEADS,),
            in_specs=seg_specs
            + [table, table, q_spec, k_spec, v_spec, q_spec, q_spec, stat_spec],
            out_specs=[q_spec, dkv_spec(2), dkv_spec(2), dkv_spec(4)],
            scratch_shapes=[
                pltpu.VMEM((2, reach, rows, rows), F32),
                pltpu.VMEM((GROUP, HEAD_DIM, rows), F32),
                pltpu.VMEM((GROUP, rows), F32),
                pltpu.VMEM((blocks, HEAD_DIM, rows), F32),
                pltpu.VMEM((blocks, HEAD_DIM, rows), F32),
                pltpu.VMEM((2, GROUP, rows, rows), BF16),
                pltpu.VMEM((2, GROUP, rows, rows), BF16),
            ],
        ),
        out_shape=[
            jax.ShapeDtypeStruct(q_t.shape, BF16),
            dkv_shape(2),
            dkv_shape(2),
            dkv_shape(4),
        ],
        compiler_params=pltpu.CompilerParams(vmem_limit_bytes=VMEM_LIMIT),
        cost_estimate=BESIDE,
    )(q_blocks, slots, seg_q, seg_k, valid_k, cos, sin, q_t, kv_t, kv_t, o_t, do_t, lse)


def feed_forward(x, dy_all, gu_w, down_w, first, held):
    count, rows, width = x.shape
    cut = down_w.shape[0]
    side = rows // 2
    held = () if held is None else tuple(held)

    def kernel(x_ref, dy_ref, gu_ref, down_ref, *refs):
        all_ref, hidden_ref, d_gu_ref, *part_refs = refs[len(held) :]
        x_in = x_ref[0]
        all_ref[0] = x_in
        gu = dot(x_in, gu_ref[...], ((1,), (0,)))
        d_hidden = dot(dy_ref[0], down_ref[...], ((1,), (1,)))
        gate_pre, up_pre = gu[:, :cut], gu[:, cut:]
        sig = jax.nn.sigmoid(gate_pre)
        swish = gate_pre * sig
        slope = sig * (1.0 + gate_pre * (1.0 - sig))
        hidden_ref[0] = (swish * up_pre).astype(BF16)
        d_gu_ref[0, :, :cut] = (d_hidden * up_pre * slope).astype(BF16)
        d_gu_ref[0, :, cut:] = (d_hidden * swish).astype(BF16)
        part = dot(d_gu_ref[0], gu_ref[...], ((1,), (1,)))
        low, high = part[:side].astype(BF16), part[side:].astype(BF16)
        if first == 0:
            part_refs[0][0] = low
            part_refs[0][1] = high
        elif first == 3:
            part_refs[0][0] = low
            part_refs[1][0] = high
        else:
            to_x, to_y, x_high, y_low = part_refs

            @pl.when(pl.program_id(0) == 0)
            def _():
                to_x[0] = low
                x_high[0] = high

            @pl.when(pl.program_id(0) == 1)
            def _():
                y_low[0] = low
                to_y[0] = high

    def block(size):
        return pl.BlockSpec((1, rows, size), lambda i: (first + i, 0, 0))

    def at(index):
        return pl.BlockSpec((1, side, width), lambda i: (index, 0, 0))

    def sums(size):
        return jax.ShapeDtypeStruct((size, side, width), BF16)

    if first == 0:
        part_specs, part_shapes = [fixed((2, side, width))], [sums(2)]
    elif first == 3:
        part_specs, part_shapes = [at(1), at(1)], [sums(2), sums(2)]
    else:
        part_specs, part_shapes = [at(0)] * 4, [sums(2), sums(2), sums(1), sums(1)]
    return pl.pallas_call(
        kernel,
        grid=(count,),
        in_specs=[
            pl.BlockSpec((1, rows, width), lambda i: (i, 0, 0)),
            block(width),
            fixed(gu_w.shape),
            fixed(down_w.shape),
        ]
        + [pl.BlockSpec(memory_space=pl.ANY)] * len(held),
        out_specs=[block(width), block(cut), block(2 * cut)] + part_specs,
        out_shape=[
            jax.ShapeDtypeStruct((4, rows, width), BF16),
            jax.ShapeDtypeStruct((4, rows, cut), BF16),
            jax.ShapeDtypeStruct((4, rows, 2 * cut), BF16),
        ]
        + part_shapes,
        input_output_aliases={4 + i: i for i in range(len(held))},
        compiler_params=pltpu.CompilerParams(vmem_limit_bytes=VMEM_LIMIT),
        cost_estimate=pl.CostEstimate(
            flops=10 * count * rows * width * cut,
            bytes_accessed=2 * (gu_w.size + down_w.size + count * rows * (4 * width + 3 * cut)),
            transcendentals=0,
        ),
    )(x, dy_all, gu_w, down_w, *held)


BESIDE = pl.CostEstimate(flops=0, bytes_accessed=0, transcendentals=0)


def fixed(shape):
    return pl.BlockSpec(shape, lambda *_: (0,) * len(shape))


def transposed_product(left, right, tile):
    depth, rows = left.shape
    cols = right.shape[1]

    def kernel(left_ref, right_ref, out_ref):
        out_ref[...] = dot(left_ref[...], right_ref[...], ((0,), (0,))).astype(BF16)

    return pl.pallas_call(
        kernel,
        grid=(rows // tile,),
        in_specs=[pl.BlockSpec((depth, tile), lambda i: (0, i)), fixed(right.shape)],
        out_specs=pl.BlockSpec((tile, cols), lambda i: (i, 0)),
        out_shape=jax.ShapeDtypeStruct((rows, cols), BF16),
        compiler_params=pltpu.CompilerParams(vmem_limit_bytes=VMEM_LIMIT),
        cost_estimate=BESIDE,
    )(left, right)


def ffn_product(hidden, down_w, side):
    rows, cut = hidden.shape
    width = down_w.shape[1]

    def kernel(left_ref, right_ref, to_x, to_y, keep):
        total = dot(left_ref[...], right_ref[...], ((1,), (0,)))
        low, high = total[:side].astype(BF16), total[side:].astype(BF16)
        places = (
            ((keep, 0), (keep, 1)), ((to_x, 0), (keep, 3)),
            ((keep, 2), (to_y, 0)), ((to_x, 1), (to_y, 1)),
        )
        for i, ((low_ref, low_at), (high_ref, high_at)) in enumerate(places):

            @pl.when(pl.program_id(0) == i)
            def _():
                low_ref[low_at] = low
                high_ref[high_at] = high

    sizes = (2, 2, 4)
    return pl.pallas_call(
        kernel,
        grid=(4,),
        in_specs=[pl.BlockSpec((rows // 4, cut), lambda i: (i, 0)), fixed(down_w.shape)],
        out_specs=[fixed((size, side, width)) for size in sizes],
        out_shape=[jax.ShapeDtypeStruct((size, side, width), BF16) for size in sizes],
        compiler_params=pltpu.CompilerParams(vmem_limit_bytes=VMEM_LIMIT),
        cost_estimate=BESIDE,
    )(hidden, down_w)


def side_product(left_t, right):
    def kernel(left_ref, right_ref, out_ref):
        total = dot(left_ref[0], right_ref[0], ((1,), (0,)))
        out_ref[...] = (total + dot(left_ref[1], right_ref[1], ((1,), (0,)))).astype(BF16)

    shape = (left_t.shape[1], right.shape[2])
    return pl.pallas_call(
        kernel,
        grid=(1,),
        in_specs=[fixed(left_t.shape), fixed(right.shape)],
        out_specs=fixed(shape),
        out_shape=jax.ShapeDtypeStruct(shape, BF16),
        compiler_params=pltpu.CompilerParams(vmem_limit_bytes=VMEM_LIMIT),
        cost_estimate=BESIDE,
    )(left_t, right)


def add_sums(ref, first, sums):
    row = lax.broadcasted_iota(jnp.int32, (8, 128), 0)
    value = jnp.zeros((8, 128), F32)
    for i, v in enumerate(sums):
        value = jnp.where(row == i, v, value)

    @pl.when(first)
    def _():
        ref[...] = jnp.zeros_like(ref)

    ref[...] += value


def side_spec(*shape):
    return pl.BlockSpec((1, *shape), lambda i: (i, 0, 0))


def out_project(tokens, attended_t, weights, gain, live):
    sides, rows, width = tokens.shape

    def kernel(x_ref, att_ref, w_ref, gain_ref, live_ref, middle_ref, second_ref, sums_ref):
        branch = dot(att_ref[0], w_ref[...], ((0,), (0,)))
        middle = x_ref[0].astype(F32) + branch
        middle_ref[0] = middle
        inverse = lax.rsqrt(jnp.mean(middle * middle, axis=-1, keepdims=True) + EPSILON)
        second_ref[0] = (middle * inverse * gain_ref[...]).astype(BF16)
        mask = live_ref[0]
        sums = [jnp.sum(mask * branch * branch), jnp.sum(mask * middle * middle)]
        add_sums(sums_ref, pl.program_id(0) == 0, sums)

    return pl.pallas_call(
        kernel,
        grid=(sides,),
        in_specs=[
            side_spec(rows, width),
            side_spec(width, rows),
            fixed((width, width)),
            fixed((1, width)),
            side_spec(rows, 1),
        ],
        out_specs=[side_spec(rows, width), side_spec(rows, width), fixed((8, 128))],
        out_shape=[
            jax.ShapeDtypeStruct(tokens.shape, F32),
            jax.ShapeDtypeStruct(tokens.shape, BF16),
            jax.ShapeDtypeStruct((8, 128), F32),
        ],
        compiler_params=pltpu.CompilerParams(vmem_limit_bytes=VMEM_LIMIT),
        cost_estimate=BESIDE,
    )(tokens, attended_t, weights, gain, live)


def norm_back(upstream, gain, value):
    inverse = lax.rsqrt(jnp.mean(value * value, axis=-1, keepdims=True) + EPSILON)
    normed = value * inverse
    scaled = upstream * gain
    grad = inverse * (scaled - normed * jnp.mean(scaled * normed, axis=-1, keepdims=True))
    return grad, jnp.sum(upstream * normed, axis=0, keepdims=True)


def add_row(ref, first, row):
    @pl.when(first)
    def _():
        ref[...] = jnp.zeros_like(ref)

    ref[...] += row


def middle_back(d_second, middle, cotangent, gain, weights):
    sides, rows, width = middle.shape

    def kernel(
        low_ref, from_y_ref, high_ref, from_x_ref, m_ref, cot_ref, gain_ref, w_ref,
        gm_ref, branch_ref, do_ref, gain_grad_ref, d_ref,
    ):
        @pl.when(pl.program_id(0) == 0)
        def _():
            d_ref[...] = low_ref[0] + from_y_ref[0].astype(F32)

        @pl.when(pl.program_id(0) == 1)
        def _():
            d_ref[...] = high_ref[0] + from_x_ref[0].astype(F32)

        grad, gain_grad = norm_back(d_ref[...], gain_ref[...], m_ref[0])
        grad_middle = cot_ref[0].astype(F32) + grad
        gm_ref[0] = grad_middle
        d_branch = grad_middle.astype(BF16)
        branch_ref[0] = d_branch
        do_ref[0] = dot(d_branch, w_ref[...], ((1,), (1,))).T.astype(BF16)
        add_row(gain_grad_ref, pl.program_id(0) == 0, gain_grad)

    return pl.pallas_call(
        kernel,
        grid=(sides,),
        in_specs=[fixed((1, rows, width))] * 4
        + [
            side_spec(rows, width),
            side_spec(rows, width),
            fixed((1, width)),
            fixed((width, width)),
        ],
        out_specs=[
            side_spec(rows, width),
            side_spec(rows, width),
            side_spec(width, rows),
            fixed((1, width)),
        ],
        out_shape=[
            jax.ShapeDtypeStruct(middle.shape, F32),
            jax.ShapeDtypeStruct(middle.shape, BF16),
            jax.ShapeDtypeStruct((sides, width, rows), BF16),
            jax.ShapeDtypeStruct((1, width), F32),
        ],
        scratch_shapes=[pltpu.VMEM((rows, width), F32)],
        compiler_params=pltpu.CompilerParams(vmem_limit_bytes=VMEM_LIMIT),
        cost_estimate=BESIDE,
    )(*d_second, middle, cotangent, gain, weights)


def first_back(d_q, d_kv, weights, tokens, grad_middle, gain, live):
    sides, rows, width = tokens.shape
    q_width, kv_width = d_q.shape[1], d_kv.shape[1]

    def kernel(
        dq_ref, dkv_ref, w_ref, x_ref, gm_ref, gain_ref, live_ref, out_ref, gain_grad_ref, sums_ref
    ):
        d_first = dot(dq_ref[0].T, w_ref[:, :q_width], ((1,), (1,)))
        d_first += dot(dkv_ref[0].T, w_ref[:, q_width : q_width + kv_width], ((1,), (1,)))
        grad, gain_grad = norm_back(d_first, gain_ref[...], x_ref[0].astype(F32))
        total = gm_ref[0] + grad
        out_ref[0] = total.astype(BF16)
        add_row(gain_grad_ref, pl.program_id(0) == 0, gain_grad)
        add_sums(sums_ref, pl.program_id(0) == 0, [jnp.sum(live_ref[0] * total * total)])

    return pl.pallas_call(
        kernel,
        grid=(sides,),
        in_specs=[
            side_spec(q_width, rows),
            side_spec(kv_width, rows),
            fixed(weights.shape),
            side_spec(rows, width),
            side_spec(rows, width),
            fixed((1, width)),
            side_spec(rows, 1),
        ],
        out_specs=[side_spec(rows, width), fixed((1, width)), fixed((8, 128))],
        out_shape=[
            jax.ShapeDtypeStruct(tokens.shape, BF16),
            jax.ShapeDtypeStruct((1, width), F32),
            jax.ShapeDtypeStruct((8, 128), F32),
        ],
        compiler_params=pltpu.CompilerParams(vmem_limit_bytes=VMEM_LIMIT),
        cost_estimate=BESIDE,
    )(d_q, d_kv, weights, tokens, grad_middle, gain, live)


def finish(middle, branch_ffn, live, gain_one, gain_two, early_sums, late_sums):
    sides, rows, width = middle.shape

    def kernel(
        m_ref, low_ref, high_ref, from_y_ref, from_x_ref, live_ref, one_ref, two_ref, early_ref,
        late_ref, out_ref, small_ref, f_ref,
    ):
        @pl.when(pl.program_id(0) == 0)
        def _():
            f_ref[...] = low_ref[0] + from_y_ref[0].astype(F32)

        @pl.when(pl.program_id(0) == 1)
        def _():
            f_ref[...] = high_ref[0] + from_x_ref[0].astype(F32)

        ffn = f_ref[...]
        result = m_ref[0] + ffn
        out_ref[0] = result.astype(BF16)
        mask = live_ref[0]
        own = [jnp.sum(mask * result * result), jnp.sum(mask * ffn * ffn), jnp.sum(mask)]
        first = pl.program_id(0) == 0
        row = lax.broadcasted_iota(jnp.int32, (8, width), 0)
        value = jnp.where(row == 2, own[0], 0.0)
        value = jnp.where(row == 5, own[1], value)
        value = jnp.where(row == 7, own[2], value)

        @pl.when(first)
        def _():
            start = jnp.where(row == 0, one_ref[...], 0.0)
            start = jnp.where(row == 1, two_ref[...], start)
            start = jnp.where(row == 3, late_ref[0:1, 0:1], start)
            start = jnp.where(row == 4, early_ref[0:1, 0:1], start)
            small_ref[...] = jnp.where(row == 6, early_ref[1:2, 0:1], start)

        small_ref[...] += value

    return pl.pallas_call(
        kernel,
        grid=(sides,),
        in_specs=[
            side_spec(rows, width),
            fixed((1, rows, width)),
            fixed((1, rows, width)),
            fixed((1, rows, width)),
            fixed((1, rows, width)),
            side_spec(rows, 1),
            fixed((1, width)),
            fixed((1, width)),
            fixed((8, 128)),
            fixed((8, 128)),
        ],
        out_specs=[side_spec(rows, width), fixed((8, width))],
        out_shape=[
            jax.ShapeDtypeStruct(middle.shape, BF16),
            jax.ShapeDtypeStruct((8, width), F32),
        ],
        scratch_shapes=[pltpu.VMEM((rows, width), F32)],
        compiler_params=pltpu.CompilerParams(vmem_limit_bytes=VMEM_LIMIT),
        cost_estimate=BESIDE,
    )(middle, *branch_ffn, live, gain_one, gain_two, early_sums, late_sums)


def norm_forward(value_rows, gain):
    inverse = lax.rsqrt(jnp.mean(value_rows * value_rows, axis=-1, keepdims=True) + EPSILON)
    normed = value_rows * inverse
    return (normed * gain, normed, inverse)


def norm_backward(upstream, gain, normed, inverse):
    scaled = upstream * gain
    grad_in = inverse * (scaled - normed * jnp.mean(scaled * normed, axis=-1, keepdims=True))
    return (grad_in, jnp.sum(upstream * normed, axis=0))


def ein(spec, left, right):
    return jnp.einsum(spec, left, right, preferred_element_type=F32)


def turn(v, cosine, sine):
    half = HEAD_DIM // 2
    a, b = v[:, :, :half], v[:, :, half:]
    return jnp.concatenate([a * cosine - b * sine, a * sine + b * cosine], axis=2)


def per_device(
    tokens, cotangent, segments, valid, norm_one, w_query, w_key, w_value, w_out,
    norm_two, w_gate, w_up, w_down,
):
    c = lax.axis_index("ctx")
    n = lax.axis_size("fsdp")
    f = lax.axis_index("fsdp")
    row_count = tokens.shape[1]
    rows = row_count // 2
    width = tokens.shape[2]
    blocks = 8
    q_width, kv_width = w_query.shape[1], w_key.shape[1]
    ff = w_gate.shape[1]
    r = w_query.shape[0]
    c_ref = c.reshape(1).astype(jnp.int32)

    q_blocks = jnp.stack([c, blocks - 1 - c]).astype(jnp.int32)
    seg_blocks = segments[0].reshape(blocks, rows)
    valid_blocks = valid[0].reshape(blocks, rows)
    seg_q = jnp.stack([take(seg_blocks, q_blocks[0], 0), take(seg_blocks, q_blocks[1], 0)])
    live = jnp.stack([take(valid_blocks, q_blocks[0], 0), take(valid_blocks, q_blocks[1], 0)])
    seg_q = seg_q[:, None, :].astype(F32)
    seg_k = seg_blocks[:, None, :].astype(F32)
    valid_k = valid_blocks[:, None, :].astype(F32)
    owners = c ^ jnp.arange(4, dtype=jnp.int32)
    block_of = jnp.stack([owners, blocks - 1 - owners], axis=1)
    every = jnp.arange(blocks, dtype=jnp.int32)
    side = (every >= 4).astype(jnp.int32)
    slots = (c ^ jnp.where(every < 4, every, blocks - 1 - every)) * 2 + side
    slots = slots.astype(jnp.int32)
    places = block_of[:, :, None] * rows + jnp.arange(rows, dtype=jnp.int32)
    half = HEAD_DIM // 2
    freqs = jnp.exp(jnp.arange(half, dtype=F32) * (-math.log(ROPE_BASE) / half))
    angles = places.astype(F32).reshape(8, 1, rows) * freqs[None, :, None]
    cosine, sine = jnp.cos(angles), jnp.sin(angles)

    tokens_own = tokens[0].reshape(2, rows, width)
    tokens_x, tokens_y = swap_x(tokens_own), swap_y(tokens_own)
    gains = jnp.stack([norm_one, norm_two], axis=1)
    gains = jnp.concatenate([gains, jnp.zeros((r, 126), BF16)], axis=1)
    qkv_shard = jnp.concatenate([w_query, w_key, w_value, gains], axis=1)
    c4 = qkv_shard.shape[1] // 4
    qkv_z = z_fetch(lax.dynamic_slice_in_dim(qkv_shard, c * c4, c4, 1))
    d4 = w_down.shape[0] // 4
    down_shard = lax.dynamic_slice_in_dim(w_down, c * d4, d4, 0)
    qkv_z, tokens_x, tokens_y = sync(qkv_z, tokens_x, tokens_y)
    qkv_x, qkv_y = swap_x(qkv_z), swap_y(qkv_z)
    picked = after(pick_columns(c_ref, w_out, w_gate, w_up, n), qkv_z)
    out_gu = lax.all_gather(picked, "fsdp", axis=0, tiled=True)
    down_w = lax.all_gather(after(down_shard, qkv_z), "fsdp", axis=0, tiled=True)
    cut = ff // 4
    live_rows = live.reshape(2, rows, 1).astype(F32)
    qkv_x, qkv_y, tokens_x, tokens_y, cosine, sine, cos_own, sin_own, live_rows = sync(
        qkv_x, qkv_y, tokens_x, tokens_y, cosine, sine, cosine[:2], sine[:2], live_rows
    )
    zh = qkv_z.shape[0] // 2
    qkv_mine = jnp.stack([qkv_z, qkv_x, qkv_y])
    qkv_d = swap_y(qkv_x[:zh]), swap_x(qkv_y[zh:])
    tokens_d = swap_y(tokens_x[:1]), swap_x(tokens_y[1:])
    qkv_other = core_swap(qkv_mine)
    qkv_d, tokens_d, qkv_other = sync(qkv_d, tokens_d, qkv_other)
    qkv_d = jnp.concatenate(qkv_d)[None]
    qkv_other_d = core_swap(qkv_d)
    dy_own = cotangent[0].reshape(2, rows, width)
    dy_pieces = ctx_fetch_direct(after(dy_own, qkv_other_d))

    first_all, q_t, kv_all, qkv_w, gain_rows = project(
        c,
        f,
        (tokens_own, tokens_x, tokens_y, *tokens_d),
        (qkv_mine, qkv_d),
        (qkv_other, qkv_other_d),
        cosine,
        sine,
        q_width,
    )
    gain_one, gain_two = gain_rows[0:1], gain_rows[1:2]
    first_all = first_all.reshape(4, 2, rows, width)
    o_t, lse = attention_forward(q_blocks, slots, seg_q, seg_k, valid_k, q_t, kv_all)
    o_t, out_gu, dy_pieces, down_w = sync(o_t, out_gu, dy_pieces, down_w)
    dy_all, gu_w = sync(
        jnp.stack(dy_pieces).reshape(4, row_count, width), out_gu[:, width:]
    )
    attended_t = o_t.reshape(2, width, rows)
    middle, x_own, early_sums = out_project(tokens_own, attended_t, out_gu, gain_two, live_rows)

    x_x, x_y = swap_x(x_own), swap_y(x_own)
    held = feed_forward(x_own.reshape(1, row_count, width), dy_all, gu_w, down_w, 0, None)
    x_x, x_y, *held = sync(x_x, x_y, *held)
    own_part = held.pop()
    x_d = jnp.concatenate([swap_y(x_x[:1]), swap_x(x_y[1:])])
    x_xy = jnp.stack([x_x, x_y]).reshape(2, row_count, width)
    held = feed_forward(x_xy, dy_all, gu_w, down_w, 1, held)
    x_d, *held = sync(x_d, *held)
    y_low, x_high = held.pop(), held.pop()
    x_d = x_d.reshape(1, row_count, width)
    *held, to_x, to_y = feed_forward(x_d, dy_all, gu_w, down_w, 3, held)
    got = swap_x(to_x), swap_y(to_y)
    x_all, hidden, d_gu = [v.reshape(4 * row_count, -1) for v in held]
    dy_all = dy_all.reshape(4 * row_count, width)
    grad_gu = transposed_product(x_all, d_gu, 256)
    ffn_parts = ffn_product(after(hidden, grad_gu), down_w, rows)
    got_low, got_high, grad_gu, ffn_parts = sync(*got, grad_gu, ffn_parts)
    got_low, got_high = got_low.astype(F32), got_high.astype(F32)
    low_own = own_part[:1].astype(F32) + got_low[:1]
    high_own = own_part[1:].astype(F32) + got_high[:1]
    from_y = swap_y((y_low.astype(F32) + got_low[1:]).astype(BF16))
    from_x = swap_x((x_high.astype(F32) + got_high[1:]).astype(BF16))
    grad_d = transposed_product(after(hidden, ffn_parts), dy_all, cut)
    d_second = low_own, from_y, high_own, from_x
    d_second, grad_d = sync(d_second, grad_d)
    own_gu = lax.psum_scatter(grad_gu, "fsdp", scatter_dimension=0, tiled=True)
    own_down = lax.psum_scatter(grad_d, "fsdp", scatter_dimension=0, tiled=True)

    k = f % 2
    nz = n // 2
    r4 = r // 4
    grad_middle, d_branch, do_t, grad_gain_two = middle_back(
        d_second, middle, dy_own, gain_two, out_gu
    )
    do_t = do_t.reshape(2, HEADS, HEAD_DIM, rows)
    whole_out = side_product(attended_t, d_branch)
    do_t, ffn_parts, whole_out = sync(do_t, ffn_parts, whole_out)
    ffn_to_x, ffn_to_y, ffn_keep = ffn_parts
    ffn_got = swap_x(ffn_to_x), swap_y(ffn_to_y)
    d_q, dkv_low, dkv_high, dkv_keep = attention_backward(
        q_blocks, slots, seg_q, seg_k, valid_k, cos_own, sin_own, q_t, kv_all, o_t, do_t, lse
    )
    d_q, dkv_low, dkv_high, dkv_keep, ffn_got = sync(d_q, dkv_low, dkv_high, dkv_keep, ffn_got)
    dkv_got = swap_x(dkv_low), swap_y(dkv_high)
    own_out = lax.psum_scatter(
        after(whole_out, dkv_low, own_gu), "fsdp", scatter_dimension=0, tiled=True
    )
    q4, kv4 = q_width // 4, kv_width // 2

    def quarter(v, size, i):
        return lax.dynamic_slice_in_dim(v, (c ^ i) * size, size, 1)

    d_q = d_q.reshape(2, q_width, rows)
    dq_parts = [quarter(d_q, q4, i) for i in range(4)]
    ffn_low, ffn_high = ffn_got[0].astype(F32), ffn_got[1].astype(F32)
    ffn_sums = (
        ffn_keep[:1].astype(F32) + ffn_low[:1],
        ffn_keep[1:2].astype(F32) + ffn_high[:1],
        (ffn_keep[2:3].astype(F32) + ffn_low[1:]).astype(BF16),
        (ffn_keep[3:].astype(F32) + ffn_high[1:]).astype(BF16),
    )
    dkv_got, dq_parts, ffn_sums = sync(dkv_got, dq_parts, ffn_sums)
    kept = dkv_keep.astype(F32)
    low_sums, high_sums = kept[:2] + dkv_got[0].astype(F32), kept[2:] + dkv_got[1].astype(F32)
    from_y, from_x = swap_y(low_sums[1].astype(BF16)), swap_x(high_sums[1].astype(BF16))
    dkv_own = jnp.stack([low_sums[0] + from_y.astype(F32), high_sums[0] + from_x.astype(F32)])
    dkv_own = dkv_own.reshape(2, 2 * KV_HEADS, HEAD_DIM, rows)
    dq_got = exchange_first(dq_parts)
    d_k = turn(dkv_own[:, :KV_HEADS], cos_own[:, None], -sin_own[:, None]).astype(BF16)
    d_kv = jnp.concatenate([d_k, dkv_own[:, KV_HEADS:].astype(BF16)], axis=1)
    d_kv = d_kv.reshape(2, 2 * kv_width, rows)
    dkv_parts = [quarter(d_kv, kv4, i) for i in range(4)]
    dkv_got = exchange_first(dkv_parts)
    dq_got, dkv_got, ffn_sums = sync(dq_got, dkv_got, ffn_sums)
    diagonal = (
        swap_y(jnp.concatenate([dq_got[0][2:], dkv_got[0][2:]], axis=1)),
        swap_x(jnp.concatenate([dq_got[1][2:], dkv_got[1][2:]], axis=1)),
    )
    ffn_last = swap_y(ffn_sums[2]), swap_x(ffn_sums[3])
    dq_pieces = [dq_parts[0], *dq_got]
    dkv_pieces = [dkv_parts[0], *dkv_got]
    diagonal, own_out = sync(diagonal, own_out)
    own_out = own_out.reshape(4, r4, width)
    out_parts = [take(own_out, c ^ i, 0) for i in range(4)]
    out_got = scatter_first(out_parts)
    grad_qkv = project_grad(first_all.reshape(8, rows, width), dq_pieces, dkv_pieces, diagonal)
    grad_qkv = grad_qkv.reshape(nz, 2, r, q4 + kv4)
    got_half = core_swap(take(grad_qkv, k ^ 1, 1))
    pair_qkv = (take(grad_qkv, k, 1).astype(F32) + got_half.astype(F32)).astype(BF16)
    pair_qkv, d_q, d_kv, ffn_last, own_gu, out_got = sync(
        pair_qkv, d_q, d_kv, ffn_last, own_gu, out_got
    )
    own_qkv = z_scatter(pair_qkv).astype(BF16)

    gu_x, gu_y = swap_x(own_gu), swap_y(own_gu)
    out_sums = scatter_pass(out_parts, out_got)
    grad_tokens, grad_gain_one, late_sums = first_back(
        d_q, d_kv, qkv_w, tokens_own, grad_middle, gain_one, live_rows
    )
    result, small = finish(
        middle, (*ffn_sums[:2], *ffn_last), live_rows, grad_gain_one, grad_gain_two, early_sums, late_sums
    )
    own_qkv, small, gu_x, gu_y, out_sums = sync(own_qkv, small, gu_x, gu_y, out_sums)

    small = small + core_swap(small)
    own_out = scatter_last(*out_sums).astype(BF16)
    qkv_pieces = ctx_fetch_direct(own_qkv)
    small, own_out, gu_x, gu_y = sync(small, own_out, gu_x, gu_y)
    small = z_sum(small)
    hr = gu_x.shape[0] // 2
    gu_d = jnp.concatenate([swap_y(gu_x[:hr]), swap_x(gu_y[hr:])])
    small, own_down, gu_d, own_out = sync(small, own_down, gu_d, own_out)
    small = sum(ctx_fetch_direct(small))
    last = ctx_fetch_direct(jnp.concatenate([own_out, own_down]))
    out_pieces, down_pieces = [v[:r4] for v in last], [v[r4:] for v in last]
    grad_q, grad_k, grad_v = join_columns(c_ref, qkv_pieces, q4, kv4)
    grad_gate_w, grad_up_w = unpick_columns(c_ref, [own_gu, gu_x, gu_y, gu_d], n)
    grad_down_w = in_order(down_pieces, 0).reshape(4 * d4, width).astype(F32)
    grad_out_w = in_order(out_pieces, 0).reshape(r, width).astype(F32)
    gain_sums = lax.dynamic_slice_in_dim(small[:2], f * r, r, 1)
    squares = small[2:8, 0]
    spreads = jnp.sqrt(squares[:5] / (squares[5] * width))
    return (
        result.reshape(1, row_count, width),
        grad_tokens.reshape(1, row_count, width),
        gain_sums[0],
        grad_q,
        grad_k,
        grad_v,
        grad_out_w,
        gain_sums[1],
        grad_gate_w,
        grad_up_w,
        grad_down_w,
        spreads,
    )


def solution(mesh):
    rows, shard, vector = P("fsdp", "ctx", None), P("fsdp", None), P("fsdp")
    return jax.shard_map(
        per_device,
        mesh=mesh,
        in_specs=(
            rows, rows, shard, shard, vector, shard, shard, shard, shard, vector,
            shard, shard, shard,
        ),
        out_specs=(
            rows, rows, vector, shard, shard, shard, shard, vector, shard, shard, shard, P(),
        ),
        check_vma=False,
    )
```

```python
import functools
import math

import jax
import jax.numpy as jnp
from jax import lax
from jax.experimental import pallas as pl
from jax.experimental.pallas import tpu as pltpu
from jax.sharding import PartitionSpec as P

HEADS = 20
KV_HEADS = 5
HEAD_DIM = 64
GROUP = HEADS // KV_HEADS
WINDOW = 1024
EPSILON = 1e-05
MASKED = -1e30
ROPE_BASE = 10000.0
VMEM_LIMIT = 60 * 2**20
BF16 = jnp.bfloat16
F32 = jnp.float32


def core_swap(v):
    n = lax.axis_size("fsdp")
    return lax.ppermute(v, "fsdp", [(i, i ^ 1) for i in range(n)])


def swap_x(v):
    return lax.ppermute(v, "ctx", [(i, i ^ 1) for i in range(4)])


def swap_y(v):
    return lax.ppermute(v, "ctx", [(i, i ^ 2) for i in range(4)])


def put(buffer, piece, index, axis):
    return lax.dynamic_update_slice_in_dim(
        buffer, jnp.expand_dims(piece, axis), index, axis
    )


def take(v, index, axis):
    return lax.dynamic_index_in_dim(v, index, axis, keepdims=False)


def place(pieces, axis):
    first = pieces[0][1]
    shape = first.shape[:axis] + (len(pieces),) + first.shape[axis:]
    buffer = jnp.zeros(shape, first.dtype)
    for index, piece in pieces:
        buffer = put(buffer, piece, index, axis)
    return buffer


def z_fetch(piece):
    n = lax.axis_size("fsdp")
    nz = n // 2
    if nz != 4:
        groups = [list(range(0, n, 2)), list(range(1, n, 2))]
        every = lax.all_gather(piece, "fsdp", axis=0, axis_index_groups=groups)
        z = lax.axis_index("fsdp") // 2
        return jnp.take(every, (z - jnp.arange(nz)) % nz, axis=0)
    pieces = [piece]
    for d in (1, 2, 3):
        pieces.append(lax.ppermute(piece, "fsdp", [(i, (i + 2 * d) % n) for i in range(n)]))
    return jnp.stack(pieces)


def z_scatter(pieces):
    n = lax.axis_size("fsdp")
    nz = n // 2
    if nz != 4:
        groups = [list(range(0, n, 2)), list(range(1, n, 2))]
        return lax.psum_scatter(
            pieces, "fsdp", scatter_dimension=0, axis_index_groups=groups
        ).astype(F32)
    z = lax.axis_index("fsdp") // 2
    total = take(pieces, z, 0).astype(F32)
    for d in (1, 2, 3):
        sent = take(pieces, (z + d) % nz, 0)
        got = lax.ppermute(sent, "fsdp", [(i, (i + 2 * d) % n) for i in range(n)])
        total = total + got.astype(F32)
    return total


def sync(*values):
    return lax.optimization_barrier(values)


def ctx_fetch(piece):
    half = piece.shape[0] // 2
    from_x = swap_x(piece)
    from_y = swap_y(piece)
    from_d = jnp.concatenate([swap_y(from_x[:half]), swap_x(from_y[half:])], axis=0)
    return [piece, from_x, from_y, from_d]


def after(v, *earlier):
    return lax.optimization_barrier((v, earlier))[0]


def ctx_fetch_direct(piece):
    diagonal = lax.ppermute(piece, "ctx", [(i, i ^ 3) for i in range(4)])
    return [piece, swap_x(piece), swap_y(piece), diagonal]


def in_order(pieces, axis):
    c = lax.axis_index("ctx")
    return place([(c ^ i, v) for i, v in enumerate(pieces)], axis)


def scatter_first(parts):
    half = parts[0].shape[0] // 2
    low_got = swap_x(jnp.concatenate([parts[1][:half], parts[3][:half]]))
    high_got = swap_y(jnp.concatenate([parts[2][half:], parts[3][half:]]))
    return low_got, high_got


def scatter_pass(parts, got):
    half = parts[0].shape[0] // 2
    rest = parts[0].shape[0] - half
    low_got, high_got = got[0].astype(F32), got[1].astype(F32)
    low_pass = (parts[2][:half].astype(F32) + low_got[half:]).astype(BF16)
    high_pass = (parts[1][half:].astype(F32) + high_got[rest:]).astype(BF16)
    low_own = parts[0][:half].astype(F32) + low_got[:half]
    high_own = parts[0][half:].astype(F32) + high_got[:rest]
    return low_own, high_own, low_pass, high_pass


def scatter_last(low_own, high_own, low_pass, high_pass):
    from_y, from_x = swap_y(low_pass), swap_x(high_pass)
    return jnp.concatenate([low_own + from_y.astype(F32), high_own + from_x.astype(F32)])


def exchange_first(parts):
    to_x = jnp.concatenate([parts[1], parts[3][:1]], axis=0)
    to_y = jnp.concatenate([parts[2], parts[3][1:]], axis=0)
    return swap_x(to_x), swap_y(to_y)


def z_sum(v):
    n = lax.axis_size("fsdp")
    if n == 8:
        return v + sum(
            lax.ppermute(v, "fsdp", [(i, (i + 2 * d) % n) for i in range(n)]) for d in (1, 2, 3)
        )
    bit = 2
    while bit < n:
        v = v + lax.ppermute(v, "fsdp", [(i, i ^ bit) for i in range(n)])
        bit *= 2
    return v


def pick_columns(c, out, gate, up, count):
    r, ff = gate.shape
    width = out.shape[1]
    group = ff // count
    strip = group // 4

    def kernel(c_ref, w_ref, gate_ref, up_ref, out_ref):
        out_ref[:, :width] = w_ref[...]
        for own in range(4):

            @pl.when(c_ref[0] == own)
            def _():
                for j in range(count):
                    at = j * group + own * strip
                    to = width + j * strip
                    out_ref[:, to : to + strip] = gate_ref[:, at : at + strip]
                    to += ff // 4
                    out_ref[:, to : to + strip] = up_ref[:, at : at + strip]

    whole = pl.BlockSpec((r, ff), lambda i, s: (0, 0))
    return pl.pallas_call(
        kernel,
        grid_spec=pltpu.PrefetchScalarGridSpec(
            num_scalar_prefetch=1,
            grid=(1,),
            in_specs=[pl.BlockSpec((r, width), lambda i, s: (0, 0)), whole, whole],
            out_specs=pl.BlockSpec((r, width + ff // 2), lambda i, s: (0, 0)),
        ),
        out_shape=jax.ShapeDtypeStruct((r, width + ff // 2), BF16),
        cost_estimate=pl.CostEstimate(flops=0, bytes_accessed=6 * r * ff, transcendentals=0),
    )(c, out, gate, up)


def unpick_columns(c, pieces, count):
    r, half = pieces[0].shape
    ff = 2 * half
    group = ff // count
    strip = group // 4

    def kernel(c_ref, *refs):
        gate_ref, up_ref = refs[4:]
        for own in range(4):

            @pl.when(c_ref[0] == own)
            def _():
                for step in range(4):
                    for j in range(count):
                        at = j * group + (own ^ step) * strip
                        piece = refs[step]
                        gate_ref[:, at : at + strip] = piece[
                            :, j * strip : (j + 1) * strip
                        ].astype(F32)
                        frm = ff // 4 + j * strip
                        up_ref[:, at : at + strip] = piece[:, frm : frm + strip].astype(F32)

    whole = pl.BlockSpec((r, ff), lambda i, s: (0, 0))
    return pl.pallas_call(
        kernel,
        grid_spec=pltpu.PrefetchScalarGridSpec(
            num_scalar_prefetch=1,
            grid=(1,),
            in_specs=[pl.BlockSpec((r, half), lambda i, s: (0, 0))] * 4,
            out_specs=[whole, whole],
        ),
        out_shape=[jax.ShapeDtypeStruct((r, ff), F32)] * 2,
        compiler_params=pltpu.CompilerParams(vmem_limit_bytes=VMEM_LIMIT),
        cost_estimate=pl.CostEstimate(flops=0, bytes_accessed=12 * r * ff, transcendentals=0),
    )(c, *pieces)


def join_columns(c, pieces, q4, kv4):
    r = pieces[0].shape[0]

    def kernel(c_ref, *refs):
        q_ref, k_ref, v_ref = refs[4:]
        for own in range(4):

            @pl.when(c_ref[0] == own)
            def _():
                for step in range(4):
                    to = own ^ step
                    piece = refs[step][...].astype(F32)
                    q_ref[:, to * q4 : (to + 1) * q4] = piece[:, :q4]
                    target = k_ref if to < 2 else v_ref
                    at = (to % 2) * kv4
                    target[:, at : at + kv4] = piece[:, q4:]

    def whole(cols):
        return pl.BlockSpec((r, cols), lambda i, s: (0, 0))

    return pl.pallas_call(
        kernel,
        grid_spec=pltpu.PrefetchScalarGridSpec(
            num_scalar_prefetch=1,
            grid=(1,),
            in_specs=[whole(q4 + kv4)] * 4,
            out_specs=[whole(4 * q4), whole(2 * kv4), whole(2 * kv4)],
        ),
        out_shape=[
            jax.ShapeDtypeStruct((r, cols), F32) for cols in (4 * q4, 2 * kv4, 2 * kv4)
        ],
        cost_estimate=pl.CostEstimate(
            flops=0, bytes_accessed=24 * r * (q4 + kv4), transcendentals=0
        ),
    )(c, *pieces)


def pair_bias(q_block, k_block, rows, seg_q, seg_k, valid_k):
    key_at = k_block * rows + lax.broadcasted_iota(jnp.int32, (rows, rows), 0)
    query_at = q_block * rows + lax.broadcasted_iota(jnp.int32, (rows, rows), 1)
    distance = query_at - key_at
    allowed = (
        (seg_q == seg_k)
        & (distance >= 0)
        & (distance < WINDOW)
        & ((valid_k == 1.0) | (distance == 0))
    )
    return jnp.where(allowed, 0.0, MASKED).astype(F32)


def first_block(q_block, rows):
    reach = (WINDOW + rows - 2) // rows
    return jnp.maximum(q_block - reach, 0)


def dot(a, b, dims):
    return lax.dot_general(a, b, (dims, ((), ())), preferred_element_type=F32)


def column(row):
    size = row.shape[1]
    return jnp.broadcast_to(row, (size, size)).T


def fill_bias(blocks_ref, seg_q_ref, seg_k_ref, valid_k_ref, bias_ref, rows):
    for side in range(2):
        b = blocks_ref[side]
        lo = first_block(b, rows)

        def body(kb, _):
            bias_ref[side, kb - lo] = pair_bias(
                b, kb, rows, seg_q_ref[side], column(seg_k_ref[kb]), column(valid_k_ref[kb])
            )
            return 0

        lax.fori_loop(lo, b + 1, body, 0)


def forward_kernel(
    blocks_ref, slots_ref, seg_q_ref, seg_k_ref, valid_k_ref, q_ref, k_ref, v_ref,
    o_ref, lse_ref, bias_ref, scores_ref, acc_ref,
):
    rows = q_ref.shape[-1]

    @pl.when(pl.program_id(0) == 0)
    def _():
        fill_bias(blocks_ref, seg_q_ref, seg_k_ref, valid_k_ref, bias_ref, rows)

    for side in range(2):
        b = blocks_ref[side]
        lo = first_block(b, rows)

        def score(kb, peaks):
            keys = k_ref[slots_ref[kb], 0].T
            bias = bias_ref[side, kb - lo]
            higher = []
            for h in range(GROUP):
                s = dot(keys, q_ref[side, h], ((1,), (0,))) + bias
                scores_ref[kb - lo, h] = s
                higher.append(jnp.maximum(peaks[h], jnp.max(s, axis=0, keepdims=True)))
            return tuple(higher)

        peaks = lax.fori_loop(
            lo, b + 1, score, (jnp.full((1, rows), -jnp.inf, F32),) * GROUP
        )
        acc_ref[...] = jnp.zeros_like(acc_ref)

        def mix(kb, totals):
            values_t = v_ref[slots_ref[kb], 0]
            more = []
            for h in range(GROUP):
                p = jnp.exp(scores_ref[kb - lo, h] - peaks[h])
                more.append(totals[h] + jnp.sum(p, axis=0, keepdims=True))
                acc_ref[h] += dot(values_t, p.astype(BF16), ((1,), (0,)))
            return tuple(more)

        totals = lax.fori_loop(lo, b + 1, mix, (jnp.zeros((1, rows), F32),) * GROUP)
        for h in range(GROUP):
            o_ref[side, h] = (acc_ref[h] / totals[h]).astype(BF16)
            lse_ref[side, 0, h : h + 1] = peaks[h] + jnp.log(totals[h])


def backward_kernel(
    blocks_ref, slots_ref, seg_q_ref, seg_k_ref, valid_k_ref, cos_ref, sin_ref, q_ref, k_ref, v_ref,
    o_ref, do_ref, lse_ref,
    dq_ref, low_ref, high_ref, keep_ref,
    bias_ref, acc_ref, center_ref, dk_ref, dv_ref, p_ref, ds_ref,
):
    rows = q_ref.shape[-1]
    half = HEAD_DIM // 2

    @pl.when(pl.program_id(0) == 0)
    def _():
        fill_bias(blocks_ref, seg_q_ref, seg_k_ref, valid_k_ref, bias_ref, rows)

    dk_ref[...] = jnp.zeros_like(dk_ref)
    dv_ref[...] = jnp.zeros_like(dv_ref)
    for side in range(2):
        b = blocks_ref[side]
        lo = first_block(b, rows)
        acc_ref[...] = jnp.zeros_like(acc_ref)
        for h in range(GROUP):
            center_ref[h : h + 1] = jnp.sum(
                o_ref[side, h].astype(F32) * do_ref[side, h].astype(F32), axis=0, keepdims=True
            )

        def soft(kb, at):
            slot = slots_ref[kb]
            keys = k_ref[slot, 0].T
            values = v_ref[slot, 0].T
            bias = bias_ref[side, kb - lo]
            for h in range(GROUP):
                s = dot(keys, q_ref[side, h], ((1,), (0,))) + bias
                p = jnp.exp(s - lse_ref[side, 0, h : h + 1])
                dp = dot(values, do_ref[side, h], ((1,), (0,)))
                p_ref[at, h] = p.astype(BF16)
                ds_ref[at, h] = (p * (dp - center_ref[h : h + 1])).astype(BF16)

        def products(kb, at):
            slot = slots_ref[kb]
            dv = dot(do_ref[side, 0], p_ref[at, 0], ((1,), (1,)))
            dk = dot(q_ref[side, 0], ds_ref[at, 0], ((1,), (1,)))
            for h in range(1, GROUP):
                dv += dot(do_ref[side, h], p_ref[at, h], ((1,), (1,)))
                dk += dot(q_ref[side, h], ds_ref[at, h], ((1,), (1,)))
            dv_ref[slot] += dv
            dk_ref[slot] += dk
            for h in range(GROUP):
                acc_ref[h] += dot(k_ref[slot, 0], ds_ref[at, h], ((1,), (0,)))

        soft(lo, 0)

        def body(kb, _):
            products(kb - 1, (kb - 1 - lo) % 2)
            soft(kb, (kb - lo) % 2)
            return 0

        lax.fori_loop(lo + 1, b + 1, body, 0)
        products(b, (b - lo) % 2)
        cos, sin = cos_ref[side], sin_ref[side]
        for h in range(GROUP):
            a, b2 = acc_ref[h, :half] * 0.125, acc_ref[h, half:] * 0.125
            turned = jnp.concatenate([a * cos + b2 * sin, b2 * cos - a * sin], axis=0)
            dq_ref[side, h] = turned.astype(BF16)
    for target, slots in ((low_ref, (2, 6)), (high_ref, (5, 7)), (keep_ref, (0, 4, 1, 3))):
        for i, slot in enumerate(slots):
            target[i, 0, 0] = dk_ref[slot].astype(BF16)
            target[i, 1, 0] = dv_ref[slot].astype(BF16)


def project(c, f, tokens, mine, other, cosine, sine, q_width):
    _, rows, width = tokens[0].shape
    blocks = 8
    _, nz, r, cols = mine[0].shape
    half = HEAD_DIM // 2
    kv_heads = 2 * KV_HEADS
    gains_at = q_width + kv_heads * HEAD_DIM

    def turned(flat_t, at, cos, sin):
        a, b = flat_t[at : at + half], flat_t[at + half : at + HEAD_DIM]
        return jnp.concatenate([a * cos - b * sin, a * sin + b * cos], axis=0)

    def kernel(at_ref, *refs):
        token_refs, mine_refs, other_refs = refs[:5], refs[5:7], refs[7:9]
        cos_ref, sin_ref, first_ref, q_ref, kv_ref, w_ref, gain_ref, x_ref = refs[9:]

        @pl.when(pl.program_id(0) == 0)
        def _():
            for core in range(2):
                for q in range(4):
                    step = q ^ at_ref[0]

                    def fill(index, which, core=core, q=q):
                        for z in range(nz):
                            z_step = (at_ref[1] // 2 - z + nz) % nz
                            for kk in range(2):
                                source = mine_refs if kk == core else other_refs
                                at = (2 * z + kk) * r
                                w_ref[at : at + r, q * cols : (q + 1) * cols] = source[which][
                                    index, z_step
                                ]

                    @pl.when((at_ref[1] % 2 == core) & (step < 3))
                    def _(step=step, fill=fill):
                        fill(step, 0)

                    @pl.when((at_ref[1] % 2 == core) & (step == 3))
                    def _(fill=fill):
                        fill(0, 1)

            gain_ref[...] = w_ref[:, gains_at:].astype(F32).T[:8]

        for i in range(3):

            @pl.when(pl.program_id(0) == i)
            def _(i=i):
                x_ref[...] = token_refs[i][...].astype(F32)

        @pl.when(pl.program_id(0) == 3)
        def _():
            x_ref[0] = token_refs[3][0].astype(F32)
            x_ref[1] = token_refs[4][0].astype(F32)

        x = x_ref[...]
        inverse = lax.rsqrt(jnp.mean(x * x, axis=-1, keepdims=True) + EPSILON)
        scaled = x * inverse * gain_ref[0:1][None]
        first_ref[...] = scaled.astype(BF16)
        first = scaled.reshape(2 * rows, width).astype(BF16)
        both = dot(first, w_ref[:, q_width:gains_at], ((1,), (0,)))
        for i in range(2):
            cos, sin = cos_ref[i], sin_ref[i]
            kv = both[i * rows : (i + 1) * rows].T
            for h in range(kv_heads):
                at = h * HEAD_DIM
                if h < KV_HEADS:
                    kv_ref[i, h] = turned(kv, at, cos, sin).astype(BF16)
                else:
                    kv_ref[i, h] = kv[at : at + HEAD_DIM].astype(BF16)

        @pl.when(pl.program_id(0) == 0)
        def _():
            both = dot(first, w_ref[:, :q_width], ((1,), (0,)))
            for i in range(2):
                cos, sin = cos_ref[i], sin_ref[i]
                q = both[i * rows : (i + 1) * rows].T
                for h in range(HEADS):
                    turned_q = turned(q, h * HEAD_DIM, cos, sin).astype(BF16)
                    q_ref[i, h] = (turned_q.astype(F32) * 0.125).astype(BF16)

    table = pl.BlockSpec((2, half, rows), lambda i, s: (i, 0, 0))
    operands = [*tokens, *mine, *other]
    return pl.pallas_call(
        kernel,
        grid_spec=pltpu.PrefetchScalarGridSpec(
            num_scalar_prefetch=1,
            grid=(blocks // 2,),
            in_specs=[fixed(v.shape) for v in operands] + [table, table],
            out_specs=[
                pl.BlockSpec((2, rows, width), lambda i, s: (i, 0, 0)),
                fixed((2, HEADS, HEAD_DIM, rows)),
                pl.BlockSpec((2, kv_heads, HEAD_DIM, rows), lambda i, s: (i, 0, 0, 0)),
                fixed((2 * nz * r, 4 * cols)),
                fixed((8, width)),
            ],
            scratch_shapes=[pltpu.VMEM((2, rows, width), F32)],
        ),
        out_shape=[
            jax.ShapeDtypeStruct((blocks, rows, width), BF16),
            jax.ShapeDtypeStruct((2, HEADS, HEAD_DIM, rows), BF16),
            jax.ShapeDtypeStruct((blocks, kv_heads, HEAD_DIM, rows), BF16),
            jax.ShapeDtypeStruct((2 * nz * r, 4 * cols), BF16),
            jax.ShapeDtypeStruct((8, width), F32),
        ],
        compiler_params=pltpu.CompilerParams(vmem_limit_bytes=VMEM_LIMIT),
        cost_estimate=pl.CostEstimate(
            flops=8_000_000_000, bytes_accessed=25_000_000, transcendentals=0
        ),
    )(jnp.stack([c, f]).astype(jnp.int32), *operands, cosine, sine)


def project_grad(first_all, dq_pieces, dkv_pieces, diagonal):
    _, rows, width = first_all.shape
    q4, kv4 = dq_pieces[0].shape[1], dkv_pieces[0].shape[1]

    def kernel(first_ref, *refs):
        out_ref = refs[-1]
        total = None
        for i in range(8):
            if i < 6:
                turned = jnp.concatenate([refs[i // 2][i % 2], refs[3 + i // 2][i % 2]], axis=0)
            else:
                turned = refs[i][0]
            term = dot(turned, first_ref[i], ((1,), (0,)))
            total = term if total is None else total + term
        out_ref[...] = total.T.astype(BF16)

    operands = [first_all, *dq_pieces, *dkv_pieces, *diagonal]
    return pl.pallas_call(
        kernel,
        grid=(1,),
        in_specs=[fixed(v.shape) for v in operands],
        out_specs=fixed((width, q4 + kv4)),
        out_shape=jax.ShapeDtypeStruct((width, q4 + kv4), BF16),
        compiler_params=pltpu.CompilerParams(vmem_limit_bytes=VMEM_LIMIT),
        cost_estimate=BESIDE,
    )(*operands)


def kernel_specs(blocks, rows):
    q_spec = pl.BlockSpec((2, GROUP, HEAD_DIM, rows), lambda g, *_: (0, g, 0, 0))
    k_spec = pl.BlockSpec((blocks, 1, HEAD_DIM, rows), lambda g, *_: (0, g, 0, 0))
    v_spec = pl.BlockSpec((blocks, 1, HEAD_DIM, rows), lambda g, *_: (0, KV_HEADS + g, 0, 0))
    stat_spec = pl.BlockSpec((2, 1, GROUP, rows), lambda g, *_: (0, g, 0, 0))
    seg_specs = [
        pl.BlockSpec((2, 1, rows), lambda g, *_: (0, 0, 0)),
        pl.BlockSpec((blocks, 1, rows), lambda g, *_: (0, 0, 0)),
        pl.BlockSpec((blocks, 1, rows), lambda g, *_: (0, 0, 0)),
    ]
    return q_spec, k_spec, v_spec, stat_spec, seg_specs


def attention_forward(q_blocks, slots, seg_q, seg_k, valid_k, q_t, kv_t):
    blocks, _, _, rows = kv_t.shape
    q_spec, k_spec, v_spec, stat_spec, seg_specs = kernel_specs(blocks, rows)
    reach = (WINDOW + rows - 2) // rows + 1
    return pl.pallas_call(
        forward_kernel,
        grid_spec=pltpu.PrefetchScalarGridSpec(
            num_scalar_prefetch=2,
            grid=(KV_HEADS,),
            in_specs=seg_specs + [q_spec, k_spec, v_spec],
            out_specs=[q_spec, stat_spec],
            scratch_shapes=[
                pltpu.VMEM((2, reach, rows, rows), F32),
                pltpu.VMEM((reach, GROUP, rows, rows), F32),
                pltpu.VMEM((GROUP, HEAD_DIM, rows), F32),
            ],
        ),
        out_shape=[
            jax.ShapeDtypeStruct(q_t.shape, BF16),
            jax.ShapeDtypeStruct((2, KV_HEADS, GROUP, rows), F32),
        ],
        compiler_params=pltpu.CompilerParams(vmem_limit_bytes=VMEM_LIMIT),
        cost_estimate=pl.CostEstimate(
            flops=20_000_000_000, bytes_accessed=6_000_000, transcendentals=0
        ),
    )(q_blocks, slots, seg_q, seg_k, valid_k, q_t, kv_t, kv_t)


def attention_backward(q_blocks, slots, seg_q, seg_k, valid_k, cos, sin, q_t, kv_t, o_t, do_t, lse):
    blocks, _, _, rows = kv_t.shape
    q_spec, k_spec, v_spec, stat_spec, seg_specs = kernel_specs(blocks, rows)
    reach = (WINDOW + rows - 2) // rows + 1
    table = pl.BlockSpec((2, HEAD_DIM // 2, rows), lambda g, *_: (0, 0, 0))

    def dkv_spec(count):
        return pl.BlockSpec((count, 2, 1, HEAD_DIM, rows), lambda g, *_: (0, 0, g, 0, 0))

    def dkv_shape(count):
        return jax.ShapeDtypeStruct((count, 2, KV_HEADS, HEAD_DIM, rows), BF16)

    return pl.pallas_call(
        backward_kernel,
        grid_spec=pltpu.PrefetchScalarGridSpec(
            num_scalar_prefetch=2,
            grid=(KV_HEADS,),
            in_specs=seg_specs
            + [table, table, q_spec, k_spec, v_spec, q_spec, q_spec, stat_spec],
            out_specs=[q_spec, dkv_spec(2), dkv_spec(2), dkv_spec(4)],
            scratch_shapes=[
                pltpu.VMEM((2, reach, rows, rows), F32),
                pltpu.VMEM((GROUP, HEAD_DIM, rows), F32),
                pltpu.VMEM((GROUP, rows), F32),
                pltpu.VMEM((blocks, HEAD_DIM, rows), F32),
                pltpu.VMEM((blocks, HEAD_DIM, rows), F32),
                pltpu.VMEM((2, GROUP, rows, rows), BF16),
                pltpu.VMEM((2, GROUP, rows, rows), BF16),
            ],
        ),
        out_shape=[
            jax.ShapeDtypeStruct(q_t.shape, BF16),
            dkv_shape(2),
            dkv_shape(2),
            dkv_shape(4),
        ],
        compiler_params=pltpu.CompilerParams(vmem_limit_bytes=VMEM_LIMIT),
        cost_estimate=BESIDE,
    )(q_blocks, slots, seg_q, seg_k, valid_k, cos, sin, q_t, kv_t, kv_t, o_t, do_t, lse)


def feed_forward(x, dy_all, gu_w, down_w, first, held):
    count, rows, width = x.shape
    cut = down_w.shape[0]
    side = rows // 2
    held = () if held is None else tuple(held)

    def kernel(x_ref, dy_ref, gu_ref, down_ref, *refs):
        all_ref, hidden_ref, d_gu_ref, *part_refs = refs[len(held) :]
        x_in = x_ref[0]
        all_ref[0] = x_in
        gu = dot(x_in, gu_ref[...], ((1,), (0,)))
        d_hidden = dot(dy_ref[0], down_ref[...], ((1,), (1,)))
        gate_pre, up_pre = gu[:, :cut], gu[:, cut:]
        sig = jax.nn.sigmoid(gate_pre)
        swish = gate_pre * sig
        slope = sig * (1.0 + gate_pre * (1.0 - sig))
        hidden_ref[0] = (swish * up_pre).astype(BF16)
        d_gu_ref[0, :, :cut] = (d_hidden * up_pre * slope).astype(BF16)
        d_gu_ref[0, :, cut:] = (d_hidden * swish).astype(BF16)
        part = dot(d_gu_ref[0], gu_ref[...], ((1,), (1,)))
        low, high = part[:side].astype(BF16), part[side:].astype(BF16)
        if first == 0:
            part_refs[0][0] = low
            part_refs[0][1] = high
        elif first == 3:
            part_refs[0][0] = low
            part_refs[1][0] = high
        else:
            to_x, to_y, x_high, y_low = part_refs

            @pl.when(pl.program_id(0) == 0)
            def _():
                to_x[0] = low
                x_high[0] = high

            @pl.when(pl.program_id(0) == 1)
            def _():
                y_low[0] = low
                to_y[0] = high

    def block(size):
        return pl.BlockSpec((1, rows, size), lambda i: (first + i, 0, 0))

    def at(index):
        return pl.BlockSpec((1, side, width), lambda i: (index, 0, 0))

    def sums(size):
        return jax.ShapeDtypeStruct((size, side, width), BF16)

    if first == 0:
        part_specs, part_shapes = [fixed((2, side, width))], [sums(2)]
    elif first == 3:
        part_specs, part_shapes = [at(1), at(1)], [sums(2), sums(2)]
    else:
        part_specs, part_shapes = [at(0)] * 4, [sums(2), sums(2), sums(1), sums(1)]
    return pl.pallas_call(
        kernel,
        grid=(count,),
        in_specs=[
            pl.BlockSpec((1, rows, width), lambda i: (i, 0, 0)),
            block(width),
            fixed(gu_w.shape),
            fixed(down_w.shape),
        ]
        + [pl.BlockSpec(memory_space=pl.ANY)] * len(held),
        out_specs=[block(width), block(cut), block(2 * cut)] + part_specs,
        out_shape=[
            jax.ShapeDtypeStruct((4, rows, width), BF16),
            jax.ShapeDtypeStruct((4, rows, cut), BF16),
            jax.ShapeDtypeStruct((4, rows, 2 * cut), BF16),
        ]
        + part_shapes,
        input_output_aliases={4 + i: i for i in range(len(held))},
        compiler_params=pltpu.CompilerParams(vmem_limit_bytes=VMEM_LIMIT),
        cost_estimate=pl.CostEstimate(
            flops=10 * count * rows * width * cut,
            bytes_accessed=2 * (gu_w.size + down_w.size + count * rows * (4 * width + 3 * cut)),
            transcendentals=0,
        ),
    )(x, dy_all, gu_w, down_w, *held)


BESIDE = pl.CostEstimate(flops=0, bytes_accessed=0, transcendentals=0)


def fixed(shape):
    return pl.BlockSpec(shape, lambda *_: (0,) * len(shape))


def transposed_product(left, right, tile):
    depth, rows = left.shape
    cols = right.shape[1]

    def kernel(left_ref, right_ref, out_ref):
        out_ref[...] = dot(left_ref[...], right_ref[...], ((0,), (0,))).astype(BF16)

    return pl.pallas_call(
        kernel,
        grid=(rows // tile,),
        in_specs=[pl.BlockSpec((depth, tile), lambda i: (0, i)), fixed(right.shape)],
        out_specs=pl.BlockSpec((tile, cols), lambda i: (i, 0)),
        out_shape=jax.ShapeDtypeStruct((rows, cols), BF16),
        compiler_params=pltpu.CompilerParams(vmem_limit_bytes=VMEM_LIMIT),
        cost_estimate=BESIDE,
    )(left, right)


def ffn_product(hidden, down_w, side):
    rows, cut = hidden.shape
    width = down_w.shape[1]

    def kernel(left_ref, right_ref, to_x, to_y, keep):
        total = dot(left_ref[...], right_ref[...], ((1,), (0,)))
        low, high = total[:side].astype(BF16), total[side:].astype(BF16)
        places = (
            ((keep, 0), (keep, 1)), ((to_x, 0), (keep, 3)),
            ((keep, 2), (to_y, 0)), ((to_x, 1), (to_y, 1)),
        )
        for i, ((low_ref, low_at), (high_ref, high_at)) in enumerate(places):

            @pl.when(pl.program_id(0) == i)
            def _():
                low_ref[low_at] = low
                high_ref[high_at] = high

    sizes = (2, 2, 4)
    return pl.pallas_call(
        kernel,
        grid=(4,),
        in_specs=[pl.BlockSpec((rows // 4, cut), lambda i: (i, 0)), fixed(down_w.shape)],
        out_specs=[fixed((size, side, width)) for size in sizes],
        out_shape=[jax.ShapeDtypeStruct((size, side, width), BF16) for size in sizes],
        compiler_params=pltpu.CompilerParams(vmem_limit_bytes=VMEM_LIMIT),
        cost_estimate=BESIDE,
    )(hidden, down_w)


def side_product(left_t, right):
    def kernel(left_ref, right_ref, out_ref):
        total = dot(left_ref[0], right_ref[0], ((1,), (0,)))
        out_ref[...] = (total + dot(left_ref[1], right_ref[1], ((1,), (0,)))).astype(BF16)

    shape = (left_t.shape[1], right.shape[2])
    return pl.pallas_call(
        kernel,
        grid=(1,),
        in_specs=[fixed(left_t.shape), fixed(right.shape)],
        out_specs=fixed(shape),
        out_shape=jax.ShapeDtypeStruct(shape, BF16),
        compiler_params=pltpu.CompilerParams(vmem_limit_bytes=VMEM_LIMIT),
        cost_estimate=BESIDE,
    )(left_t, right)


def add_sums(ref, first, sums):
    row = lax.broadcasted_iota(jnp.int32, (8, 128), 0)
    value = jnp.zeros((8, 128), F32)
    for i, v in enumerate(sums):
        value = jnp.where(row == i, v, value)

    @pl.when(first)
    def _():
        ref[...] = jnp.zeros_like(ref)

    ref[...] += value


def side_spec(*shape):
    return pl.BlockSpec((1, *shape), lambda i: (i, 0, 0))


def out_project(tokens, attended_t, weights, gain, live):
    sides, rows, width = tokens.shape

    def kernel(x_ref, att_ref, w_ref, gain_ref, live_ref, middle_ref, second_ref, sums_ref):
        branch = dot(att_ref[0], w_ref[...], ((0,), (0,)))
        middle = x_ref[0].astype(F32) + branch
        middle_ref[0] = middle
        inverse = lax.rsqrt(jnp.mean(middle * middle, axis=-1, keepdims=True) + EPSILON)
        second_ref[0] = (middle * inverse * gain_ref[...]).astype(BF16)
        mask = live_ref[0]
        sums = [jnp.sum(mask * branch * branch), jnp.sum(mask * middle * middle)]
        add_sums(sums_ref, pl.program_id(0) == 0, sums)

    return pl.pallas_call(
        kernel,
        grid=(sides,),
        in_specs=[
            side_spec(rows, width),
            side_spec(width, rows),
            fixed((width, width)),
            fixed((1, width)),
            side_spec(rows, 1),
        ],
        out_specs=[side_spec(rows, width), side_spec(rows, width), fixed((8, 128))],
        out_shape=[
            jax.ShapeDtypeStruct(tokens.shape, F32),
            jax.ShapeDtypeStruct(tokens.shape, BF16),
            jax.ShapeDtypeStruct((8, 128), F32),
        ],
        compiler_params=pltpu.CompilerParams(vmem_limit_bytes=VMEM_LIMIT),
        cost_estimate=BESIDE,
    )(tokens, attended_t, weights, gain, live)


def norm_back(upstream, gain, value):
    inverse = lax.rsqrt(jnp.mean(value * value, axis=-1, keepdims=True) + EPSILON)
    normed = value * inverse
    scaled = upstream * gain
    grad = inverse * (scaled - normed * jnp.mean(scaled * normed, axis=-1, keepdims=True))
    return grad, jnp.sum(upstream * normed, axis=0, keepdims=True)


def add_row(ref, first, row):
    @pl.when(first)
    def _():
        ref[...] = jnp.zeros_like(ref)

    ref[...] += row


def middle_back(d_second, middle, cotangent, gain, weights):
    sides, rows, width = middle.shape

    def kernel(
        low_ref, from_y_ref, high_ref, from_x_ref, m_ref, cot_ref, gain_ref, w_ref,
        gm_ref, branch_ref, do_ref, gain_grad_ref, d_ref,
    ):
        @pl.when(pl.program_id(0) == 0)
        def _():
            d_ref[...] = low_ref[0] + from_y_ref[0].astype(F32)

        @pl.when(pl.program_id(0) == 1)
        def _():
            d_ref[...] = high_ref[0] + from_x_ref[0].astype(F32)

        grad, gain_grad = norm_back(d_ref[...], gain_ref[...], m_ref[0])
        grad_middle = cot_ref[0].astype(F32) + grad
        gm_ref[0] = grad_middle
        d_branch = grad_middle.astype(BF16)
        branch_ref[0] = d_branch
        do_ref[0] = dot(d_branch, w_ref[...], ((1,), (1,))).T.astype(BF16)
        add_row(gain_grad_ref, pl.program_id(0) == 0, gain_grad)

    return pl.pallas_call(
        kernel,
        grid=(sides,),
        in_specs=[fixed((1, rows, width))] * 4
        + [
            side_spec(rows, width),
            side_spec(rows, width),
            fixed((1, width)),
            fixed((width, width)),
        ],
        out_specs=[
            side_spec(rows, width),
            side_spec(rows, width),
            side_spec(width, rows),
            fixed((1, width)),
        ],
        out_shape=[
            jax.ShapeDtypeStruct(middle.shape, F32),
            jax.ShapeDtypeStruct(middle.shape, BF16),
            jax.ShapeDtypeStruct((sides, width, rows), BF16),
            jax.ShapeDtypeStruct((1, width), F32),
        ],
        scratch_shapes=[pltpu.VMEM((rows, width), F32)],
        compiler_params=pltpu.CompilerParams(vmem_limit_bytes=VMEM_LIMIT),
        cost_estimate=BESIDE,
    )(*d_second, middle, cotangent, gain, weights)


def first_back(d_q, d_kv, weights, tokens, grad_middle, gain, live):
    sides, rows, width = tokens.shape
    q_width, kv_width = d_q.shape[1], d_kv.shape[1]

    def kernel(
        dq_ref, dkv_ref, w_ref, x_ref, gm_ref, gain_ref, live_ref, out_ref, gain_grad_ref, sums_ref
    ):
        d_first = dot(dq_ref[0].T, w_ref[:, :q_width], ((1,), (1,)))
        d_first += dot(dkv_ref[0].T, w_ref[:, q_width : q_width + kv_width], ((1,), (1,)))
        grad, gain_grad = norm_back(d_first, gain_ref[...], x_ref[0].astype(F32))
        total = gm_ref[0] + grad
        out_ref[0] = total.astype(BF16)
        add_row(gain_grad_ref, pl.program_id(0) == 0, gain_grad)
        add_sums(sums_ref, pl.program_id(0) == 0, [jnp.sum(live_ref[0] * total * total)])

    return pl.pallas_call(
        kernel,
        grid=(sides,),
        in_specs=[
            side_spec(q_width, rows),
            side_spec(kv_width, rows),
            fixed(weights.shape),
            side_spec(rows, width),
            side_spec(rows, width),
            fixed((1, width)),
            side_spec(rows, 1),
        ],
        out_specs=[side_spec(rows, width), fixed((1, width)), fixed((8, 128))],
        out_shape=[
            jax.ShapeDtypeStruct(tokens.shape, BF16),
            jax.ShapeDtypeStruct((1, width), F32),
            jax.ShapeDtypeStruct((8, 128), F32),
        ],
        compiler_params=pltpu.CompilerParams(vmem_limit_bytes=VMEM_LIMIT),
        cost_estimate=BESIDE,
    )(d_q, d_kv, weights, tokens, grad_middle, gain, live)


def finish(middle, branch_ffn, live, gain_one, gain_two, early_sums, late_sums):
    sides, rows, width = middle.shape

    def kernel(
        m_ref, low_ref, high_ref, from_y_ref, from_x_ref, live_ref, one_ref, two_ref, early_ref,
        late_ref, out_ref, small_ref, f_ref,
    ):
        @pl.when(pl.program_id(0) == 0)
        def _():
            f_ref[...] = low_ref[0] + from_y_ref[0].astype(F32)

        @pl.when(pl.program_id(0) == 1)
        def _():
            f_ref[...] = high_ref[0] + from_x_ref[0].astype(F32)

        ffn = f_ref[...]
        result = m_ref[0] + ffn
        out_ref[0] = result.astype(BF16)
        mask = live_ref[0]
        own = [jnp.sum(mask * result * result), jnp.sum(mask * ffn * ffn), jnp.sum(mask)]
        first = pl.program_id(0) == 0
        row = lax.broadcasted_iota(jnp.int32, (8, width), 0)
        value = jnp.where(row == 2, own[0], 0.0)
        value = jnp.where(row == 5, own[1], value)
        value = jnp.where(row == 7, own[2], value)

        @pl.when(first)
        def _():
            start = jnp.where(row == 0, one_ref[...], 0.0)
            start = jnp.where(row == 1, two_ref[...], start)
            start = jnp.where(row == 3, late_ref[0:1, 0:1], start)
            start = jnp.where(row == 4, early_ref[0:1, 0:1], start)
            small_ref[...] = jnp.where(row == 6, early_ref[1:2, 0:1], start)

        small_ref[...] += value

    return pl.pallas_call(
        kernel,
        grid=(sides,),
        in_specs=[
            side_spec(rows, width),
            fixed((1, rows, width)),
            fixed((1, rows, width)),
            fixed((1, rows, width)),
            fixed((1, rows, width)),
            side_spec(rows, 1),
            fixed((1, width)),
            fixed((1, width)),
            fixed((8, 128)),
            fixed((8, 128)),
        ],
        out_specs=[side_spec(rows, width), fixed((8, width))],
        out_shape=[
            jax.ShapeDtypeStruct(middle.shape, BF16),
            jax.ShapeDtypeStruct((8, width), F32),
        ],
        scratch_shapes=[pltpu.VMEM((rows, width), F32)],
        compiler_params=pltpu.CompilerParams(vmem_limit_bytes=VMEM_LIMIT),
        cost_estimate=BESIDE,
    )(middle, *branch_ffn, live, gain_one, gain_two, early_sums, late_sums)


def norm_forward(value_rows, gain):
    inverse = lax.rsqrt(jnp.mean(value_rows * value_rows, axis=-1, keepdims=True) + EPSILON)
    normed = value_rows * inverse
    return (normed * gain, normed, inverse)


def norm_backward(upstream, gain, normed, inverse):
    scaled = upstream * gain
    grad_in = inverse * (scaled - normed * jnp.mean(scaled * normed, axis=-1, keepdims=True))
    return (grad_in, jnp.sum(upstream * normed, axis=0))


def ein(spec, left, right):
    return jnp.einsum(spec, left, right, preferred_element_type=F32)


def turn(v, cosine, sine):
    half = HEAD_DIM // 2
    a, b = v[:, :, :half], v[:, :, half:]
    return jnp.concatenate([a * cosine - b * sine, a * sine + b * cosine], axis=2)


def per_device(
    tokens, cotangent, segments, valid, norm_one, w_query, w_key, w_value, w_out,
    norm_two, w_gate, w_up, w_down,
):
    c = lax.axis_index("ctx")
    n = lax.axis_size("fsdp")
    f = lax.axis_index("fsdp")
    row_count = tokens.shape[1]
    rows = row_count // 2
    width = tokens.shape[2]
    blocks = 8
    q_width, kv_width = w_query.shape[1], w_key.shape[1]
    ff = w_gate.shape[1]
    r = w_query.shape[0]
    c_ref = c.reshape(1).astype(jnp.int32)

    q_blocks = jnp.stack([c, blocks - 1 - c]).astype(jnp.int32)
    seg_blocks = segments[0].reshape(blocks, rows)
    valid_blocks = valid[0].reshape(blocks, rows)
    seg_q = jnp.stack([take(seg_blocks, q_blocks[0], 0), take(seg_blocks, q_blocks[1], 0)])
    live = jnp.stack([take(valid_blocks, q_blocks[0], 0), take(valid_blocks, q_blocks[1], 0)])
    seg_q = seg_q[:, None, :].astype(F32)
    seg_k = seg_blocks[:, None, :].astype(F32)
    valid_k = valid_blocks[:, None, :].astype(F32)
    owners = c ^ jnp.arange(4, dtype=jnp.int32)
    block_of = jnp.stack([owners, blocks - 1 - owners], axis=1)
    every = jnp.arange(blocks, dtype=jnp.int32)
    side = (every >= 4).astype(jnp.int32)
    slots = (c ^ jnp.where(every < 4, every, blocks - 1 - every)) * 2 + side
    slots = slots.astype(jnp.int32)
    places = block_of[:, :, None] * rows + jnp.arange(rows, dtype=jnp.int32)
    half = HEAD_DIM // 2
    freqs = jnp.exp(jnp.arange(half, dtype=F32) * (-math.log(ROPE_BASE) / half))
    angles = places.astype(F32).reshape(8, 1, rows) * freqs[None, :, None]
    cosine, sine = jnp.cos(angles), jnp.sin(angles)

    tokens_own = tokens[0].reshape(2, rows, width)
    tokens_x, tokens_y = swap_x(tokens_own), swap_y(tokens_own)
    gains = jnp.stack([norm_one, norm_two], axis=1)
    gains = jnp.concatenate([gains, jnp.zeros((r, 126), BF16)], axis=1)
    qkv_shard = jnp.concatenate([w_query, w_key, w_value, gains], axis=1)
    c4 = qkv_shard.shape[1] // 4
    qkv_z = z_fetch(lax.dynamic_slice_in_dim(qkv_shard, c * c4, c4, 1))
    d4 = w_down.shape[0] // 4
    down_shard = lax.dynamic_slice_in_dim(w_down, c * d4, d4, 0)
    qkv_z, tokens_x, tokens_y = sync(qkv_z, tokens_x, tokens_y)
    qkv_x, qkv_y = swap_x(qkv_z), swap_y(qkv_z)
    picked = after(pick_columns(c_ref, w_out, w_gate, w_up, n), qkv_z)
    out_gu = lax.all_gather(picked, "fsdp", axis=0, tiled=True)
    down_w = lax.all_gather(after(down_shard, qkv_z), "fsdp", axis=0, tiled=True)
    cut = ff // 4
    live_rows = live.reshape(2, rows, 1).astype(F32)
    qkv_x, qkv_y, tokens_x, tokens_y, cosine, sine, cos_own, sin_own, live_rows = sync(
        qkv_x, qkv_y, tokens_x, tokens_y, cosine, sine, cosine[:2], sine[:2], live_rows
    )
    zh = qkv_z.shape[0] // 2
    qkv_mine = jnp.stack([qkv_z, qkv_x, qkv_y])
    qkv_d = swap_y(qkv_x[:zh]), swap_x(qkv_y[zh:])
    tokens_d = swap_y(tokens_x[:1]), swap_x(tokens_y[1:])
    qkv_other = core_swap(qkv_mine)
    qkv_d, tokens_d, qkv_other = sync(qkv_d, tokens_d, qkv_other)
    qkv_d = jnp.concatenate(qkv_d)[None]
    qkv_other_d = core_swap(qkv_d)
    dy_own = cotangent[0].reshape(2, rows, width)
    dy_pieces = ctx_fetch_direct(after(dy_own, qkv_other_d))

    first_all, q_t, kv_all, qkv_w, gain_rows = project(
        c,
        f,
        (tokens_own, tokens_x, tokens_y, *tokens_d),
        (qkv_mine, qkv_d),
        (qkv_other, qkv_other_d),
        cosine,
        sine,
        q_width,
    )
    gain_one, gain_two = gain_rows[0:1], gain_rows[1:2]
    first_all = first_all.reshape(4, 2, rows, width)
    o_t, lse = attention_forward(q_blocks, slots, seg_q, seg_k, valid_k, q_t, kv_all)
    o_t, out_gu, dy_pieces = sync(o_t, out_gu, dy_pieces)
    dy_all, gu_w, down_w = sync(
        jnp.stack(dy_pieces).reshape(4, row_count, width), out_gu[:, width:], down_w
    )
    attended_t = o_t.reshape(2, width, rows)
    middle, x_own, early_sums = out_project(tokens_own, attended_t, out_gu, gain_two, live_rows)

    x_x, x_y = swap_x(x_own), swap_y(x_own)
    held = feed_forward(x_own.reshape(1, row_count, width), dy_all, gu_w, down_w, 0, None)
    x_x, x_y, *held = sync(x_x, x_y, *held)
    own_part = held.pop()
    x_d = jnp.concatenate([swap_y(x_x[:1]), swap_x(x_y[1:])])
    x_xy = jnp.stack([x_x, x_y]).reshape(2, row_count, width)
    held = feed_forward(x_xy, dy_all, gu_w, down_w, 1, held)
    x_d, *held = sync(x_d, *held)
    y_low, x_high = held.pop(), held.pop()
    x_d = x_d.reshape(1, row_count, width)
    *held, to_x, to_y = feed_forward(x_d, dy_all, gu_w, down_w, 3, held)
    got = swap_x(to_x), swap_y(to_y)
    x_all, hidden, d_gu = [v.reshape(4 * row_count, -1) for v in held]
    dy_all = dy_all.reshape(4 * row_count, width)
    grad_gu = transposed_product(x_all, d_gu, 256)
    ffn_parts = ffn_product(after(hidden, grad_gu), down_w, rows)
    got_low, got_high, grad_gu, ffn_parts = sync(*got, grad_gu, ffn_parts)
    got_low, got_high = got_low.astype(F32), got_high.astype(F32)
    low_own = own_part[:1].astype(F32) + got_low[:1]
    high_own = own_part[1:].astype(F32) + got_high[:1]
    from_y = swap_y((y_low.astype(F32) + got_low[1:]).astype(BF16))
    from_x = swap_x((x_high.astype(F32) + got_high[1:]).astype(BF16))
    grad_d = transposed_product(after(hidden, ffn_parts), dy_all, cut)
    d_second = low_own, from_y, high_own, from_x
    d_second, grad_d = sync(d_second, grad_d)
    own_gu = lax.psum_scatter(grad_gu, "fsdp", scatter_dimension=0, tiled=True)
    own_down = lax.psum_scatter(grad_d, "fsdp", scatter_dimension=0, tiled=True)

    k = f % 2
    nz = n // 2
    r4 = r // 4
    grad_middle, d_branch, do_t, grad_gain_two = middle_back(
        d_second, middle, dy_own, gain_two, out_gu
    )
    do_t = do_t.reshape(2, HEADS, HEAD_DIM, rows)
    whole_out = side_product(attended_t, d_branch)
    do_t, ffn_parts, whole_out = sync(do_t, ffn_parts, whole_out)
    ffn_to_x, ffn_to_y, ffn_keep = ffn_parts
    ffn_got = swap_x(ffn_to_x), swap_y(ffn_to_y)
    d_q, dkv_low, dkv_high, dkv_keep = attention_backward(
        q_blocks, slots, seg_q, seg_k, valid_k, cos_own, sin_own, q_t, kv_all, o_t, do_t, lse
    )
    d_q, dkv_low, dkv_high, dkv_keep, ffn_got = sync(d_q, dkv_low, dkv_high, dkv_keep, ffn_got)
    dkv_got = swap_x(dkv_low), swap_y(dkv_high)
    own_out = lax.psum_scatter(
        after(whole_out, dkv_low, own_gu), "fsdp", scatter_dimension=0, tiled=True
    )
    q4, kv4 = q_width // 4, kv_width // 2

    def quarter(v, size, i):
        return lax.dynamic_slice_in_dim(v, (c ^ i) * size, size, 1)

    d_q = d_q.reshape(2, q_width, rows)
    dq_parts = [quarter(d_q, q4, i) for i in range(4)]
    ffn_low, ffn_high = ffn_got[0].astype(F32), ffn_got[1].astype(F32)
    ffn_sums = (
        ffn_keep[:1].astype(F32) + ffn_low[:1],
        ffn_keep[1:2].astype(F32) + ffn_high[:1],
        (ffn_keep[2:3].astype(F32) + ffn_low[1:]).astype(BF16),
        (ffn_keep[3:].astype(F32) + ffn_high[1:]).astype(BF16),
    )
    dkv_got, dq_parts, ffn_sums = sync(dkv_got, dq_parts, ffn_sums)
    kept = dkv_keep.astype(F32)
    low_sums, high_sums = kept[:2] + dkv_got[0].astype(F32), kept[2:] + dkv_got[1].astype(F32)
    from_y, from_x = swap_y(low_sums[1].astype(BF16)), swap_x(high_sums[1].astype(BF16))
    dkv_own = jnp.stack([low_sums[0] + from_y.astype(F32), high_sums[0] + from_x.astype(F32)])
    dkv_own = dkv_own.reshape(2, 2 * KV_HEADS, HEAD_DIM, rows)
    dq_got = exchange_first(dq_parts)
    d_k = turn(dkv_own[:, :KV_HEADS], cos_own[:, None], -sin_own[:, None]).astype(BF16)
    d_kv = jnp.concatenate([d_k, dkv_own[:, KV_HEADS:].astype(BF16)], axis=1)
    d_kv = d_kv.reshape(2, 2 * kv_width, rows)
    dkv_parts = [quarter(d_kv, kv4, i) for i in range(4)]
    dkv_got = exchange_first(dkv_parts)
    dq_got, dkv_got, ffn_sums = sync(dq_got, dkv_got, ffn_sums)
    diagonal = (
        swap_y(jnp.concatenate([dq_got[0][2:], dkv_got[0][2:]], axis=1)),
        swap_x(jnp.concatenate([dq_got[1][2:], dkv_got[1][2:]], axis=1)),
    )
    ffn_last = swap_y(ffn_sums[2]), swap_x(ffn_sums[3])
    dq_pieces = [dq_parts[0], *dq_got]
    dkv_pieces = [dkv_parts[0], *dkv_got]
    diagonal, own_out = sync(diagonal, own_out)
    own_out = own_out.reshape(4, r4, width)
    out_parts = [take(own_out, c ^ i, 0) for i in range(4)]
    out_got = scatter_first(out_parts)
    grad_qkv = project_grad(first_all.reshape(8, rows, width), dq_pieces, dkv_pieces, diagonal)
    grad_qkv = grad_qkv.reshape(nz, 2, r, q4 + kv4)
    got_half = core_swap(take(grad_qkv, k ^ 1, 1))
    pair_qkv = (take(grad_qkv, k, 1).astype(F32) + got_half.astype(F32)).astype(BF16)
    pair_qkv, d_q, d_kv, ffn_last, own_gu, out_got = sync(
        pair_qkv, d_q, d_kv, ffn_last, own_gu, out_got
    )
    own_qkv = z_scatter(pair_qkv).astype(BF16)

    gu_x, gu_y = swap_x(own_gu), swap_y(own_gu)
    out_sums = scatter_pass(out_parts, out_got)
    grad_tokens, grad_gain_one, late_sums = first_back(
        d_q, d_kv, qkv_w, tokens_own, grad_middle, gain_one, live_rows
    )
    result, small = finish(
        middle, (*ffn_sums[:2], *ffn_last), live_rows, grad_gain_one, grad_gain_two, early_sums, late_sums
    )
    own_qkv, small, gu_x, gu_y, out_sums = sync(own_qkv, small, gu_x, gu_y, out_sums)

    small = small + core_swap(small)
    own_out = scatter_last(*out_sums).astype(BF16)
    qkv_pieces = ctx_fetch_direct(own_qkv)
    small, own_out, gu_x, gu_y = sync(small, own_out, gu_x, gu_y)
    small = z_sum(small)
    hr = gu_x.shape[0] // 2
    gu_d = jnp.concatenate([swap_y(gu_x[:hr]), swap_x(gu_y[hr:])])
    small, own_down, gu_d, own_out = sync(small, own_down, gu_d, own_out)
    small = sum(ctx_fetch_direct(small))
    last = ctx_fetch_direct(jnp.concatenate([own_out, own_down]))
    out_pieces, down_pieces = [v[:r4] for v in last], [v[r4:] for v in last]
    grad_q, grad_k, grad_v = join_columns(c_ref, qkv_pieces, q4, kv4)
    grad_gate_w, grad_up_w = unpick_columns(c_ref, [own_gu, gu_x, gu_y, gu_d], n)
    grad_down_w = in_order(down_pieces, 0).reshape(4 * d4, width).astype(F32)
    grad_out_w = in_order(out_pieces, 0).reshape(r, width).astype(F32)
    gain_sums = lax.dynamic_slice_in_dim(small[:2], f * r, r, 1)
    squares = small[2:8, 0]
    spreads = jnp.sqrt(squares[:5] / (squares[5] * width))
    return (
        result.reshape(1, row_count, width),
        grad_tokens.reshape(1, row_count, width),
        gain_sums[0],
        grad_q,
        grad_k,
        grad_v,
        grad_out_w,
        gain_sums[1],
        grad_gate_w,
        grad_up_w,
        grad_down_w,
        spreads,
    )


def solution(mesh):
    rows, shard, vector = P("fsdp", "ctx", None), P("fsdp", None), P("fsdp")
    return jax.shard_map(
        per_device,
        mesh=mesh,
        in_specs=(
            rows, rows, shard, shard, vector, shard, shard, shard, shard, vector,
            shard, shard, shard,
        ),
        out_specs=(
            rows, rows, vector, shard, shard, shard, shard, vector, shard, shard, shard, P(),
        ),
        check_vma=False,
    )
```
